256 devices in a mesh: frame: 32 (over x_hi, z, core), space: 8 (over y, x_lo).
Axes of the slice: x: 4 (x_hi: 2, x_lo: 2; x = x_hi * 2 + x_lo), y: 4, z: 8, core: 2. Of those that a mesh axis runs over, the one named last changes fastest.
Arguments:
- frames_in: bfloat16 [128, 16, 64, 320], P('frame', 'space'), may hold values from -15 to 15
- kernel_space: bfloat16 [3, 3, 320, 320], replicated, may hold values from -0.109375 to 0.109375
- kernel_time: bfloat16 [3, 320, 320], replicated, may hold values from -0.1875 to 0.1875
- norm_gain: float32 [320], replicated, may hold values from 0.5 to 1.5
- proj_in: bfloat16 [320, 1280], replicated, may hold values from -0.3125 to 0.3125
- proj_query: bfloat16 [1280, 640], replicated, may hold values from -0.15625 to 0.15625
- proj_key: bfloat16 [1280, 640], replicated, may hold values from -0.15625 to 0.15625
- proj_value: bfloat16 [1280, 640], replicated, may hold values from -0.15625 to 0.15625
- proj_out: bfloat16 [640, 1280], replicated, may hold values from -0.25 to 0.25
- frame_bias: float32 [10, 32, 32], replicated, may hold values from -400 to 400
- cotangent: bfloat16 [32, 8, 32, 1280], P('frame', 'space'), may hold values from -24 to 24
Outputs:
- coarse_out: bfloat16 [32, 8, 32, 1280], P('frame', 'space')
- grad_frames: bfloat16 [128, 16, 64, 320], P('frame', 'space')
- grad_gain: float32 [320], replicated
The draws below stay inside these ranges and needn't reach their ends.
All inputs are finite; a program needn't handle non-finite values.
Results may differ from the reference program's by a relative error of at most 0.015.
Values may be sent and summed in bfloat16 or wider, within the bound.
No kernel may reach another device: no remote copies, remote signals or barrier semaphores. Data moves between devices by JAX's collectives and lax.ppermute only.
A program may use at most 64 MiB of HBM per device.

```python
import math
import jax
import jax.numpy as jnp
from jax import lax

C = 320
CC = 1280
HEADS = 10
GROUPS = 32
W = 64
QW = 640
F = 128
H = 16
NCF = 32
H2 = 8
W2 = 32


def draw_frames_in(key, part):
    key = jax.random.fold_in(key, 3)
    sample_key = jax.random.fold_in(key, 0)
    row_pos = jnp.arange(H, dtype=jnp.float32)[None, :, None, None] / max(H - 1, 1)
    row_scale = 1.0 + 2.0 * row_pos
    sample = jnp.clip(jax.random.normal(sample_key, (F, H, W, C), jnp.float32), -4.0, 4.0) * row_scale
    return sample.astype(jnp.bfloat16)


def draw_frame_bias(key, part):
    key = jax.random.fold_in(key, 7)
    base_key = jax.random.fold_in(key, 0)
    baseline = jax.random.normal(base_key, (HEADS, NCF, NCF), jnp.float32)
    return baseline


def block_levels(own_key, extent, cuts, least, largest):
    def one(axis_at, shards_of):
        heights = jax.random.uniform(jax.random.fold_in(jax.random.fold_in(own_key, 6), axis_at), (shards_of,), jnp.float32, least / len(cuts), largest / len(cuts))
        return jnp.repeat(jnp.exp(heights), extent[axis_at] // shards_of).reshape((-1,) + (1,) * (len(extent) - axis_at - 1))

    gain = one(*cuts[0])
    for cut in cuts[1:]:
        gain = gain * one(*cut)
    return gain


def gaussian(stream_key, dims, scale, reach, shards=(), kind=jnp.bfloat16):
    loudness = block_levels(stream_key, dims, shards, -0.22, 0.18) if shards else 1.0
    values = jax.random.normal(stream_key, dims, jnp.float32) * scale * loudness
    return jnp.minimum(jnp.maximum(values, -reach), reach).astype(kind)


def setup_inputs(seed: int = 0) -> dict:
    splits = jax.random.split(jax.random.key(seed), 12)
    frames_in = draw_frames_in(jax.random.fold_in(splits[11], 71), 0)
    kernel_space = gaussian(splits[1], (3, 3, C, C), (9 * C) ** -0.5, 0.109375)
    kernel_time = gaussian(splits[2], (3, C, C), (3 * C) ** -0.5, 0.1875)
    norm_gain = jnp.clip(1.0 + 0.1 * jax.random.normal(splits[3], (C,), jnp.float32), 0.5, 1.5)
    proj_in = gaussian(splits[4], (C, CC), C ** -0.5, 0.3125)
    proj_query = gaussian(splits[5], (CC, QW), CC ** -0.5, 0.15625)
    proj_key = gaussian(splits[6], (CC, QW), CC ** -0.5, 0.15625)
    proj_value = gaussian(splits[7], (CC, QW), CC ** -0.5, 0.15625)
    proj_out = gaussian(splits[8], (QW, CC), QW ** -0.5, 0.25)
    frame_bias = draw_frame_bias(jax.random.fold_in(splits[11], 71), 0)
    cotangent = gaussian(splits[10], (NCF, H2, W2, CC), 4.0, 24.0, ((0, 32), (1, 8)))
    return dict(frames_in=frames_in, kernel_space=kernel_space, kernel_time=kernel_time, norm_gain=norm_gain, proj_in=proj_in, proj_query=proj_query, proj_key=proj_key, proj_value=proj_value, proj_out=proj_out, frame_bias=frame_bias, cotangent=cotangent)


def dot_transposed(matrix, weight):
    return lax.dot_general(matrix, weight, (((1,), (1,)), ((), ())), preferred_element_type=jnp.float32)

def project(tensor, weight):
    flat = tensor.reshape(-1, tensor.shape[-1])
    return jnp.dot(flat, weight, preferred_element_type=jnp.float32).reshape(tensor.shape[:-1] + (weight.shape[1],))

def project_back(tensor, weight):
    flat = tensor.reshape(-1, tensor.shape[-1])
    return dot_transposed(flat, weight).reshape(tensor.shape[:-1] + (weight.shape[0],))

def space_conv(padded, kernel, transpose):
    frames, padded_rows, padded_cols, channels = padded.shape
    row_count = padded_rows - 2
    col_count = padded_cols - 2
    running = jnp.zeros((frames * row_count * col_count, channels), jnp.float32)
    for row_off in range(3):
        for col_off in range(3):
            if transpose:
                window = padded[:, 2 - row_off:2 - row_off + row_count, 2 - col_off:2 - col_off + col_count]
                running = running + dot_transposed(window.reshape(-1, channels), kernel[row_off, col_off])
            else:
                window = padded[:, row_off:row_off + row_count, col_off:col_off + col_count]
                running = running + jnp.dot(window.reshape(-1, channels), kernel[row_off, col_off], preferred_element_type=jnp.float32)
    return running.reshape(frames, row_count, col_count, channels)

def time_conv(padded, kernel, transpose):
    frames = padded.shape[0] - 2
    channels = padded.shape[3]
    running = jnp.zeros((frames * padded.shape[1] * padded.shape[2], channels), jnp.float32)
    for tap_index in range(3):
        if transpose:
            window = padded[2 - tap_index:2 - tap_index + frames].reshape(-1, channels)
            running = running + dot_transposed(window, kernel[tap_index])
        else:
            window = padded[tap_index:tap_index + frames].reshape(-1, channels)
            running = running + jnp.dot(window, kernel[tap_index], preferred_element_type=jnp.float32)
    return running.reshape((frames,) + padded.shape[1:])

def group_reduce(tensor):
    per_channel = lax.optimization_barrier(jnp.sum(tensor, axis=(1, 2)))
    return lax.optimization_barrier(jnp.sum(per_channel.reshape(tensor.shape[0], GROUPS, -1), axis=2))

def spread(statistic, channels):
    return jnp.repeat(statistic, channels // GROUPS, axis=1)[:, None, None, :]

def pool(tensor):
    frames, row_count, col_count, channels = tensor.shape
    return lax.optimization_barrier(jnp.mean(tensor.reshape(frames // 4, 4, row_count // 2, 2, col_count // 2, 2, channels), axis=(1, 3, 5)))

def unpool(tensor):
    coarse_frames, half_rows, half_cols, channels = tensor.shape
    grown = jnp.broadcast_to(tensor[:, None, :, None, :, None, :], (coarse_frames, 4, half_rows, 2, half_cols, 2, channels))
    return grown.reshape(coarse_frames * 4, half_rows * 2, half_cols * 2, channels) / 16.0

def split_heads(tensor, head_count):
    return tensor.reshape(tensor.shape[0], tensor.shape[1], head_count, -1).astype(jnp.float32)

def probabilities(queries, keys_in, bias):
    head_count = bias.shape[0]
    factor = 1.0 / math.sqrt(queries.shape[-1] // head_count)
    scores = jnp.einsum('ipnd,jpnd->pnij', split_heads(queries, head_count), split_heads(keys_in, head_count)) * factor + bias[None]
    row_max = lax.optimization_barrier(jnp.max(scores, axis=-1, keepdims=True))
    expd = jnp.exp(scores - row_max)
    return (expd / lax.optimization_barrier(jnp.sum(expd, axis=-1, keepdims=True)), factor)

def attend(queries, keys_in, values_in, bias):
    head_count = bias.shape[0]
    weights, factor = probabilities(queries, keys_in, bias)
    rounded = lax.optimization_barrier(weights.astype(jnp.bfloat16)).astype(jnp.float32)
    blended = jnp.einsum('pnij,jpnd->ipnd', rounded, split_heads(values_in, head_count))
    return blended.reshape(queries.shape).astype(jnp.bfloat16)

def attend_back(queries, keys_in, values_in, bias, grad_out):
    head_count = bias.shape[0]
    weights, factor = probabilities(queries, keys_in, bias)
    rounded = lax.optimization_barrier(weights.astype(jnp.bfloat16)).astype(jnp.float32)
    grad_heads = split_heads(grad_out, head_count)
    grad_weights = jnp.einsum('ipnd,jpnd->pnij', grad_heads, split_heads(values_in, head_count))
    grad_values = jnp.einsum('pnij,ipnd->jpnd', rounded, grad_heads)
    grad_scores = weights * (grad_weights - lax.optimization_barrier(jnp.sum(weights * grad_weights, axis=-1, keepdims=True)))
    grad_rounded = lax.optimization_barrier(grad_scores.astype(jnp.bfloat16)).astype(jnp.float32)
    grad_queries = jnp.einsum('pnij,jpnd->ipnd', grad_rounded, split_heads(keys_in, head_count)) * factor
    grad_keys = jnp.einsum('pnij,ipnd->jpnd', grad_rounded, split_heads(queries, head_count)) * factor
    out_shape = queries.shape
    return (grad_queries.reshape(out_shape).astype(jnp.bfloat16), grad_keys.reshape(out_shape).astype(jnp.bfloat16), grad_values.reshape(out_shape).astype(jnp.bfloat16))

def reference(frames_in, kernel_space, kernel_time, norm_gain, proj_in, proj_query, proj_key, proj_value, proj_out, frame_bias, cotangent):
    frames, height, width, channels = frames_in.shape
    cell_count = height * width * (channels // GROUPS)
    padded = jnp.pad(frames_in, ((0, 0), (1, 1), (1, 1), (0, 0)))
    spatial = space_conv(padded, kernel_space, False).astype(jnp.bfloat16)
    temporal = time_conv(jnp.pad(spatial, ((1, 1), (0, 0), (0, 0), (0, 0))), kernel_time, False)
    group_mean = group_reduce(temporal) / cell_count
    group_square = group_reduce(temporal * temporal) / cell_count
    inv_std = lax.rsqrt(group_square - group_mean * group_mean + 1e-05)
    normed = (temporal - spread(group_mean, channels)) * spread(inv_std, channels)
    gated = normed * norm_gain
    sigmoid_val = jax.nn.sigmoid(gated)
    fine_out = frames_in.astype(jnp.float32) + gated * sigmoid_val
    pooled = pool(fine_out).astype(jnp.bfloat16)
    coarse_frames, half_rows, half_cols = pooled.shape[:3]
    pooled = pooled.reshape(coarse_frames, half_rows * half_cols, channels)
    cot_rows = cotangent.reshape(coarse_frames, half_rows * half_cols, -1)
    coarse_in = lax.optimization_barrier(project(pooled, proj_in).astype(jnp.bfloat16))
    queries = project(coarse_in, proj_query).astype(jnp.bfloat16)
    keys_out = project(coarse_in, proj_key).astype(jnp.bfloat16)
    values_out = project(coarse_in, proj_value).astype(jnp.bfloat16)
    blended = attend(queries, keys_out, values_out, frame_bias)
    coarse_out = (coarse_in.astype(jnp.float32) + project(blended, proj_out)).astype(jnp.bfloat16)
    grad_heads = project_back(cot_rows, proj_out).astype(jnp.bfloat16)
    grad_queries, grad_keys, grad_values = attend_back(queries, keys_out, values_out, frame_bias, grad_heads)
    grad_coarse = (cot_rows.astype(jnp.float32) + project_back(grad_queries, proj_query) + project_back(grad_keys, proj_key) + project_back(grad_values, proj_value)).astype(jnp.bfloat16)
    grad_pooled = lax.optimization_barrier(project_back(grad_coarse, proj_in).astype(jnp.bfloat16))
    grad_fine = unpool(grad_pooled.astype(jnp.float32).reshape(coarse_frames, half_rows, half_cols, channels))
    grad_gated = grad_fine * sigmoid_val * (1.0 + gated * (1.0 - sigmoid_val))
    grad_gain = lax.optimization_barrier(jnp.sum(grad_gated * normed, axis=(0, 1, 2)))
    grad_normed = grad_gated * norm_gain
    first_mean = group_reduce(grad_normed) / cell_count
    second_mean = group_reduce(grad_normed * normed) / cell_count
    grad_temporal = (spread(inv_std, channels) * (grad_normed - spread(first_mean, channels) - normed * spread(second_mean, channels))).astype(jnp.bfloat16)
    grad_spatial = time_conv(jnp.pad(grad_temporal, ((1, 1), (0, 0), (0, 0), (0, 0))), kernel_time, True).astype(jnp.bfloat16)
    grad_frames = (grad_fine + space_conv(jnp.pad(grad_spatial, ((0, 0), (1, 1), (1, 1), (0, 0))), kernel_space, True)).astype(jnp.bfloat16)
    return (coarse_out.reshape(cotangent.shape), grad_frames, grad_gain)
```

```python
import math

import jax
import jax.numpy as jnp
from jax import lax
from jax.experimental import pallas as pl
from jax.experimental.pallas import tpu as pltpu
from jax.sharding import PartitionSpec as P

GROUPS = 32
LANES = 128
SLOT = 384
PAYLOAD = 16
bf16 = jnp.bfloat16
f32 = jnp.float32


def dot(a, b):
    return jnp.dot(a, b, preferred_element_type=f32)


def dot_nt(a, b):
    return lax.dot_general(a, b, (((1,), (1,)), ((), ())), preferred_element_type=f32)


def dot_tn(a, b):
    return lax.dot_general(a, b, (((0,), (0,)), ((), ())), preferred_element_type=f32)


def dot_exact(a, b):
    return jnp.dot(a, b, preferred_element_type=f32, precision=lax.Precision.HIGHEST)


def call(kernel, out_shape, *operands, scratch=()):
    return pl.pallas_call(
        kernel,
        out_shape=out_shape,
        in_specs=[pl.BlockSpec(memory_space=pltpu.VMEM)] * len(operands),
        out_specs=jax.tree.map(lambda _: pl.BlockSpec(memory_space=pltpu.VMEM), out_shape),
        scratch_shapes=list(scratch),
        compiler_params=pltpu.CompilerParams(vmem_limit_bytes=50 * 1024 * 1024),
    )(*operands)


def shape(dims, dtype):
    return jax.ShapeDtypeStruct(dims, dtype)


def taps(cells):
    wide = cells.astype(f32)
    columns = cells.shape[1]
    col = lax.broadcasted_iota(jnp.int32, cells.shape, 1)
    left = jnp.where(col == 0, 0.0, pltpu.roll(wide, 1, 1)).astype(bf16)
    right = jnp.where(col == columns - 1, 0.0, pltpu.roll(wide, columns - 1, 1)).astype(bf16)
    merged = jnp.concatenate([left, cells, right], axis=2)
    return merged.reshape(-1, merged.shape[2])


def space_own(cells, weight, part):
    first = taps(cells[:, 0])
    second = taps(cells[:, 1])
    part[0] = dot(first, weight[1]) + dot(second, weight[2])
    part[1] = dot(second, weight[1]) + dot(first, weight[0])


def space_edges(part, above, below, weight):
    at = lax.axis_index("space")
    count = lax.axis_size("space")
    upper = jnp.where(at > 0, above[:, 0], jnp.zeros_like(above[:, 0]))
    lower = jnp.where(at < count - 1, below[:, 0], jnp.zeros_like(below[:, 0]))
    return part[0] + dot(taps(upper), weight[0]), part[1] + dot(taps(lower), weight[2])


def spatial_finish(part, above, below, weight, spatial, first, last):
    rows = space_edges(part, above, below, weight)
    for at, row in enumerate(rows):
        row = row.astype(bf16).reshape(spatial.shape[0], *spatial.shape[2:])
        spatial[:, at] = row
        first[0, at] = row[0]
        last[0, at] = row[-1]


def time_own(cells, weight, part):
    frames, _, _, channels = cells.shape
    flat = cells[...].reshape(-1, channels)
    step = flat.shape[0] // frames
    part[...] = dot(flat, weight[1])
    part[step:] += dot(flat[:-step], weight[0])
    part[:-step] += dot(flat[step:], weight[2])


def time_edges(part, before, after, weight):
    at = lax.axis_index("frame")
    count = lax.axis_size("frame")
    channels = before.shape[-1]
    earlier = jnp.where(at > 0, before[...], jnp.zeros_like(before[...])).reshape(-1, channels)
    later = jnp.where(at < count - 1, after[...], jnp.zeros_like(after[...])).reshape(-1, channels)
    step = earlier.shape[0]
    head = part[:step] + dot(earlier, weight[0])
    tail = part[-step:] + dot(later, weight[2])
    return jnp.concatenate([head, part[step:-step], tail], axis=0)


def members(channels):
    channel = lax.broadcasted_iota(jnp.int32, (channels, LANES), 0)
    group = lax.broadcasted_iota(jnp.int32, (channels, LANES), 1)
    width = channels // GROUPS
    return jnp.where((channel >= group * width) & (channel < (group + 1) * width), 1.0, 0.0)


def spread(statistic, channels):
    return lax.dot_general(
        statistic,
        members(channels),
        (((1,), (1,)), ((), ())),
        preferred_element_type=f32,
        precision=lax.Precision.HIGHEST,
    )


def temporal_finish(part, before, after, weight, temporal, stats, *, frames):
    cells = time_edges(part, before, after, weight)
    temporal[...] = cells
    step = cells.shape[0] // frames
    split = cells.reshape(frames, step, cells.shape[1])
    sums = jnp.concatenate([jnp.sum(split, axis=1), jnp.sum(split * split, axis=1)], axis=0)
    stats[...] = jnp.broadcast_to(dot_exact(sums, members(cells.shape[1]))[None], stats.shape)


def moments(stats, frames, cell_count, channels):
    total = jnp.sum(stats[...], axis=0)
    mean = total[:frames] / cell_count
    inv = lax.rsqrt(total[frames:] / cell_count - mean * mean + 1e-05)
    return spread(mean, channels), spread(inv, channels)


def pairs(half, value):
    row = lax.broadcasted_iota(jnp.int32, (half, 2 * half), 0)
    col = lax.broadcasted_iota(jnp.int32, (half, 2 * half), 1)
    return jnp.where((col == 2 * row) | (col == 2 * row + 1), value, 0.0)


def pack(parts, wide, chunks, payload):
    wide[...] = jnp.zeros_like(wide)
    chunks[...] = jnp.zeros_like(chunks)
    for at, part in parts:
        wide[:, at : at + part.shape[1]] = part.astype(f32)
    pixels = wide.shape[0]
    for k in range(wide.shape[1] // LANES):
        chunks[pl.ds(k, pixels, stride=PAYLOAD), :] = wide[:, k * LANES : (k + 1) * LANES]
    payload[...] = chunks[...].reshape(payload.shape).astype(bf16)


def unpack(payload, wide, chunks):
    chunks[...] = payload[...].astype(f32).reshape(chunks.shape)
    pixels = wide.shape[0]
    for k in range(wide.shape[1] // LANES):
        wide[:, k * LANES : (k + 1) * LANES] = chunks[pl.ds(k, pixels, stride=PAYLOAD), :]


def activation(normed, gain):
    gated = normed * gain
    sig = jax.nn.sigmoid(gated)
    return gated * sig, sig * (1.0 + gated * (1.0 - sig))


def pool_out(
    temporal, stats, cells, gain, grad_heads, cot_in, payload, pooled, wide, chunks, *, cell_count
):
    frames, rows, columns, channels = cells.shape
    mean, inv = moments(stats, frames, cell_count, channels)
    half = columns // 2
    fine = jnp.zeros((columns, channels), f32)
    sway = jnp.zeros((columns, channels), f32)
    for f in range(frames):
        for r in range(rows):
            at = (f * rows + r) * columns
            normed = (temporal[at : at + columns] - mean[f : f + 1]) * inv[f : f + 1]
            silu, slope = activation(normed, gain[...])
            fine += cells[f, r].astype(f32) + silu
            sway += slope * normed
    select = pairs(half, 1.0 / 16.0)
    low = dot_exact(select, fine).astype(bf16)
    pooled[...] = low
    pack(
        [
            (0, low),
            (SLOT, dot_exact(select, sway)),
            (2 * SLOT, cot_in[...]),
            (3 * SLOT, grad_heads[...]),
        ],
        wide,
        chunks,
        payload,
    )


def slopes(temporal, stats, gain, normed_out, slope_out, first, second, inv_out, *, dims, cell_count):
    frames, rows, columns = dims
    channels = temporal.shape[1]
    mean, inv = moments(stats, frames, cell_count, channels)
    inv_out[...] = inv
    select = pairs(columns // 2, 1.0)
    for f in range(frames):
        lead = jnp.zeros((columns, channels), f32)
        sway = jnp.zeros((columns, channels), f32)
        for r in range(rows):
            at = (f * rows + r) * columns
            normed = (temporal[at : at + columns] - mean[f : f + 1]) * inv[f : f + 1]
            slope = activation(normed, gain[...])[1] * gain[...] * (1.0 / 16.0)
            normed_out[at : at + columns] = normed
            slope_out[at : at + columns] = slope
            lead += slope
            sway += slope * normed
        first[f] = dot_exact(select, lead)
        second[f] = dot_exact(select, sway)


def coarse(payload, merged, bias, out, wide, chunks, *, heads, channels):
    unpack(payload, wide, chunks)
    frames = payload.shape[0]
    pooled = wide[:, :channels].astype(bf16)
    sway = wide[:, SLOT : SLOT + channels]
    cot_in = wide[:, 2 * SLOT : 2 * SLOT + channels]
    width = merged.shape[1] // 3
    grad_heads = wide[:, 3 * SLOT : 3 * SLOT + width].astype(bf16)
    depth = width // heads
    factor = 1.0 / math.sqrt(depth)
    qkv = dot(pooled, merged[...]).astype(bf16)
    queries, keys, values = (qkv[:, i * width : (i + 1) * width] for i in range(3))
    row = lax.broadcasted_iota(jnp.int32, (heads, frames, width), 0)
    lane = lax.broadcasted_iota(jnp.int32, (heads, frames, width), 2)
    own = (lane >= row * depth) & (lane < (row + 1) * depth)

    def by_head(matrix):
        tiled = jnp.broadcast_to(matrix.astype(f32)[None], (heads, frames, width))
        return jnp.where(own, tiled, 0.0).astype(bf16).reshape(heads * frames, width)

    def gather(product):
        return jnp.sum(jnp.where(own, product.reshape(heads, frames, width), 0.0), axis=0)

    query_rows = by_head(queries)
    grad_rows = by_head(grad_heads)
    scores = dot_nt(query_rows, keys) * factor + bias[...]
    expd = jnp.exp(scores - jnp.max(scores, axis=1, keepdims=True))
    weights = expd / jnp.sum(expd, axis=1, keepdims=True)
    rounded = weights.astype(bf16)
    blended = gather(dot(rounded, values))
    grad_weights = dot_nt(grad_rows, values)
    grad_values = dot_tn(rounded, grad_rows)
    centre = jnp.sum(weights * grad_weights, axis=1, keepdims=True)
    grad_scores = (weights * (grad_weights - centre)).astype(bf16)
    grad_queries = gather(dot(grad_scores, keys)) * factor
    grad_keys = dot_tn(grad_scores, query_rows) * factor
    grads = jnp.concatenate([grad_queries, grad_keys, grad_values], axis=1).astype(bf16)
    grad_pooled = (cot_in + dot_nt(grads, merged[...])).astype(bf16)
    gain = jnp.sum(grad_pooled.astype(f32) * sway, axis=0, keepdims=True)
    high = gain.astype(bf16).astype(f32)
    pack(
        [
            (0, grad_pooled),
            (SLOT, jnp.broadcast_to(high, (frames, channels))),
            (2 * SLOT, jnp.broadcast_to(gain - high, (frames, channels))),
            (3 * SLOT, blended),
        ],
        wide,
        chunks,
        out,
    )


def totals(payload, first, second, stats, grad_pooled, blended, wide, chunks):
    unpack(payload, wide, chunks)
    frames, _, channels = first.shape
    low = wide[:, :channels]
    grad_pooled[...] = low.astype(bf16)
    blended[...] = wide[:, 3 * SLOT : 3 * SLOT + blended.shape[1]].astype(bf16)
    gain = jnp.sum(wide[:, SLOT : 2 * SLOT] + wide[:, 2 * SLOT : 3 * SLOT], axis=0, keepdims=True)
    sums = jnp.concatenate(
        [jnp.sum(first[...] * low[None], axis=1), jnp.sum(second[...] * low[None], axis=1)], axis=0
    )
    block = jnp.concatenate(
        [
            dot_exact(sums, members(channels)),
            *[gain[:, k * LANES : (k + 1) * LANES] for k in range(SLOT // LANES)],
            jnp.zeros((stats.shape[1] - 2 * frames - SLOT // LANES, LANES), f32),
        ],
        axis=0,
    )
    stats[...] = jnp.broadcast_to(block[None], stats.shape)


def unpooled(grad_pooled):
    half = grad_pooled.shape[0]
    row = lax.broadcasted_iota(jnp.int32, (2 * half, half), 0)
    col = lax.broadcasted_iota(jnp.int32, (2 * half, half), 1)
    grow = jnp.where((row == 2 * col) | (row == 2 * col + 1), 1.0, 0.0).astype(bf16)
    return dot(grow, grad_pooled[...])


def norm_back(
    stats, grad_pooled, normed, slope, inv, grad, first, last, gain, *, cell_count
):
    frames, rows, columns, channels = grad.shape
    total = jnp.sum(stats[...], axis=0)
    for k in range(gain.shape[1] // LANES):
        gain[:, k * LANES : (k + 1) * LANES] = total[2 * frames + k : 2 * frames + k + 1]
    means = spread(total[: 2 * frames] / cell_count, channels)
    grown = unpooled(grad_pooled)
    for f in range(frames):
        for r in range(rows):
            at = (f * rows + r) * columns
            here = slice(at, at + columns)
            value = inv[f : f + 1] * (
                grown * slope[here]
                - means[f : f + 1]
                - normed[here] * means[frames + f : frames + f + 1]
            )
            value = value.astype(bf16)
            grad[f, r] = value
            if f == 0:
                first[0, r] = value
            if f == frames - 1:
                last[0, r] = value


def time_back_finish(part, before, after, weight, grad, top, bottom):
    cells = time_edges(part, before, after, weight).astype(bf16).reshape(grad.shape)
    grad[...] = cells
    top[...] = cells[:, :1]
    bottom[...] = cells[:, -1:]


def space_back_finish(part, above, below, weight, grad_pooled, out):
    grown = unpooled(grad_pooled) * (1.0 / 16.0)
    for at, row in enumerate(space_edges(part, above, below, weight)):
        row = row.reshape(out.shape[0], *out.shape[2:]) + grown[None]
        out[:, at] = row.astype(bf16)


def prepare(cot, proj_in, proj_query, proj_key, proj_value, proj_out, merged, grad_heads, cot_in):
    width = proj_query.shape[1]
    for at, weight in enumerate((proj_query, proj_key, proj_value)):
        merged[:, at * width : (at + 1) * width] = dot(proj_in[...], weight[...]).astype(bf16)
    grad_heads[...] = dot_nt(cot[...], proj_out[...]).astype(bf16)
    cot_in[...] = dot_nt(cot[...], proj_in[...])


def coarse_finish(pooled, proj_in, blended, proj_out, out):
    low = dot(pooled[...], proj_in[...]).astype(bf16).astype(f32)
    out[...] = (low + dot(blended[...], proj_out[...])).astype(bf16)


def neighbours(tail, head, axis):
    count = lax.axis_size(axis)
    return (
        lax.ppermute(tail, axis, [(i, (i + 1) % count) for i in range(count)]),
        lax.ppermute(head, axis, [((i + 1) % count, i) for i in range(count)]),
    )


def exchange(payload, axis):
    return lax.all_to_all(payload, axis, split_axis=0, concat_axis=0, tiled=True)


def local(
    frames_in,
    kernel_space,
    kernel_time,
    norm_gain,
    proj_in,
    proj_query,
    proj_key,
    proj_value,
    proj_out,
    frame_bias,
    cotangent,
):
    frames, rows, columns, channels = frames_in.shape
    bands = lax.axis_size("space")
    cell_count = rows * bands * columns * (channels // GROUPS)
    cells = frames * rows * columns
    half = columns // 2
    heads = frame_bias.shape[0]
    width = proj_query.shape[1]
    depth = cotangent.shape[-1]
    flat = shape((cells, channels), f32)
    edge = shape((1, rows, columns, channels), bf16)
    band = shape(frames_in.shape, bf16)
    gain = norm_gain.reshape(1, channels)
    packing = (
        pltpu.VMEM((half, 3 * SLOT + width), f32),
        pltpu.VMEM((half * PAYLOAD, LANES), f32),
    )
    payload = shape((half, PAYLOAD, LANES), bf16)
    partial = shape((rows, frames * columns, channels), f32)

    weight_space = kernel_space.reshape(3, 3 * channels, channels)
    back_space = jnp.flip(kernel_space, (0, 1)).swapaxes(2, 3).reshape(3, 3 * channels, channels)
    back_time = jnp.flip(kernel_time, 0).swapaxes(1, 2)

    above, below = neighbours(frames_in[:, -1:], frames_in[:, :1], "space")
    part = call(space_own, partial, frames_in, weight_space)
    cot = cotangent.reshape(half, depth)
    merged, grad_heads, cot_in = call(
        prepare,
        (
            shape((channels, 3 * width), bf16),
            shape((half, width), bf16),
            shape((half, channels), f32),
        ),
        cot,
        proj_in,
        proj_query,
        proj_key,
        proj_value,
        proj_out,
    )
    spatial, first, last = call(
        spatial_finish, (band, edge, edge), part, above, below, weight_space
    )
    before, after = neighbours(last, first, "frame")
    part = call(time_own, flat, spatial, kernel_time)
    temporal, stats = call(
        lambda *refs: temporal_finish(*refs, frames=frames),
        (flat, shape((bands, 2 * frames, LANES), f32)),
        part,
        before,
        after,
        kernel_time,
    )
    stats = exchange(stats, "space")
    sent, pooled = call(
        lambda *refs: pool_out(*refs, cell_count=cell_count),
        (payload, shape((half, channels), bf16)),
        temporal,
        stats,
        frames_in,
        gain,
        grad_heads,
        cot_in,
        scratch=packing,
    )
    received = exchange(sent, "frame")
    normed, slope, slope_sum, sway_sum, inv = call(
        lambda *refs: slopes(*refs, dims=(frames, rows, columns), cell_count=cell_count),
        (
            flat,
            flat,
            shape((frames, half, channels), f32),
            shape((frames, half, channels), f32),
            shape((frames, channels), f32),
        ),
        temporal,
        stats,
        gain,
    )
    sent = call(
        lambda *refs: coarse(*refs, heads=heads, channels=channels),
        payload,
        received,
        merged,
        frame_bias.reshape(-1, frame_bias.shape[-1]),
        scratch=packing,
    )
    received = exchange(sent, "frame")
    stats, grad_pooled, blended = call(
        totals,
        (
            shape((bands, 16, LANES), f32),
            shape((half, channels), bf16),
            shape((half, width), bf16),
        ),
        received,
        slope_sum,
        sway_sum,
        scratch=packing,
    )
    stats = exchange(stats, "space")
    coarse_out = call(
        coarse_finish, shape((half, depth), bf16), pooled, proj_in, blended, proj_out
    )
    grad_temporal, first, last, grad_gain = call(
        lambda *refs: norm_back(*refs, cell_count=cell_count),
        (band, edge, edge, shape((1, SLOT), f32)),
        stats,
        grad_pooled,
        normed,
        slope,
        inv,
    )
    before, after = neighbours(last, first, "frame")
    part = call(time_own, flat, grad_temporal, back_time)
    row_edge = shape((frames, 1, columns, channels), bf16)
    grad_spatial, top, bottom = call(
        time_back_finish, (band, row_edge, row_edge), part, before, after, back_time
    )
    above, below = neighbours(bottom, top, "space")
    part = call(space_own, partial, grad_spatial, back_space)
    grad_frames = call(
        space_back_finish, band, part, above, below, back_space, grad_pooled
    )
    return coarse_out.reshape(cotangent.shape), grad_frames, grad_gain[0, :channels]


def solution(mesh):
    in_specs = (
        P("frame", "space", None, None),
        P(),
        P(),
        P(),
        P(),
        P(),
        P(),
        P(),
        P(),
        P(),
        P("frame", "space", None, None),
    )
    out_specs = (P("frame", "space", None, None), P("frame", "space", None, None), P())
    return jax.shard_map(local, mesh=mesh, in_specs=in_specs, out_specs=out_specs, check_vma=False)
```

```python
import math

import jax
import jax.numpy as jnp
from jax import lax
from jax.experimental import pallas as pl
from jax.experimental.pallas import tpu as pltpu
from jax.sharding import PartitionSpec as P

GROUPS = 32
LANES = 128
SLOT = 384
PAYLOAD = 16
bf16 = jnp.bfloat16
f32 = jnp.float32


def dot(a, b):
    return jnp.dot(a, b, preferred_element_type=f32)


def dot_nt(a, b):
    return lax.dot_general(a, b, (((1,), (1,)), ((), ())), preferred_element_type=f32)


def dot_tn(a, b):
    return lax.dot_general(a, b, (((0,), (0,)), ((), ())), preferred_element_type=f32)


def dot_exact(a, b):
    return jnp.dot(a, b, preferred_element_type=f32, precision=lax.Precision.HIGHEST)


def call(kernel, out_shape, *operands, scratch=(), limit=12, far=(), far_out=(), pin=(), after=()):
    count = len(operands)
    near = pl.BlockSpec(memory_space=pltpu.VMEM)
    away = pl.BlockSpec(memory_space=pltpu.HBM)
    single = not isinstance(out_shape, tuple)
    shapes = (out_shape,) if single else out_shape
    out_specs = tuple(away if i in far_out else near for i in range(len(shapes)))
    places = {**{i: pltpu.HBM for i in far_out}, **{i: pltpu.VMEM for i in pin}}
    shapes = tuple(
        places[i](each.shape, each.dtype) if i in places else each for i, each in enumerate(shapes)
    )
    operands = [
        pltpu.with_memory_space_constraint(each, pltpu.HBM) if i in far else each
        for i, each in enumerate(operands)
    ]

    def body(*refs):
        kernel(*refs[:count], *refs[count + len(after) :])

    return pl.pallas_call(
        body,
        out_shape=shapes[0] if single else shapes,
        in_specs=[away if i in far else near for i in range(count)] + [near] * len(after),
        out_specs=out_specs[0] if single else out_specs,
        scratch_shapes=list(scratch),
        compiler_params=pltpu.CompilerParams(vmem_limit_bytes=limit * 1024 * 1024),
    )(*operands, *after)


def start(*copies):
    for source, target, semaphore in copies:
        pltpu.make_async_copy(source, target, semaphore).start()


def wait(*copies):
    for source, target, semaphore in copies:
        pltpu.make_async_copy(source, target, semaphore).wait()


def shape(dims, dtype):
    return jax.ShapeDtypeStruct(dims, dtype)


def taps(cells):
    wide = cells.astype(f32)
    columns = cells.shape[1]
    col = lax.broadcasted_iota(jnp.int32, cells.shape, 1)
    left = jnp.where(col == 0, 0.0, pltpu.roll(wide, 1, 1)).astype(bf16)
    right = jnp.where(col == columns - 1, 0.0, pltpu.roll(wide, columns - 1, 1)).astype(bf16)
    merged = jnp.concatenate([left, cells, right], axis=2)
    return merged.reshape(-1, merged.shape[2])


def space_own(cells, weight, part):
    first = taps(cells[:, 0])
    second = taps(cells[:, 1])
    part[0] = dot(first, weight[1]) + dot(second, weight[2])
    part[1] = dot(second, weight[1]) + dot(first, weight[0])


def space_edges(part, above, below, weight):
    at = lax.axis_index("space")
    count = lax.axis_size("space")
    upper = jnp.where(at > 0, above[:, 0], jnp.zeros_like(above[:, 0]))
    lower = jnp.where(at < count - 1, below[:, 0], jnp.zeros_like(below[:, 0]))
    return part[0] + dot(taps(upper), weight[0]), part[1] + dot(taps(lower), weight[2])


def spatial_finish(part, above, below, weight, spatial, first, last):
    rows = space_edges(part, above, below, weight)
    for at, row in enumerate(rows):
        row = row.astype(bf16).reshape(spatial.shape[0], *spatial.shape[2:])
        spatial[:, at] = row
        first[0, at] = row[0]
        last[0, at] = row[-1]


def time_own(cells, weight, part):
    frames, _, _, channels = cells.shape
    flat = cells[...].reshape(-1, channels)
    step = flat.shape[0] // frames
    part[...] = dot(flat, weight[1])
    part[step:] += dot(flat[:-step], weight[0])
    part[:-step] += dot(flat[step:], weight[2])


def time_edges(part, before, after, weight):
    at = lax.axis_index("frame")
    count = lax.axis_size("frame")
    channels = before.shape[-1]
    earlier = jnp.where(at > 0, before[...], jnp.zeros_like(before[...])).reshape(-1, channels)
    later = jnp.where(at < count - 1, after[...], jnp.zeros_like(after[...])).reshape(-1, channels)
    step = earlier.shape[0]
    head = part[:step] + dot(earlier, weight[0])
    tail = part[-step:] + dot(later, weight[2])
    return jnp.concatenate([head, part[step:-step], tail], axis=0)


def members(channels):
    channel = lax.broadcasted_iota(jnp.int32, (channels, LANES), 0)
    group = lax.broadcasted_iota(jnp.int32, (channels, LANES), 1)
    width = channels // GROUPS
    return jnp.where((channel >= group * width) & (channel < (group + 1) * width), 1.0, 0.0)


def spread(statistic, channels):
    return lax.dot_general(
        statistic,
        members(channels),
        (((1,), (1,)), ((), ())),
        preferred_element_type=f32,
        precision=lax.Precision.HIGHEST,
    )


def temporal_finish(part, before, after, weight, temporal, stats, *, frames):
    cells = time_edges(part, before, after, weight)
    temporal[...] = cells
    step = cells.shape[0] // frames
    split = cells.reshape(frames, step, cells.shape[1])
    sums = jnp.concatenate([jnp.sum(split, axis=1), jnp.sum(split * split, axis=1)], axis=0)
    stats[...] = jnp.broadcast_to(dot_exact(sums, members(cells.shape[1]))[None], stats.shape)


def moments(stats, frames, cell_count, channels):
    total = jnp.sum(stats[...], axis=0)
    mean = total[:frames] / cell_count
    inv = lax.rsqrt(total[frames:] / cell_count - mean * mean + 1e-05)
    return spread(mean, channels), spread(inv, channels)


def pairs(half, value):
    row = lax.broadcasted_iota(jnp.int32, (half, 2 * half), 0)
    col = lax.broadcasted_iota(jnp.int32, (half, 2 * half), 1)
    return jnp.where((col == 2 * row) | (col == 2 * row + 1), value, 0.0)


def pack(parts, wide, chunks, payload):
    wide[...] = jnp.zeros_like(wide)
    chunks[...] = jnp.zeros_like(chunks)
    for at, part in parts:
        wide[:, at : at + part.shape[1]] = part.astype(f32)
    pixels = wide.shape[0]
    for k in range(wide.shape[1] // LANES):
        chunks[pl.ds(k, pixels, stride=PAYLOAD), :] = wide[:, k * LANES : (k + 1) * LANES]
    payload[...] = chunks[...].reshape(payload.shape).astype(bf16)


def unpack(payload, wide, chunks):
    chunks[...] = payload[...].astype(f32).reshape(chunks.shape)
    pixels = wide.shape[0]
    for k in range(wide.shape[1] // LANES):
        wide[:, k * LANES : (k + 1) * LANES] = chunks[pl.ds(k, pixels, stride=PAYLOAD), :]


def activation(normed, gain):
    gated = normed * gain
    sig = jax.nn.sigmoid(gated)
    return gated * sig, sig * (1.0 + gated * (1.0 - sig))


def pool_out(
    temporal, stats, cells, gain, grad_heads, cot_in, payload, pooled, wide, chunks, *, cell_count
):
    frames, rows, columns, channels = cells.shape
    mean, inv = moments(stats, frames, cell_count, channels)
    half = columns // 2
    fine = jnp.zeros((columns, channels), f32)
    sway = jnp.zeros((columns, channels), f32)
    for f in range(frames):
        for r in range(rows):
            at = (f * rows + r) * columns
            normed = (temporal[at : at + columns] - mean[f : f + 1]) * inv[f : f + 1]
            silu, slope = activation(normed, gain[...])
            fine += cells[f, r].astype(f32) + silu
            sway += slope * normed
    select = pairs(half, 1.0 / 16.0)
    low = dot_exact(select, fine).astype(bf16)
    pooled[...] = low
    pack(
        [
            (0, low),
            (SLOT, dot_exact(select, sway)),
            (2 * SLOT, cot_in[...]),
            (3 * SLOT, grad_heads[...]),
        ],
        wide,
        chunks,
        payload,
    )


def slopes(temporal, stats, gain, normed_out, slope_out, first, second, inv_out, *, dims, cell_count):
    frames, rows, columns = dims
    channels = temporal.shape[1]
    mean, inv = moments(stats, frames, cell_count, channels)
    inv_out[...] = inv
    select = pairs(columns // 2, 1.0)
    for f in range(frames):
        lead = jnp.zeros((columns, channels), f32)
        sway = jnp.zeros((columns, channels), f32)
        for r in range(rows):
            at = (f * rows + r) * columns
            normed = (temporal[at : at + columns] - mean[f : f + 1]) * inv[f : f + 1]
            slope = activation(normed, gain[...])[1] * gain[...] * (1.0 / 16.0)
            normed_out[at : at + columns] = normed
            slope_out[at : at + columns] = slope
            lead += slope
            sway += slope * normed
        first[f] = dot_exact(select, lead)
        second[f] = dot_exact(select, sway)


def coarse(payload, merged, bias, out, wide, chunks, bias_here, sems, *, heads, channels):
    bias_copy = (bias, bias_here, sems.at[0])
    start(bias_copy)
    unpack(payload, wide, chunks)
    frames = payload.shape[0]
    pooled = wide[:, :channels].astype(bf16)
    sway = wide[:, SLOT : SLOT + channels]
    cot_in = wide[:, 2 * SLOT : 2 * SLOT + channels]
    width = merged.shape[1] // 3
    grad_heads = wide[:, 3 * SLOT : 3 * SLOT + width].astype(bf16)
    depth = width // heads
    factor = 1.0 / math.sqrt(depth)
    qkv = dot(pooled, merged[...]).astype(bf16)
    queries, keys, values = (qkv[:, i * width : (i + 1) * width] for i in range(3))
    row = lax.broadcasted_iota(jnp.int32, (heads, frames, width), 0)
    lane = lax.broadcasted_iota(jnp.int32, (heads, frames, width), 2)
    own = (lane >= row * depth) & (lane < (row + 1) * depth)

    def by_head(matrix):
        tiled = jnp.broadcast_to(matrix.astype(f32)[None], (heads, frames, width))
        return jnp.where(own, tiled, 0.0).astype(bf16).reshape(heads * frames, width)

    def gather(product):
        return jnp.sum(jnp.where(own, product.reshape(heads, frames, width), 0.0), axis=0)

    query_rows = by_head(queries)
    grad_rows = by_head(grad_heads)
    wait(bias_copy)
    scores = dot_nt(query_rows, keys) * factor + bias_here[...].reshape(heads * frames, frames)
    expd = jnp.exp(scores - jnp.max(scores, axis=1, keepdims=True))
    weights = expd / jnp.sum(expd, axis=1, keepdims=True)
    rounded = weights.astype(bf16)
    blended = gather(dot(rounded, values))
    grad_weights = dot_nt(grad_rows, values)
    grad_values = dot_tn(rounded, grad_rows)
    centre = jnp.sum(weights * grad_weights, axis=1, keepdims=True)
    grad_scores = (weights * (grad_weights - centre)).astype(bf16)
    grad_queries = gather(dot(grad_scores, keys)) * factor
    grad_keys = dot_tn(grad_scores, query_rows) * factor
    grads = jnp.concatenate([grad_queries, grad_keys, grad_values], axis=1).astype(bf16)
    grad_pooled = (cot_in + dot_nt(grads, merged[...])).astype(bf16)
    gain = jnp.sum(grad_pooled.astype(f32) * sway, axis=0, keepdims=True)
    high = gain.astype(bf16).astype(f32)
    pack(
        [
            (0, grad_pooled),
            (SLOT, jnp.broadcast_to(high, (frames, channels))),
            (2 * SLOT, jnp.broadcast_to(gain - high, (frames, channels))),
            (3 * SLOT, blended),
        ],
        wide,
        chunks,
        out,
    )


def totals(payload, first, second, stats, grad_pooled, blended, wide, chunks):
    unpack(payload, wide, chunks)
    frames, _, channels = first.shape
    low = wide[:, :channels]
    grad_pooled[...] = low.astype(bf16)
    blended[...] = wide[:, 3 * SLOT : 3 * SLOT + blended.shape[1]].astype(bf16)
    gain = jnp.sum(wide[:, SLOT : 2 * SLOT] + wide[:, 2 * SLOT : 3 * SLOT], axis=0, keepdims=True)
    sums = jnp.concatenate(
        [jnp.sum(first[...] * low[None], axis=1), jnp.sum(second[...] * low[None], axis=1)], axis=0
    )
    block = jnp.concatenate(
        [
            dot_exact(sums, members(channels)),
            *[gain[:, k * LANES : (k + 1) * LANES] for k in range(SLOT // LANES)],
            jnp.zeros((stats.shape[1] - 2 * frames - SLOT // LANES, LANES), f32),
        ],
        axis=0,
    )
    stats[...] = jnp.broadcast_to(block[None], stats.shape)


def unpooled(grad_pooled):
    half = grad_pooled.shape[0]
    row = lax.broadcasted_iota(jnp.int32, (2 * half, half), 0)
    col = lax.broadcasted_iota(jnp.int32, (2 * half, half), 1)
    grow = jnp.where((row == 2 * col) | (row == 2 * col + 1), 1.0, 0.0).astype(bf16)
    return dot(grow, grad_pooled[...])


def norm_back(
    stats, grad_pooled, normed, slope, inv, grad, first, last, gain, *, cell_count
):
    frames, rows, columns, channels = grad.shape
    total = jnp.sum(stats[...], axis=0)
    for k in range(gain.shape[1] // LANES):
        gain[:, k * LANES : (k + 1) * LANES] = total[2 * frames + k : 2 * frames + k + 1]
    means = spread(total[: 2 * frames] / cell_count, channels)
    grown = unpooled(grad_pooled)
    for f in range(frames):
        for r in range(rows):
            at = (f * rows + r) * columns
            here = slice(at, at + columns)
            value = inv[f : f + 1] * (
                grown * slope[here]
                - means[f : f + 1]
                - normed[here] * means[frames + f : frames + f + 1]
            )
            value = value.astype(bf16)
            grad[f, r] = value
            if f == 0:
                first[0, r] = value
            if f == frames - 1:
                last[0, r] = value


def time_back_finish(part, before, after, weight, grad, top, bottom):
    cells = time_edges(part, before, after, weight).astype(bf16).reshape(grad.shape)
    grad[...] = cells
    top[...] = cells[:, :1]
    bottom[...] = cells[:, -1:]


def space_back_finish(part, above, below, weight, grad_pooled, out):
    grown = unpooled(grad_pooled) * (1.0 / 16.0)
    for at, row in enumerate(space_edges(part, above, below, weight)):
        row = row.reshape(out.shape[0], *out.shape[2:]) + grown[None]
        out[:, at] = row.astype(bf16)


def project_cot(cot, proj_in, proj_out, grad_heads, cot_in, low, high, sems):
    copies = ((proj_in, low, sems.at[0]), (proj_out, high, sems.at[1]))
    start(*copies)
    wait(copies[0])
    cot_in[...] = dot_nt(cot[...], low[...])
    wait(copies[1])
    grad_heads[...] = dot_nt(cot[...], high[...]).astype(bf16)


def merge(proj_in, proj_query, proj_key, proj_value, merged, token, low, weights, sems):
    width = proj_query.shape[1]
    first = (proj_in, low, sems.at[3])
    copies = [
        (weight, weights.at[at], sems.at[at])
        for at, weight in enumerate((proj_query, proj_key, proj_value))
    ]
    start(first, *copies)
    wait(first)
    for at in range(3):
        wait(copies[at])
        merged[:, at * width : (at + 1) * width] = dot(low[...], weights[at]).astype(bf16)
    token[...] = jnp.zeros_like(token)


def turn(kernel_space, kernel_time, back_space, back_time, token, space, turned, time, sems):
    channels = kernel_time.shape[-1]
    inward = ((kernel_time, time, sems.at[0]), (kernel_space, space, sems.at[1]))
    outward = [(turned.at[i], back_space.at[i], sems.at[2 + i]) for i in range(3)]
    start(*inward)
    wait(inward[0])
    for i in range(3):
        back_time[i] = time[2 - i].T
    wait(inward[1])
    for i in range(3):
        for j in range(3):
            turned[i, j * channels : (j + 1) * channels] = space[2 - i, 2 - j].T
        start(outward[i])
    token[...] = jnp.zeros_like(token)
    wait(*outward)


def coarse_finish(pooled, proj_in, blended, proj_out, out, token, low, high, sems):
    copies = ((proj_in, low, sems.at[0]), (proj_out, high, sems.at[1]))
    start(*copies)
    wait(copies[0])
    base = dot(pooled[...], low[...]).astype(bf16).astype(f32)
    wait(copies[1])
    out[...] = (base + dot(blended[...], high[...])).astype(bf16)
    token[...] = jnp.zeros_like(token)


def neighbours(tail, head, axis):
    count = lax.axis_size(axis)
    return (
        lax.ppermute(tail, axis, [(i, (i + 1) % count) for i in range(count)]),
        lax.ppermute(head, axis, [((i + 1) % count, i) for i in range(count)]),
    )


def exchange(payload, axis):
    return lax.all_to_all(payload, axis, split_axis=0, concat_axis=0, tiled=True)


def local(
    frames_in,
    kernel_space,
    kernel_time,
    norm_gain,
    proj_in,
    proj_query,
    proj_key,
    proj_value,
    proj_out,
    frame_bias,
    cotangent,
):
    frames, rows, columns, channels = frames_in.shape
    bands = lax.axis_size("space")
    cell_count = rows * bands * columns * (channels // GROUPS)
    cells = frames * rows * columns
    half = columns // 2
    heads = frame_bias.shape[0]
    width = proj_query.shape[1]
    depth = cotangent.shape[-1]
    flat = shape((cells, channels), f32)
    edge = shape((1, rows, columns, channels), bf16)
    band = shape(frames_in.shape, bf16)
    gain = norm_gain.reshape(1, channels)
    packing = (
        pltpu.VMEM((half, 3 * SLOT + width), f32),
        pltpu.VMEM((half * PAYLOAD, LANES), f32),
    )
    payload = shape((half, PAYLOAD, LANES), bf16)
    partial = shape((rows, frames * columns, channels), f32)

    weight_space = kernel_space.reshape(3, 3 * channels, channels)

    above, below = neighbours(frames_in[:, -1:], frames_in[:, :1], "space")
    part = call(space_own, partial, frames_in, weight_space)
    cot = cotangent.reshape(half, depth)
    token = shape((8, LANES), f32)
    low = pltpu.VMEM(proj_in.shape, bf16)
    high = pltpu.VMEM(proj_out.shape, bf16)
    grad_heads, cot_in = call(
        project_cot,
        (shape((half, width), bf16), shape((half, channels), f32)),
        cot,
        proj_in,
        proj_out,
        scratch=(low, high, pltpu.SemaphoreType.DMA((2,))),
        far=(1, 2),
    )
    spatial, first, last = call(
        spatial_finish,
        (band, edge, edge),
        part,
        above,
        below,
        weight_space,
        after=(cot_in,),
    )
    before, after = neighbours(last, first, "frame")
    part = call(time_own, flat, spatial, kernel_time)
    temporal, stats = call(
        lambda *refs: temporal_finish(*refs, frames=frames),
        (flat, shape((bands, 2 * frames, LANES), f32)),
        part,
        before,
        after,
        kernel_time,
        pin=(0,),
    )
    merged, merged_token = call(
        merge,
        (shape((channels, 3 * width), bf16), token),
        proj_in,
        proj_query,
        proj_key,
        proj_value,
        scratch=(
            low,
            pltpu.VMEM((3, *proj_query.shape), bf16),
            pltpu.SemaphoreType.DMA((4,)),
        ),
        far=(0, 1, 2, 3),
        pin=(0,),
        after=(stats,),
    )
    stats = exchange(stats, "space")
    sent, pooled = call(
        lambda *refs: pool_out(*refs, cell_count=cell_count),
        (payload, shape((half, channels), bf16)),
        temporal,
        stats,
        frames_in,
        gain,
        grad_heads,
        cot_in,
        scratch=packing,
        after=(merged_token,),
    )
    back_space, back_time, turn_token = call(
        turn,
        (shape(weight_space.shape, bf16), shape(kernel_time.shape, bf16), token),
        kernel_space,
        kernel_time,
        scratch=(
            pltpu.VMEM(kernel_space.shape, bf16),
            pltpu.VMEM(weight_space.shape, bf16),
            pltpu.VMEM(kernel_time.shape, bf16),
            pltpu.SemaphoreType.DMA((5,)),
        ),
        far=(0, 1),
        far_out=(0,),
        after=(pooled,),
    )
    received = exchange(sent, "frame")
    normed, slope, slope_sum, sway_sum, inv = call(
        lambda *refs: slopes(*refs, dims=(frames, rows, columns), cell_count=cell_count),
        (
            flat,
            flat,
            shape((frames, half, channels), f32),
            shape((frames, half, channels), f32),
            shape((frames, channels), f32),
        ),
        temporal,
        stats,
        gain,
        pin=(0, 1, 2, 3, 4),
    )
    sent = call(
        lambda *refs: coarse(*refs, heads=heads, channels=channels),
        payload,
        received,
        merged,
        frame_bias,
        scratch=(
            *packing,
            pltpu.VMEM(frame_bias.shape, f32),
            pltpu.SemaphoreType.DMA((1,)),
        ),
        far=(2,),
        after=(turn_token,),
    )
    received = exchange(sent, "frame")
    stats, grad_pooled, blended = call(
        totals,
        (
            shape((bands, 16, LANES), f32),
            shape((half, channels), bf16),
            shape((half, width), bf16),
        ),
        received,
        slope_sum,
        sway_sum,
        scratch=packing,
    )
    coarse_out, coarse_token = call(
        coarse_finish,
        (shape((half, depth), bf16), token),
        pooled,
        proj_in,
        blended,
        proj_out,
        scratch=(low, high, pltpu.SemaphoreType.DMA((2,))),
        far=(1, 3),
        after=(stats,),
    )
    stats = exchange(stats, "space")
    grad_temporal, first, last, grad_gain = call(
        lambda *refs: norm_back(*refs, cell_count=cell_count),
        (band, edge, edge, shape((1, SLOT), f32)),
        stats,
        grad_pooled,
        normed,
        slope,
        inv,
        after=(coarse_token,),
    )
    before, after = neighbours(last, first, "frame")
    part = call(time_own, flat, grad_temporal, back_time)
    row_edge = shape((frames, 1, columns, channels), bf16)
    grad_spatial, top, bottom = call(
        time_back_finish, (band, row_edge, row_edge), part, before, after, back_time
    )
    above, below = neighbours(bottom, top, "space")
    part = call(space_own, partial, grad_spatial, back_space)
    grad_frames = call(
        space_back_finish, band, part, above, below, back_space, grad_pooled
    )
    return coarse_out.reshape(cotangent.shape), grad_frames, grad_gain[0, :channels]


def solution(mesh):
    in_specs = (
        P("frame", "space", None, None),
        P(),
        P(),
        P(),
        P(),
        P(),
        P(),
        P(),
        P(),
        P(),
        P("frame", "space", None, None),
    )
    out_specs = (P("frame", "space", None, None), P("frame", "space", None, None), P())
    return jax.shard_map(local, mesh=mesh, in_specs=in_specs, out_specs=out_specs, check_vma=False)
```

```python
import math

import jax
import jax.numpy as jnp
from jax import lax
from jax.experimental import pallas as pl
from jax.experimental.pallas import tpu as pltpu
from jax.sharding import PartitionSpec as P

GROUPS = 32
LANES = 128
SLOT = 384
PAYLOAD = 16
bf16 = jnp.bfloat16
f32 = jnp.float32


def dot(a, b):
    return jnp.dot(a, b, preferred_element_type=f32)


def dot_nt(a, b):
    return lax.dot_general(a, b, (((1,), (1,)), ((), ())), preferred_element_type=f32)


def dot_tn(a, b):
    return lax.dot_general(a, b, (((0,), (0,)), ((), ())), preferred_element_type=f32)


def dot_exact(a, b):
    return jnp.dot(a, b, preferred_element_type=f32, precision=lax.Precision.HIGHEST)


def call(kernel, out_shape, *operands, scratch=(), limit=12, far=(), far_out=(), pin=(), after=()):
    count = len(operands)
    near = pl.BlockSpec(memory_space=pltpu.VMEM)
    away = pl.BlockSpec(memory_space=pltpu.HBM)
    single = not isinstance(out_shape, tuple)
    shapes = (out_shape,) if single else out_shape
    out_specs = tuple(away if i in far_out else near for i in range(len(shapes)))
    places = {**{i: pltpu.HBM for i in far_out}, **{i: pltpu.VMEM for i in pin}}
    shapes = tuple(
        places[i](each.shape, each.dtype) if i in places else each for i, each in enumerate(shapes)
    )
    operands = [
        pltpu.with_memory_space_constraint(each, pltpu.HBM) if i in far else each
        for i, each in enumerate(operands)
    ]

    def body(*refs):
        kernel(*refs[:count], *refs[count + len(after) :])

    return pl.pallas_call(
        body,
        out_shape=shapes[0] if single else shapes,
        in_specs=[away if i in far else near for i in range(count)] + [near] * len(after),
        out_specs=out_specs[0] if single else out_specs,
        scratch_shapes=list(scratch),
        compiler_params=pltpu.CompilerParams(vmem_limit_bytes=limit * 1024 * 1024),
    )(*operands, *after)


def start(*copies):
    for source, target, semaphore in copies:
        pltpu.make_async_copy(source, target, semaphore).start()


def wait(*copies):
    for source, target, semaphore in copies:
        pltpu.make_async_copy(source, target, semaphore).wait()


def shape(dims, dtype):
    return jax.ShapeDtypeStruct(dims, dtype)


def taps(cells):
    wide = cells.astype(f32)
    columns = cells.shape[1]
    col = lax.broadcasted_iota(jnp.int32, cells.shape, 1)
    left = jnp.where(col == 0, 0.0, pltpu.roll(wide, 1, 1)).astype(bf16)
    right = jnp.where(col == columns - 1, 0.0, pltpu.roll(wide, columns - 1, 1)).astype(bf16)
    return [each.reshape(-1, cells.shape[2]) for each in (left, cells, right)]


def row_sum(cells, weight, i, back):
    if back:
        return sum(dot_nt(cells[j], weight[2 - i, 2 - j]) for j in range(3))
    channels = cells[0].shape[1]
    merged = jnp.concatenate(cells, axis=1)
    return dot(merged, weight[i].reshape(3 * channels, channels))


def space_own(cells, weight_far, part, weight, sems, *, back):
    copies = [(weight_far.at[i], weight.at[i], sems.at[i]) for i in range(3)]
    start(*copies)
    first = taps(cells[:, 0])
    second = taps(cells[:, 1])
    wait(*copies)
    part[0] = row_sum(first, weight, 1, back) + row_sum(second, weight, 2, back)
    part[1] = row_sum(second, weight, 1, back) + row_sum(first, weight, 0, back)


def space_edges(part, above, below, weight, back):
    at = lax.axis_index("space")
    count = lax.axis_size("space")
    upper = jnp.where(at > 0, above[:, 0], jnp.zeros_like(above[:, 0]))
    lower = jnp.where(at < count - 1, below[:, 0], jnp.zeros_like(below[:, 0]))
    return (
        part[0] + row_sum(taps(upper), weight, 0, back),
        part[1] + row_sum(taps(lower), weight, 2, back),
    )


def spatial_finish(part, above, below, weight, spatial, first, last):
    rows = space_edges(part, above, below, weight, False)
    for at, row in enumerate(rows):
        row = row.astype(bf16).reshape(spatial.shape[0], *spatial.shape[2:])
        spatial[:, at] = row
        first[0, at] = row[0]
        last[0, at] = row[-1]


def time_own(cells, weight_far, part, weight, sems):
    copy = (weight_far, weight, sems.at[0])
    start(copy)
    frames, _, _, channels = cells.shape
    flat = cells[...].reshape(-1, channels)
    step = flat.shape[0] // frames
    wait(copy)
    part[...] = dot(flat, weight[1])
    part[step:] += dot(flat[:-step], weight[0])
    part[:-step] += dot(flat[step:], weight[2])


def time_edges(part, before, after, weight):
    at = lax.axis_index("frame")
    count = lax.axis_size("frame")
    channels = before.shape[-1]
    earlier = jnp.where(at > 0, before[...], jnp.zeros_like(before[...])).reshape(-1, channels)
    later = jnp.where(at < count - 1, after[...], jnp.zeros_like(after[...])).reshape(-1, channels)
    step = earlier.shape[0]
    head = part[:step] + dot(earlier, weight[0])
    tail = part[-step:] + dot(later, weight[2])
    return jnp.concatenate([head, part[step:-step], tail], axis=0)


def members(channels):
    channel = lax.broadcasted_iota(jnp.int32, (channels, LANES), 0)
    group = lax.broadcasted_iota(jnp.int32, (channels, LANES), 1)
    width = channels // GROUPS
    return jnp.where((channel >= group * width) & (channel < (group + 1) * width), 1.0, 0.0)


def spread(statistic, channels):
    return lax.dot_general(
        statistic,
        members(channels),
        (((1,), (1,)), ((), ())),
        preferred_element_type=f32,
        precision=lax.Precision.HIGHEST,
    )


def temporal_finish(part, before, after, weight, temporal, stats, *, frames):
    cells = time_edges(part, before, after, weight)
    temporal[...] = cells
    step = cells.shape[0] // frames
    split = cells.reshape(frames, step, cells.shape[1])
    sums = jnp.concatenate([jnp.sum(split, axis=1), jnp.sum(split * split, axis=1)], axis=0)
    stats[...] = jnp.broadcast_to(dot_exact(sums, members(cells.shape[1]))[None], stats.shape)


def moments(stats, frames, cell_count, channels):
    total = jnp.sum(stats[...], axis=0)
    mean = total[:frames] / cell_count
    inv = lax.rsqrt(total[frames:] / cell_count - mean * mean + 1e-05)
    return spread(mean, channels), spread(inv, channels)


def pairs(half, value):
    row = lax.broadcasted_iota(jnp.int32, (half, 2 * half), 0)
    col = lax.broadcasted_iota(jnp.int32, (half, 2 * half), 1)
    return jnp.where((col == 2 * row) | (col == 2 * row + 1), value, 0.0)


def pack(parts, wide, chunks, payload):
    wide[...] = jnp.zeros_like(wide)
    chunks[...] = jnp.zeros_like(chunks)
    for at, part in parts:
        wide[:, at : at + part.shape[1]] = part.astype(f32)
    pixels = wide.shape[0]
    for k in range(wide.shape[1] // LANES):
        chunks[pl.ds(k, pixels, stride=PAYLOAD), :] = wide[:, k * LANES : (k + 1) * LANES]
    payload[...] = chunks[...].reshape(payload.shape).astype(bf16)


def unpack(payload, wide, chunks):
    chunks[...] = payload[...].astype(f32).reshape(chunks.shape)
    pixels = wide.shape[0]
    for k in range(wide.shape[1] // LANES):
        wide[:, k * LANES : (k + 1) * LANES] = chunks[pl.ds(k, pixels, stride=PAYLOAD), :]


def activation(normed, gain):
    gated = normed * gain
    sig = jax.nn.sigmoid(gated)
    return gated * sig, sig * (1.0 + gated * (1.0 - sig))


def pool_out(
    temporal, stats, cells, gain, grad_heads, cot_in, payload, pooled, wide, chunks, *, cell_count
):
    frames, rows, columns, channels = cells.shape
    mean, inv = moments(stats, frames, cell_count, channels)
    half = columns // 2
    fine = jnp.zeros((columns, channels), f32)
    sway = jnp.zeros((columns, channels), f32)
    for f in range(frames):
        for r in range(rows):
            at = (f * rows + r) * columns
            normed = (temporal[at : at + columns] - mean[f : f + 1]) * inv[f : f + 1]
            silu, slope = activation(normed, gain[...])
            fine += cells[f, r].astype(f32) + silu
            sway += slope * normed
    select = pairs(half, 1.0 / 16.0)
    low = dot_exact(select, fine).astype(bf16)
    pooled[...] = low
    pack(
        [
            (0, low),
            (SLOT, dot_exact(select, sway)),
            (2 * SLOT, cot_in[...]),
            (3 * SLOT, grad_heads[...]),
        ],
        wide,
        chunks,
        payload,
    )


def slopes(
    temporal,
    stats,
    gain,
    normed_out,
    slope_out,
    first,
    second,
    inv_out,
    head,
    tail,
    token,
    *,
    dims,
    cell_count,
):
    frames, rows, columns = dims
    channels = temporal.shape[1]
    step = rows * columns
    mean, inv = moments(stats, frames, cell_count, channels)
    inv_out[...] = inv
    for f in range(frames):
        here = slice(f * step, (f + 1) * step)
        normed = (temporal[here] - mean[f : f + 1]) * inv[f : f + 1]
        slope = slope_of(normed, gain)
        normed_out[here] = normed.astype(bf16)
        slope_out[here] = slope.astype(bf16)
        first[f] = by_pixel(slope, rows, columns)
        second[f] = by_pixel(slope * normed, rows, columns)
    for f, edge in ((0, head), (frames - 1, tail)):
        high = inv[f : f + 1].astype(bf16).astype(f32)
        edge[:step] = normed_out[f * step : (f + 1) * step]
        edge[step:] = jnp.concatenate(
            [high, inv[f : f + 1] - high, jnp.zeros((edge.shape[0] - step - 2, channels), f32)],
            axis=0,
        ).astype(bf16)
    token[...] = jnp.zeros_like(token)


def slope_of(normed, gain):
    return activation(normed, gain[...])[1] * gain[...] * (1.0 / 16.0)


def by_pixel(cells, rows, columns):
    total = cells[:columns]
    for r in range(1, rows):
        total = total + cells[r * columns : (r + 1) * columns]
    return dot_exact(pairs(columns // 2, 1.0), total)


def slopes_beside(before, after, gain, slope_out, first, second, inv_out, *, dims):
    _, rows, columns = dims
    step = rows * columns
    for at, edge in enumerate((before, after)):
        normed = edge[:step].astype(f32)
        extra = edge[step:].astype(f32)
        inv_out[at : at + 1] = extra[0:1] + extra[1:2]
        slope = slope_of(normed, gain)
        slope_out[at] = slope.astype(bf16)
        first[at] = by_pixel(slope, rows, columns)
        second[at] = by_pixel(slope * normed, rows, columns)


def coarse(payload, merged, bias, out, wide, out_wide, chunks, bias_here, sems, *, heads, channels):
    bias_copy = (bias, bias_here, sems.at[0])
    start(bias_copy)
    unpack(payload, wide, chunks)
    frames = payload.shape[0]
    pooled = wide[:, :channels].astype(bf16)
    sway = wide[:, SLOT : SLOT + channels]
    cot_in = wide[:, 2 * SLOT : 2 * SLOT + channels]
    width = merged.shape[1] // 3
    grad_heads = wide[:, 3 * SLOT : 3 * SLOT + width].astype(bf16)
    depth = width // heads
    factor = 1.0 / math.sqrt(depth)
    qkv = dot(pooled, merged[...]).astype(bf16)
    queries, keys, values = (qkv[:, i * width : (i + 1) * width] for i in range(3))
    row = lax.broadcasted_iota(jnp.int32, (heads, frames, width), 0)
    lane = lax.broadcasted_iota(jnp.int32, (heads, frames, width), 2)
    own = (lane >= row * depth) & (lane < (row + 1) * depth)

    def by_head(matrix):
        tiled = jnp.broadcast_to(matrix.astype(f32)[None], (heads, frames, width))
        return jnp.where(own, tiled, 0.0).astype(bf16).reshape(heads * frames, width)

    def gather(product):
        return jnp.sum(jnp.where(own, product.reshape(heads, frames, width), 0.0), axis=0)

    query_rows = by_head(queries)
    grad_rows = by_head(grad_heads)
    wait(bias_copy)
    scores = dot_nt(query_rows, keys) * factor + bias_here[...].reshape(heads * frames, frames)
    expd = jnp.exp(scores - jnp.max(scores, axis=1, keepdims=True))
    weights = expd / jnp.sum(expd, axis=1, keepdims=True)
    rounded = weights.astype(bf16)
    blended = gather(dot(rounded, values))
    grad_weights = dot_nt(grad_rows, values)
    grad_values = dot_tn(rounded, grad_rows)
    centre = jnp.sum(weights * grad_weights, axis=1, keepdims=True)
    grad_scores = (weights * (grad_weights - centre)).astype(bf16)
    grad_queries = gather(dot(grad_scores, keys)) * factor
    grad_keys = dot_tn(grad_scores, query_rows) * factor
    grads = jnp.concatenate([grad_queries, grad_keys, grad_values], axis=1).astype(bf16)
    grad_pooled = (cot_in + dot_nt(grads, merged[...])).astype(bf16)
    low = grad_pooled.astype(f32)
    gain = jnp.sum(low * sway, axis=0, keepdims=True)
    outside = jnp.zeros((1, channels), f32)
    pack(
        [
            (0, jnp.concatenate([outside, low[:-1]], axis=0)),
            (channels, low),
            (2 * channels, jnp.concatenate([low[1:], outside], axis=0)),
            (3 * channels, jnp.broadcast_to(gain, (frames, channels))),
            (4 * channels, blended),
        ],
        out_wide,
        chunks,
        out,
    )


def totals(
    payload, first, second, beside_first, beside_second, stats, grad_pooled, blended, wide, chunks
):
    unpack(payload, wide, chunks)
    frames, _, channels = first.shape
    lows = [wide[:, i * channels : (i + 1) * channels] for i in range(3)]
    for i, low in enumerate(lows):
        grad_pooled[i] = low.astype(bf16)
    blended[...] = wide[:, 4 * channels : 4 * channels + blended.shape[1]].astype(bf16)
    gain = jnp.sum(wide[:, 3 * channels : 4 * channels], axis=0, keepdims=True)

    def over(own, beside):
        return [
            jnp.sum(beside[0] * lows[0], axis=0, keepdims=True),
            jnp.sum(own[...] * lows[1][None], axis=1),
            jnp.sum(beside[1] * lows[2], axis=0, keepdims=True),
        ]

    sums = jnp.concatenate(
        [*over(first, beside_first), *over(second, beside_second)], axis=0
    )
    gain = jnp.concatenate([gain, jnp.zeros((1, SLOT - channels), f32)], axis=1)
    count = 2 * (frames + 2)
    block = jnp.concatenate(
        [
            dot_exact(sums, members(channels)),
            *[gain[:, k * LANES : (k + 1) * LANES] for k in range(SLOT // LANES)],
            jnp.zeros((stats.shape[1] - count - SLOT // LANES, LANES), f32),
        ],
        axis=0,
    )
    stats[...] = jnp.broadcast_to(block[None], stats.shape)


def unpooled(grad_pooled):
    half = grad_pooled.shape[0]
    row = lax.broadcasted_iota(jnp.int32, (2 * half, half), 0)
    col = lax.broadcasted_iota(jnp.int32, (2 * half, half), 1)
    grow = jnp.where((row == 2 * col) | (row == 2 * col + 1), 1.0, 0.0).astype(bf16)
    return dot(grow, grad_pooled)


def norm_back(
    stats,
    grad_pooled,
    normed,
    slope,
    inv,
    before,
    after,
    beside_slope,
    beside_inv,
    weight,
    grad,
    top,
    bottom,
    gain,
    cells,
    time,
    sems,
    *,
    cell_count,
):
    copy = (weight, time, sems.at[0])
    start(copy)
    frames, rows, columns, channels = grad.shape
    step = rows * columns
    count = frames + 2
    total = jnp.sum(stats[...], axis=0)
    for k in range(gain.shape[1] // LANES):
        gain[:, k * LANES : (k + 1) * LANES] = total[2 * count + k : 2 * count + k + 1]
    means = spread(total[: 2 * count] / cell_count, channels)
    at = lax.axis_index("frame")
    last = lax.axis_size("frame") - 1

    def back(f, low, cells_normed, cells_slope, scale):
        grown = unpooled(low)
        grown = jnp.concatenate([grown] * rows, axis=0)
        return scale * (
            grown * cells_slope.astype(f32)
            - means[f : f + 1]
            - cells_normed.astype(f32) * means[count + f : count + f + 1]
        )

    early = back(0, grad_pooled[0], before[:step], beside_slope[0], beside_inv[0:1])
    cells[:step] = jnp.where(at > 0, early, 0.0).astype(bf16)
    for f in range(frames):
        here = slice(f * step, (f + 1) * step)
        value = back(f + 1, grad_pooled[1], normed[here], slope[here], inv[f : f + 1])
        cells[(f + 1) * step : (f + 2) * step] = value.astype(bf16)
    late = back(
        count - 1, grad_pooled[2], after[:step], beside_slope[1], beside_inv[1:2]
    )
    cells[(count - 1) * step :] = jnp.where(at < last, late, 0.0).astype(bf16)
    size = frames * step
    wait(copy)
    sums = dot_nt(cells[:size], time[2])
    sums += dot_nt(cells[step : step + size], time[1])
    sums += dot_nt(cells[2 * step :], time[0])
    spatial = sums.astype(bf16).reshape(grad.shape)
    grad[...] = spatial
    top[...] = spatial[:, :1]
    bottom[...] = spatial[:, -1:]


def space_back_finish(part, above, below, weight, grad_pooled, out):
    grown = unpooled(grad_pooled[1]) * (1.0 / 16.0)
    for at, row in enumerate(space_edges(part, above, below, weight, True)):
        row = row.reshape(out.shape[0], *out.shape[2:]) + grown[None]
        out[:, at] = row.astype(bf16)


def project_cot(cot, proj_in, proj_out, grad_heads, cot_in, low, high, sems):
    copies = ((proj_in, low, sems.at[0]), (proj_out, high, sems.at[1]))
    start(*copies)
    wait(copies[0])
    cot_in[...] = dot_nt(cot[...], low[...])
    wait(copies[1])
    grad_heads[...] = dot_nt(cot[...], high[...]).astype(bf16)


def merge(proj_in, proj_query, proj_key, proj_value, merged, token, low, weights, sems):
    width = proj_query.shape[1]
    first = (proj_in, low, sems.at[3])
    copies = [
        (weight, weights.at[at], sems.at[at])
        for at, weight in enumerate((proj_query, proj_key, proj_value))
    ]
    start(first, *copies)
    wait(first)
    for at in range(3):
        wait(copies[at])
        merged[:, at * width : (at + 1) * width] = dot(low[...], weights[at]).astype(bf16)
    token[...] = jnp.zeros_like(token)


def coarse_finish(pooled, proj_in, blended, proj_out, out, token, low, high, sems):
    copies = ((proj_in, low, sems.at[0]), (proj_out, high, sems.at[1]))
    start(*copies)
    wait(copies[0])
    base = dot(pooled[...], low[...]).astype(bf16).astype(f32)
    wait(copies[1])
    out[...] = (base + dot(blended[...], high[...])).astype(bf16)
    token[...] = jnp.zeros_like(token)


def neighbours(tail, head, axis):
    count = lax.axis_size(axis)
    return (
        lax.ppermute(tail, axis, [(i, (i + 1) % count) for i in range(count)]),
        lax.ppermute(head, axis, [((i + 1) % count, i) for i in range(count)]),
    )


def exchange(payload, axis):
    return lax.all_to_all(payload, axis, split_axis=0, concat_axis=0, tiled=True)


def local(
    frames_in,
    kernel_space,
    kernel_time,
    norm_gain,
    proj_in,
    proj_query,
    proj_key,
    proj_value,
    proj_out,
    frame_bias,
    cotangent,
):
    frames, rows, columns, channels = frames_in.shape
    bands = lax.axis_size("space")
    cell_count = rows * bands * columns * (channels // GROUPS)
    cells = frames * rows * columns
    half = columns // 2
    heads = frame_bias.shape[0]
    width = proj_query.shape[1]
    depth = cotangent.shape[-1]
    flat = shape((cells, channels), f32)
    low_flat = shape((cells, channels), bf16)
    edge = shape((1, rows, columns, channels), bf16)
    band = shape(frames_in.shape, bf16)
    gain = norm_gain.reshape(1, channels)
    packing = (
        pltpu.VMEM((half, 3 * SLOT + width), f32),
        pltpu.VMEM((half * PAYLOAD, LANES), f32),
    )
    payload = shape((half, PAYLOAD, LANES), bf16)
    partial = shape((rows, frames * columns, channels), f32)

    above, below = neighbours(frames_in[:, -1:], frames_in[:, :1], "space")
    space_here = shape(kernel_space.shape, bf16)
    part, weight = call(
        lambda *refs: space_own(*refs, back=False),
        (partial, space_here),
        frames_in,
        kernel_space,
        scratch=(pltpu.SemaphoreType.DMA((3,)),),
        far=(1,),
        pin=(0, 1),
    )
    cot = cotangent.reshape(half, depth)
    token = shape((8, LANES), f32)
    low = pltpu.VMEM(proj_in.shape, bf16)
    high = pltpu.VMEM(proj_out.shape, bf16)
    grad_heads, cot_in = call(
        project_cot,
        (shape((half, width), bf16), shape((half, channels), f32)),
        cot,
        proj_in,
        proj_out,
        scratch=(low, high, pltpu.SemaphoreType.DMA((2,))),
        far=(1, 2),
    )
    spatial, first, last = call(
        spatial_finish,
        (band, edge, edge),
        part,
        above,
        below,
        weight,
        after=(cot_in,),
    )
    before, after = neighbours(last, first, "frame")
    part, weight = call(
        time_own,
        (flat, shape(kernel_time.shape, bf16)),
        spatial,
        kernel_time,
        scratch=(pltpu.SemaphoreType.DMA((1,)),),
        far=(1,),
        pin=(0, 1),
    )
    temporal, stats = call(
        lambda *refs: temporal_finish(*refs, frames=frames),
        (flat, shape((bands, 2 * frames, LANES), f32)),
        part,
        before,
        after,
        weight,
        pin=(0,),
    )
    merged, merged_token = call(
        merge,
        (shape((channels, 3 * width), bf16), token),
        proj_in,
        proj_query,
        proj_key,
        proj_value,
        scratch=(
            low,
            pltpu.VMEM((3, *proj_query.shape), bf16),
            pltpu.SemaphoreType.DMA((4,)),
        ),
        far=(0, 1, 2, 3),
        pin=(0,),
        after=(stats,),
    )
    stats = exchange(stats, "space")
    sent, pooled = call(
        lambda *refs: pool_out(*refs, cell_count=cell_count),
        (payload, shape((half, channels), bf16)),
        temporal,
        stats,
        frames_in,
        gain,
        grad_heads,
        cot_in,
        scratch=packing,
        after=(merged_token,),
    )
    received = exchange(sent, "frame")
    dims = (frames, rows, columns)
    pixels = shape((frames, half, channels), f32)
    beside_pixels = shape((2, half, channels), f32)
    edge_frame = shape((rows * columns + 16, channels), bf16)
    normed, slope, slope_sum, sway_sum, inv, head, tail, slopes_token = call(
        lambda *refs: slopes(*refs, dims=dims, cell_count=cell_count),
        (low_flat, low_flat, pixels, pixels, shape((frames, channels), f32), edge_frame, edge_frame, token),
        temporal,
        stats,
        gain,
        pin=(0, 1, 2, 3, 4),
        after=(pooled,),
    )
    before, after = neighbours(tail, head, "frame")
    sent = call(
        lambda *refs: coarse(*refs, heads=heads, channels=channels),
        payload,
        received,
        merged,
        frame_bias,
        scratch=(
            packing[0],
            pltpu.VMEM((half, 4 * channels + width), f32),
            packing[1],
            pltpu.VMEM(frame_bias.shape, f32),
            pltpu.SemaphoreType.DMA((1,)),
        ),
        far=(2,),
        after=(slopes_token,),
    )
    beside_slope, beside_first, beside_second, beside_inv = call(
        lambda *refs: slopes_beside(*refs, dims=dims),
        (
            shape((2, rows * columns, channels), bf16),
            beside_pixels,
            beside_pixels,
            shape((2, channels), f32),
        ),
        before,
        after,
        gain,
        pin=(0, 1, 2, 3),
    )
    received = exchange(sent, "frame")
    stats, grad_pooled, blended = call(
        totals,
        (
            shape((bands, 16, LANES), f32),
            shape((3, half, channels), bf16),
            shape((half, width), bf16),
        ),
        received,
        slope_sum,
        sway_sum,
        beside_first,
        beside_second,
        scratch=(pltpu.VMEM((half, 4 * channels + width), f32), packing[1]),
    )
    coarse_out, coarse_token = call(
        coarse_finish,
        (shape((half, depth), bf16), token),
        pooled,
        proj_in,
        blended,
        proj_out,
        scratch=(low, high, pltpu.SemaphoreType.DMA((2,))),
        far=(1, 3),
        after=(stats,),
    )
    stats = exchange(stats, "space")
    row_edge = shape((frames, 1, columns, channels), bf16)
    grad_spatial, top, bottom, grad_gain = call(
        lambda *refs: norm_back(*refs, cell_count=cell_count),
        (band, row_edge, row_edge, shape((1, SLOT), f32)),
        stats,
        grad_pooled,
        normed,
        slope,
        inv,
        before,
        after,
        beside_slope,
        beside_inv,
        kernel_time,
        scratch=(
            pltpu.VMEM(((frames + 2) * rows * columns, channels), bf16),
            pltpu.VMEM(kernel_time.shape, bf16),
            pltpu.SemaphoreType.DMA((1,)),
        ),
        far=(9,),
        after=(coarse_token,),
    )
    above, below = neighbours(bottom, top, "space")
    part, weight = call(
        lambda *refs: space_own(*refs, back=True),
        (partial, space_here),
        grad_spatial,
        kernel_space,
        scratch=(pltpu.SemaphoreType.DMA((3,)),),
        far=(1,),
        pin=(0, 1),
    )
    grad_frames = call(space_back_finish, band, part, above, below, weight, grad_pooled)
    return coarse_out.reshape(cotangent.shape), grad_frames, grad_gain[0, :channels]


def solution(mesh):
    in_specs = (
        P("frame", "space", None, None),
        P(),
        P(),
        P(),
        P(),
        P(),
        P(),
        P(),
        P(),
        P(),
        P("frame", "space", None, None),
    )
    out_specs = (P("frame", "space", None, None), P("frame", "space", None, None), P())
    return jax.shard_map(local, mesh=mesh, in_specs=in_specs, out_specs=out_specs, check_vma=False)
```

```python
import math

import jax
import jax.numpy as jnp
from jax import lax
from jax.experimental import pallas as pl
from jax.experimental.pallas import tpu as pltpu
from jax.sharding import PartitionSpec as P

GROUPS = 32
LANES = 128
SLOT = 384
PAYLOAD = 16
bf16 = jnp.bfloat16
f32 = jnp.float32


def dot(a, b):
    return jnp.dot(a, b, preferred_element_type=f32)


def dot_nt(a, b):
    return lax.dot_general(a, b, (((1,), (1,)), ((), ())), preferred_element_type=f32)


def dot_tn(a, b):
    return lax.dot_general(a, b, (((0,), (0,)), ((), ())), preferred_element_type=f32)


def dot_exact(a, b):
    return jnp.dot(a, b, preferred_element_type=f32, precision=lax.Precision.HIGHEST)


def call(kernel, out_shape, *operands, scratch=(), limit=12, far=(), far_out=(), pin=(), after=()):
    count = len(operands)
    near = pl.BlockSpec(memory_space=pltpu.VMEM)
    away = pl.BlockSpec(memory_space=pltpu.HBM)
    single = not isinstance(out_shape, tuple)
    shapes = (out_shape,) if single else out_shape
    out_specs = tuple(away if i in far_out else near for i in range(len(shapes)))
    places = {**{i: pltpu.HBM for i in far_out}, **{i: pltpu.VMEM for i in pin}}
    shapes = tuple(
        places[i](each.shape, each.dtype) if i in places else each for i, each in enumerate(shapes)
    )
    operands = [
        pltpu.with_memory_space_constraint(each, pltpu.HBM) if i in far else each
        for i, each in enumerate(operands)
    ]

    def body(*refs):
        kernel(*refs[:count], *refs[count + len(after) :])

    return pl.pallas_call(
        body,
        out_shape=shapes[0] if single else shapes,
        in_specs=[away if i in far else near for i in range(count)] + [near] * len(after),
        out_specs=out_specs[0] if single else out_specs,
        scratch_shapes=list(scratch),
        compiler_params=pltpu.CompilerParams(vmem_limit_bytes=limit * 1024 * 1024),
    )(*operands, *after)


def start(*copies):
    for source, target, semaphore in copies:
        pltpu.make_async_copy(source, target, semaphore).start()


def wait(*copies):
    for source, target, semaphore in copies:
        pltpu.make_async_copy(source, target, semaphore).wait()


def shape(dims, dtype):
    return jax.ShapeDtypeStruct(dims, dtype)


def taps(cells):
    wide = cells.astype(f32)
    columns = cells.shape[1]
    col = lax.broadcasted_iota(jnp.int32, cells.shape, 1)
    left = jnp.where(col == 0, 0.0, pltpu.roll(wide, 1, 1)).astype(bf16)
    right = jnp.where(col == columns - 1, 0.0, pltpu.roll(wide, columns - 1, 1)).astype(bf16)
    return [each.reshape(-1, cells.shape[2]) for each in (left, cells, right)]


def row_sum(cells, weight, i, back):
    if back:
        return sum(dot_nt(cells[j], weight[2 - i, 2 - j]) for j in range(3))
    channels = cells[0].shape[1]
    merged = jnp.concatenate(cells, axis=1)
    return dot(merged, weight[i].reshape(3 * channels, channels))


def rims(cells, outer_top, outer_bottom, inner_top, inner_bottom, sems):
    last = cells.shape[0] - 1
    copies = []
    for row, (outer, inner) in ((0, (outer_top, inner_top)), (1, (outer_bottom, inner_bottom))):
        copies += [
            (cells.at[0, row], outer.at[0], sems.at[row, 0]),
            (cells.at[last, row], outer.at[1], sems.at[row, 1]),
            (cells.at[pl.ds(1, last - 1), row], inner, sems.at[row, 2]),
        ]
    start(*copies)
    wait(*copies)


def space_first(cells_far, weight_far, part, weight, cells, sems, cells_sem):
    copy = (cells_far, cells, cells_sem.at[0])
    start(copy)
    space_own(cells, weight_far, part, weight, sems, back=False, copy=copy)


def space_own(cells, weight_far, part, weight, sems, *, back, copy=None):
    copies = [(weight_far.at[i], weight.at[i], sems.at[i]) for i in range(3)]
    start(*copies)
    if copy:
        wait(copy)
    first = taps(cells[:, 0])
    second = taps(cells[:, 1])
    wait(*copies)
    part[0] = row_sum(first, weight, 1, back) + row_sum(second, weight, 2, back)
    part[1] = row_sum(second, weight, 1, back) + row_sum(first, weight, 0, back)


def inside(above, below):
    at = lax.axis_index("space")
    last = lax.axis_size("space") - 1
    return (
        jnp.where(at > 0, above, jnp.zeros_like(above)),
        jnp.where(at < last, below, jnp.zeros_like(below)),
    )


def space_edges(part, above, below, weight, back):
    upper, lower = inside(above[:, 0], below[:, 0])
    return (
        part[0] + row_sum(taps(upper), weight, 0, back),
        part[1] + row_sum(taps(lower), weight, 2, back),
    )


def spatial_outer(part, above, below, weight, first, last):
    columns = above.shape[1]
    for r, (i, rim) in enumerate(zip((0, 2), inside(above[...], below[...]))):
        own = jnp.concatenate([part[r, :columns], part[r, -columns:]], axis=0)
        row = (own + row_sum(taps(rim), weight, i, False)).astype(bf16)
        first[0, r] = row[:columns]
        last[0, r] = row[columns:]


def spatial_inner(part, above, below, weight, first, last, time_far, sums, time, cells, sems):
    copy = (time_far, time, sems.at[0])
    start(copy)
    columns = above.shape[1]
    frames, rows = cells.shape[:2]
    for r, (i, rim) in enumerate(zip((0, 2), inside(above[...], below[...]))):
        row = part[r, columns:-columns] + row_sum(taps(rim), weight, i, False)
        cells[1 : frames - 1, r] = row.astype(bf16).reshape(frames - 2, *cells.shape[2:])
    cells[0] = first[0]
    cells[frames - 1] = last[0]
    wait(copy)
    time_own(cells, time, sums)


def time_own(cells, weight, part):
    frames, _, _, channels = cells.shape
    flat = cells[...].reshape(-1, channels)
    step = flat.shape[0] // frames
    part[...] = dot(flat, weight[1])
    part[step:] += dot(flat[:-step], weight[0])
    part[:-step] += dot(flat[step:], weight[2])


def time_edges(part, before, after, weight):
    at = lax.axis_index("frame")
    count = lax.axis_size("frame")
    channels = before.shape[-1]
    earlier = jnp.where(at > 0, before[...], jnp.zeros_like(before[...])).reshape(-1, channels)
    later = jnp.where(at < count - 1, after[...], jnp.zeros_like(after[...])).reshape(-1, channels)
    step = earlier.shape[0]
    head = part[:step] + dot(earlier, weight[0])
    tail = part[-step:] + dot(later, weight[2])
    return jnp.concatenate([head, part[step:-step], tail], axis=0)


def members(channels):
    channel = lax.broadcasted_iota(jnp.int32, (channels, LANES), 0)
    group = lax.broadcasted_iota(jnp.int32, (channels, LANES), 1)
    width = channels // GROUPS
    return jnp.where((channel >= group * width) & (channel < (group + 1) * width), 1.0, 0.0)


def spread(statistic, channels):
    return lax.dot_general(
        statistic,
        members(channels),
        (((1,), (1,)), ((), ())),
        preferred_element_type=f32,
        precision=lax.Precision.HIGHEST,
    )


def temporal_finish(part, before, after, weight, temporal, stats, *, frames):
    cells = time_edges(part, before, after, weight)
    temporal[...] = cells
    step = cells.shape[0] // frames
    split = cells.reshape(frames, step, cells.shape[1])
    sums = jnp.concatenate([jnp.sum(split, axis=1), jnp.sum(split * split, axis=1)], axis=0)
    stats[...] = jnp.broadcast_to(dot_exact(sums, members(cells.shape[1]))[None], stats.shape)


def moments(stats, frames, cell_count, channels):
    total = jnp.sum(stats[...], axis=0)
    mean = total[:frames] / cell_count
    inv = lax.rsqrt(total[frames:] / cell_count - mean * mean + 1e-05)
    return spread(mean, channels), spread(inv, channels)


def pairs(half, value):
    row = lax.broadcasted_iota(jnp.int32, (half, 2 * half), 0)
    col = lax.broadcasted_iota(jnp.int32, (half, 2 * half), 1)
    return jnp.where((col == 2 * row) | (col == 2 * row + 1), value, 0.0)


def pack(parts, wide, chunks, payload):
    wide[...] = jnp.zeros_like(wide)
    chunks[...] = jnp.zeros_like(chunks)
    for at, part in parts:
        wide[:, at : at + part.shape[1]] = part.astype(f32)
    pixels = wide.shape[0]
    for k in range(wide.shape[1] // LANES):
        chunks[pl.ds(k, pixels, stride=PAYLOAD), :] = wide[:, k * LANES : (k + 1) * LANES]
    payload[...] = chunks[...].reshape(payload.shape).astype(bf16)


def unpack(payload, wide, chunks):
    chunks[...] = payload[...].astype(f32).reshape(chunks.shape)
    pixels = wide.shape[0]
    for k in range(wide.shape[1] // LANES):
        wide[:, k * LANES : (k + 1) * LANES] = chunks[pl.ds(k, pixels, stride=PAYLOAD), :]


def activation(normed, gain):
    gated = normed * gain
    sig = jax.nn.sigmoid(gated)
    return gated * sig, sig * (1.0 + gated * (1.0 - sig))


def pool_out(
    temporal, stats, cells, gain, grad_heads, cot_in, payload, pooled, wide, chunks, *, cell_count
):
    frames, rows, columns, channels = cells.shape
    mean, inv = moments(stats, frames, cell_count, channels)
    half = columns // 2
    fine = jnp.zeros((columns, channels), f32)
    sway = jnp.zeros((columns, channels), f32)
    for f in range(frames):
        for r in range(rows):
            at = (f * rows + r) * columns
            normed = (temporal[at : at + columns] - mean[f : f + 1]) * inv[f : f + 1]
            silu, slope = activation(normed, gain[...])
            fine += cells[f, r].astype(f32) + silu
            sway += slope * normed
    select = pairs(half, 1.0 / 16.0)
    low = dot_exact(select, fine).astype(bf16)
    pooled[...] = low
    pack(
        [
            (0, low),
            (SLOT, dot_exact(select, sway)),
            (2 * SLOT, cot_in[...]),
            (3 * SLOT, grad_heads[...]),
        ],
        wide,
        chunks,
        payload,
    )


def slopes(
    temporal, stats, gain, normed_out, slope_out, inv_out, head, tail, token, *, frames, cell_count
):
    channels = temporal.shape[1]
    step = temporal.shape[0] // frames
    mean, inv = moments(stats, frames, cell_count, channels)
    inv_out[...] = inv
    for f in range(frames):
        here = slice(f * step, (f + 1) * step)
        normed = (temporal[here] - mean[f : f + 1]) * inv[f : f + 1]
        normed_out[here] = normed.astype(bf16)
        slope_out[here] = slope_of(normed, gain)
    for f, edge in ((0, head), (frames - 1, tail)):
        high = inv[f : f + 1].astype(bf16).astype(f32)
        edge[:step] = normed_out[f * step : (f + 1) * step]
        edge[step:] = jnp.concatenate(
            [high, inv[f : f + 1] - high, jnp.zeros((edge.shape[0] - step - 2, channels), f32)],
            axis=0,
        ).astype(bf16)
    token[...] = jnp.zeros_like(token)


def slope_of(normed, gain):
    return (activation(normed, gain[...])[1] * gain[...] * (1.0 / 16.0)).astype(bf16)


def slopes_beside(before, after, gain, slope_out, inv_out):
    step = slope_out.shape[1]
    for at, edge in enumerate((before, after)):
        extra = edge[step:].astype(f32)
        inv_out[at : at + 1] = extra[0:1] + extra[1:2]
        slope_out[at] = slope_of(edge[:step].astype(f32), gain)


def coarse(payload, merged, bias, out, wide, out_wide, chunks, bias_here, sems, *, heads, channels):
    bias_copy = (bias, bias_here, sems.at[0])
    start(bias_copy)
    unpack(payload, wide, chunks)
    frames = payload.shape[0]
    pooled = wide[:, :channels].astype(bf16)
    sway = wide[:, SLOT : SLOT + channels]
    cot_in = wide[:, 2 * SLOT : 2 * SLOT + channels]
    width = merged.shape[1] // 3
    grad_heads = wide[:, 3 * SLOT : 3 * SLOT + width].astype(bf16)
    depth = width // heads
    factor = 1.0 / math.sqrt(depth)
    qkv = dot(pooled, merged[...]).astype(bf16)
    queries, keys, values = (qkv[:, i * width : (i + 1) * width] for i in range(3))
    row = lax.broadcasted_iota(jnp.int32, (heads, frames, width), 0)
    lane = lax.broadcasted_iota(jnp.int32, (heads, frames, width), 2)
    own = (lane >= row * depth) & (lane < (row + 1) * depth)

    def by_head(matrix):
        tiled = jnp.broadcast_to(matrix.astype(f32)[None], (heads, frames, width))
        return jnp.where(own, tiled, 0.0).astype(bf16).reshape(heads * frames, width)

    def gather(product):
        return jnp.sum(jnp.where(own, product.reshape(heads, frames, width), 0.0), axis=0)

    query_rows = by_head(queries)
    grad_rows = by_head(grad_heads)
    wait(bias_copy)
    scores = dot_nt(query_rows, keys) * factor + bias_here[...].reshape(heads * frames, frames)
    expd = jnp.exp(scores - jnp.max(scores, axis=1, keepdims=True))
    weights = expd / jnp.sum(expd, axis=1, keepdims=True)
    rounded = weights.astype(bf16)
    blended = gather(dot(rounded, values))
    grad_weights = dot_nt(grad_rows, values)
    grad_values = dot_tn(rounded, grad_rows)
    centre = jnp.sum(weights * grad_weights, axis=1, keepdims=True)
    grad_scores = (weights * (grad_weights - centre)).astype(bf16)
    grad_queries = gather(dot(grad_scores, keys)) * factor
    grad_keys = dot_tn(grad_scores, query_rows) * factor
    grads = jnp.concatenate([grad_queries, grad_keys, grad_values], axis=1).astype(bf16)
    grad_pooled = (cot_in + dot_nt(grads, merged[...])).astype(bf16)
    low = grad_pooled.astype(f32)
    gain = jnp.sum(low * sway, axis=0, keepdims=True)
    outside = jnp.zeros((1, channels), f32)
    pack(
        [
            (0, jnp.concatenate([outside, low[:-1]], axis=0)),
            (channels, low),
            (2 * channels, jnp.concatenate([low[1:], outside], axis=0)),
            (3 * channels, jnp.broadcast_to(gain, (frames, channels))),
            (4 * channels, blended),
        ],
        out_wide,
        chunks,
        out,
    )


def totals(
    payload,
    normed,
    slope,
    before,
    after,
    beside_slope,
    stats,
    grad_pooled,
    blended,
    wide,
    chunks,
    *,
    frames,
):
    unpack(payload, wide, chunks)
    channels = normed.shape[1]
    step = normed.shape[0] // frames
    for i in range(3):
        grad_pooled[i] = wide[:, i * channels : (i + 1) * channels].astype(bf16)
    blended[...] = wide[:, 4 * channels : 4 * channels + blended.shape[1]].astype(bf16)
    gain = jnp.sum(wide[:, 3 * channels : 4 * channels], axis=0, keepdims=True)
    grown = [unpooled(grad_pooled[i]) for i in range(3)]
    firsts, seconds = [], []

    def add(low, cells_slope, cells_normed):
        repeated = jnp.concatenate([low] * (step // low.shape[0]), axis=0)
        first = repeated * cells_slope.astype(f32)
        firsts.append(jnp.sum(first, axis=0, keepdims=True))
        seconds.append(jnp.sum(first * cells_normed.astype(f32), axis=0, keepdims=True))

    add(grown[0], beside_slope[0], before[:step])
    for f in range(frames):
        here = slice(f * step, (f + 1) * step)
        add(grown[1], slope[here], normed[here])
    add(grown[2], beside_slope[1], after[:step])
    gain = jnp.concatenate([gain, jnp.zeros((1, SLOT - channels), f32)], axis=1)
    count = 2 * (frames + 2)
    block = jnp.concatenate(
        [
            dot_exact(jnp.concatenate(firsts + seconds, axis=0), members(channels)),
            *[gain[:, k * LANES : (k + 1) * LANES] for k in range(SLOT // LANES)],
            jnp.zeros((stats.shape[1] - count - SLOT // LANES, LANES), f32),
        ],
        axis=0,
    )
    stats[...] = jnp.broadcast_to(block[None], stats.shape)


def unpooled(grad_pooled):
    half = grad_pooled.shape[0]
    row = lax.broadcasted_iota(jnp.int32, (2 * half, half), 0)
    col = lax.broadcasted_iota(jnp.int32, (2 * half, half), 1)
    grow = jnp.where((row == 2 * col) | (row == 2 * col + 1), 1.0, 0.0).astype(bf16)
    return dot(grow, grad_pooled)


def norm_back(
    stats,
    grad_pooled,
    normed,
    slope,
    inv,
    before,
    after,
    beside_slope,
    beside_inv,
    weight,
    grad,
    top,
    bottom,
    gain,
    cells,
    time,
    sems,
    *,
    cell_count,
):
    copy = (weight, time, sems.at[0])
    start(copy)
    frames, rows, columns, channels = grad.shape
    step = rows * columns
    count = frames + 2
    total = jnp.sum(stats[...], axis=0)
    for k in range(gain.shape[1] // LANES):
        gain[:, k * LANES : (k + 1) * LANES] = total[2 * count + k : 2 * count + k + 1]
    means = spread(total[: 2 * count] / cell_count, channels)
    at = lax.axis_index("frame")
    last = lax.axis_size("frame") - 1

    def back(f, low, cells_normed, cells_slope, scale):
        grown = unpooled(low)
        grown = jnp.concatenate([grown] * rows, axis=0)
        return scale * (
            grown * cells_slope.astype(f32)
            - means[f : f + 1]
            - cells_normed.astype(f32) * means[count + f : count + f + 1]
        )

    early = back(0, grad_pooled[0], before[:step], beside_slope[0], beside_inv[0:1])
    cells[:step] = jnp.where(at > 0, early, 0.0).astype(bf16)
    for f in range(frames):
        here = slice(f * step, (f + 1) * step)
        value = back(f + 1, grad_pooled[1], normed[here], slope[here], inv[f : f + 1])
        cells[(f + 1) * step : (f + 2) * step] = value.astype(bf16)
    late = back(
        count - 1, grad_pooled[2], after[:step], beside_slope[1], beside_inv[1:2]
    )
    cells[(count - 1) * step :] = jnp.where(at < last, late, 0.0).astype(bf16)
    size = frames * step
    wait(copy)
    sums = dot_nt(cells[:size], time[2])
    sums += dot_nt(cells[step : step + size], time[1])
    sums += dot_nt(cells[2 * step :], time[0])
    spatial = sums.astype(bf16).reshape(grad.shape)
    grad[...] = spatial
    top[...] = spatial[:, :1]
    bottom[...] = spatial[:, -1:]


def space_back_finish(part, above, below, weight, grad_pooled, out):
    grown = unpooled(grad_pooled[1]) * (1.0 / 16.0)
    for at, row in enumerate(space_edges(part, above, below, weight, True)):
        row = row.reshape(out.shape[0], *out.shape[2:]) + grown[None]
        out[:, at] = row.astype(bf16)


def project_cot(cot, proj_in, proj_out, grad_heads, cot_in, low, high, sems):
    copies = ((proj_in, low, sems.at[0]), (proj_out, high, sems.at[1]))
    start(*copies)
    wait(copies[0])
    cot_in[...] = dot_nt(cot[...], low[...])
    wait(copies[1])
    grad_heads[...] = dot_nt(cot[...], high[...]).astype(bf16)


def merge(proj_in, proj_query, proj_key, proj_value, merged, low, weights, sems):
    depth, width = proj_query.shape
    parts = weights.shape[0]
    piece = depth // parts
    first = (proj_in, low, sems.at[0, 3])
    start(first)
    copies = []
    for k in range(parts):
        here = pl.ds(k * piece, piece)
        copies.append(
            [
                (weight.at[here], weights.at[k, :, pl.ds(at * width, width)], sems.at[k, at])
                for at, weight in enumerate((proj_query, proj_key, proj_value))
            ]
        )
        start(*copies[k])
    wait(first)
    sums = None
    for k in range(parts):
        wait(*copies[k])
        product = dot(low[:, k * piece : (k + 1) * piece], weights[k])
        sums = product if sums is None else sums + product
    merged[...] = sums.astype(bf16)


def coarse_finish(pooled, proj_in, blended, proj_out, out, token, low, high, sems):
    copies = ((proj_in, low, sems.at[0]), (proj_out, high, sems.at[1]))
    start(*copies)
    wait(copies[0])
    base = dot(pooled[...], low[...]).astype(bf16).astype(f32)
    wait(copies[1])
    out[...] = (base + dot(blended[...], high[...])).astype(bf16)
    token[...] = jnp.zeros_like(token)


def neighbours(tail, head, axis):
    count = lax.axis_size(axis)
    return (
        lax.ppermute(tail, axis, [(i, (i + 1) % count) for i in range(count)]),
        lax.ppermute(head, axis, [((i + 1) % count, i) for i in range(count)]),
    )


def exchange(payload, axis):
    return lax.all_to_all(payload, axis, split_axis=0, concat_axis=0, tiled=True)


def local(
    frames_in,
    kernel_space,
    kernel_time,
    norm_gain,
    proj_in,
    proj_query,
    proj_key,
    proj_value,
    proj_out,
    frame_bias,
    cotangent,
):
    frames, rows, columns, channels = frames_in.shape
    bands = lax.axis_size("space")
    cell_count = rows * bands * columns * (channels // GROUPS)
    cells = frames * rows * columns
    half = columns // 2
    heads = frame_bias.shape[0]
    width = proj_query.shape[1]
    depth = cotangent.shape[-1]
    flat = shape((cells, channels), f32)
    low_flat = shape((cells, channels), bf16)
    edge = shape((1, rows, columns, channels), bf16)
    band = shape(frames_in.shape, bf16)
    gain = norm_gain.reshape(1, channels)
    packing = (
        pltpu.VMEM((half, 3 * SLOT + width), f32),
        pltpu.VMEM((half * PAYLOAD, LANES), f32),
    )
    payload = shape((half, PAYLOAD, LANES), bf16)
    partial = shape((rows, frames * columns, channels), f32)

    outer = shape((2, columns, channels), bf16)
    inner = shape((frames - 2, columns, channels), bf16)
    outer_top, outer_bottom, inner_top, inner_bottom = call(
        rims,
        (outer, outer, inner, inner),
        frames_in,
        scratch=(pltpu.SemaphoreType.DMA((2, 3)),),
        far=(0,),
        pin=(0, 1, 2, 3),
    )
    outer_above, outer_below = neighbours(outer_bottom, outer_top, "space")
    inner_above, inner_below = neighbours(inner_bottom, inner_top, "space")
    space_here = shape(kernel_space.shape, bf16)
    part, weight = call(
        space_first,
        (partial, space_here),
        frames_in,
        kernel_space,
        scratch=(
            pltpu.VMEM(frames_in.shape, bf16),
            pltpu.SemaphoreType.DMA((3,)),
            pltpu.SemaphoreType.DMA((1,)),
        ),
        far=(0, 1),
        pin=(0, 1),
    )
    first, last = call(
        spatial_outer, (edge, edge), part, outer_above, outer_below, weight, pin=(0, 1)
    )
    before, after = neighbours(last, first, "frame")
    part, weight = call(
        spatial_inner,
        (flat, shape(kernel_time.shape, bf16)),
        part,
        inner_above,
        inner_below,
        weight,
        first,
        last,
        kernel_time,
        scratch=(pltpu.VMEM(frames_in.shape, bf16), pltpu.SemaphoreType.DMA((1,))),
        far=(6,),
        pin=(0, 1),
    )
    temporal, stats = call(
        lambda *refs: temporal_finish(*refs, frames=frames),
        (flat, shape((bands, 2 * frames, LANES), f32)),
        part,
        before,
        after,
        weight,
        pin=(0,),
    )
    cot = cotangent.reshape(half, depth)
    token = shape((8, LANES), f32)
    low = pltpu.VMEM(proj_in.shape, bf16)
    high = pltpu.VMEM(proj_out.shape, bf16)
    grad_heads, cot_in = call(
        project_cot,
        (shape((half, width), bf16), shape((half, channels), f32)),
        cot,
        proj_in,
        proj_out,
        scratch=(low, high, pltpu.SemaphoreType.DMA((2,))),
        far=(1, 2),
        after=(stats,),
    )
    stats = exchange(stats, "space")
    sent, pooled = call(
        lambda *refs: pool_out(*refs, cell_count=cell_count),
        (payload, shape((half, channels), bf16)),
        temporal,
        stats,
        frames_in,
        gain,
        grad_heads,
        cot_in,
        scratch=packing,
    )
    received = exchange(sent, "frame")
    edge_frame = shape((rows * columns + 16, channels), bf16)
    normed, slope, inv, head, tail, slopes_token = call(
        lambda *refs: slopes(*refs, frames=frames, cell_count=cell_count),
        (low_flat, low_flat, shape((frames, channels), f32), edge_frame, edge_frame, token),
        temporal,
        stats,
        gain,
        pin=(0, 1, 2),
        after=(pooled,),
    )
    merged = call(
        merge,
        shape((channels, 3 * width), bf16),
        proj_in,
        proj_query,
        proj_key,
        proj_value,
        scratch=(
            low,
            pltpu.VMEM((5, depth // 5, 3 * width), bf16),
            pltpu.SemaphoreType.DMA((5, 4)),
        ),
        far=(0, 1, 2, 3),
        pin=(0,),
        after=(slopes_token,),
    )
    before, after = neighbours(tail, head, "frame")
    sent = call(
        lambda *refs: coarse(*refs, heads=heads, channels=channels),
        payload,
        received,
        merged,
        frame_bias,
        scratch=(
            packing[0],
            pltpu.VMEM((half, 4 * channels + width), f32),
            packing[1],
            pltpu.VMEM(frame_bias.shape, f32),
            pltpu.SemaphoreType.DMA((1,)),
        ),
        far=(2,),
    )
    beside_slope, beside_inv = call(
        slopes_beside,
        (shape((2, rows * columns, channels), bf16), shape((2, channels), f32)),
        before,
        after,
        gain,
        pin=(0, 1),
    )
    received = exchange(sent, "frame")
    stats, grad_pooled, blended = call(
        lambda *refs: totals(*refs, frames=frames),
        (
            shape((bands, 16, LANES), f32),
            shape((3, half, channels), bf16),
            shape((half, width), bf16),
        ),
        received,
        normed,
        slope,
        before,
        after,
        beside_slope,
        scratch=(pltpu.VMEM((half, 4 * channels + width), f32), packing[1]),
    )
    coarse_out, coarse_token = call(
        coarse_finish,
        (shape((half, depth), bf16), token),
        pooled,
        proj_in,
        blended,
        proj_out,
        scratch=(low, high, pltpu.SemaphoreType.DMA((2,))),
        far=(1, 3),
        after=(stats,),
    )
    stats = exchange(stats, "space")
    row_edge = shape((frames, 1, columns, channels), bf16)
    grad_spatial, top, bottom, grad_gain = call(
        lambda *refs: norm_back(*refs, cell_count=cell_count),
        (band, row_edge, row_edge, shape((1, SLOT), f32)),
        stats,
        grad_pooled,
        normed,
        slope,
        inv,
        before,
        after,
        beside_slope,
        beside_inv,
        kernel_time,
        scratch=(
            pltpu.VMEM(((frames + 2) * rows * columns, channels), bf16),
            pltpu.VMEM(kernel_time.shape, bf16),
            pltpu.SemaphoreType.DMA((1,)),
        ),
        far=(9,),
        after=(coarse_token,),
    )
    above, below = neighbours(bottom, top, "space")
    part, weight = call(
        lambda *refs: space_own(*refs, back=True),
        (partial, space_here),
        grad_spatial,
        kernel_space,
        scratch=(pltpu.SemaphoreType.DMA((3,)),),
        far=(1,),
        pin=(0, 1),
    )
    grad_frames = call(space_back_finish, band, part, above, below, weight, grad_pooled)
    return coarse_out.reshape(cotangent.shape), grad_frames, grad_gain[0, :channels]


def solution(mesh):
    in_specs = (
        P("frame", "space", None, None),
        P(),
        P(),
        P(),
        P(),
        P(),
        P(),
        P(),
        P(),
        P(),
        P("frame", "space", None, None),
    )
    out_specs = (P("frame", "space", None, None), P("frame", "space", None, None), P())
    return jax.shard_map(local, mesh=mesh, in_specs=in_specs, out_specs=out_specs, check_vma=False)
```

```python
import math

import jax
import jax.numpy as jnp
from jax import lax
from jax.experimental import pallas as pl
from jax.experimental.pallas import tpu as pltpu
from jax.sharding import PartitionSpec as P

GROUPS = 32
LANES = 128
SLOT = 384
PAYLOAD = 16
bf16 = jnp.bfloat16
f32 = jnp.float32


def dot(a, b):
    return jnp.dot(a, b, preferred_element_type=f32)


def dot_nt(a, b):
    return lax.dot_general(a, b, (((1,), (1,)), ((), ())), preferred_element_type=f32)


def dot_tn(a, b):
    return lax.dot_general(a, b, (((0,), (0,)), ((), ())), preferred_element_type=f32)


def thirds(a):
    high = a.astype(bf16)
    rest = a - high.astype(f32)
    mid = rest.astype(bf16)
    return high, mid, (rest - mid.astype(f32)).astype(bf16)


def dot_sums(a, chosen):
    rows = a.shape[0]
    pad = -rows % 16
    if pad:
        a = jnp.concatenate([a, jnp.zeros((pad, a.shape[1]), f32)], axis=0)
    out = dot(jnp.concatenate(thirds(a), axis=0), chosen)
    step = rows + pad
    return (out[:step] + out[step : 2 * step] + out[2 * step :])[:rows]


def dot_chosen(chosen, b):
    return dot(jnp.concatenate([chosen] * 3, axis=1), jnp.concatenate(thirds(b), axis=0))


def call(kernel, out_shape, *operands, scratch=(), limit=12, far=(), far_out=(), pin=(), alias=None, after=()):
    count = len(operands)
    near = pl.BlockSpec(memory_space=pltpu.VMEM)
    away = pl.BlockSpec(memory_space=pltpu.HBM)
    single = not isinstance(out_shape, tuple)
    shapes = (out_shape,) if single else out_shape
    out_specs = tuple(away if i in far_out else near for i in range(len(shapes)))
    places = {**{i: pltpu.HBM for i in far_out}, **{i: pltpu.VMEM for i in pin}}
    shapes = tuple(
        places[i](each.shape, each.dtype) if i in places else each for i, each in enumerate(shapes)
    )
    operands = [
        pltpu.with_memory_space_constraint(each, pltpu.HBM) if i in far else each
        for i, each in enumerate(operands)
    ]

    def body(*refs):
        kernel(*refs[:count], *refs[count + len(after) :])

    return pl.pallas_call(
        body,
        out_shape=shapes[0] if single else shapes,
        in_specs=[away if i in far else near for i in range(count)] + [near] * len(after),
        out_specs=out_specs[0] if single else out_specs,
        scratch_shapes=list(scratch),
        input_output_aliases=alias or {},
        compiler_params=pltpu.CompilerParams(vmem_limit_bytes=limit * 1024 * 1024),
    )(*operands, *after)


def start(*copies):
    for source, target, semaphore in copies:
        pltpu.make_async_copy(source, target, semaphore).start()


def wait(*copies):
    for source, target, semaphore in copies:
        pltpu.make_async_copy(source, target, semaphore).wait()


def shape(dims, dtype):
    return jax.ShapeDtypeStruct(dims, dtype)


def taps(cells):
    wide = cells.astype(f32)
    columns = cells.shape[1]
    col = lax.broadcasted_iota(jnp.int32, cells.shape, 1)
    left = jnp.where(col == 0, 0.0, pltpu.roll(wide, 1, 1)).astype(bf16)
    right = jnp.where(col == columns - 1, 0.0, pltpu.roll(wide, columns - 1, 1)).astype(bf16)
    return [each.reshape(-1, cells.shape[2]) for each in (left, cells, right)]


def row_sum(cells, weight, i, back):
    if back:
        return sum(dot_nt(cells[j], weight[2 - i, 2 - j]) for j in range(3))
    channels = cells[0].shape[1]
    merged = jnp.concatenate(cells, axis=1)
    return dot(merged, weight[i].reshape(3 * channels, channels))


def rims(cells, outer_top, outer_bottom, inner_top, inner_bottom, sems):
    last = cells.shape[0] - 1
    copies = []
    for row, (outer, inner) in ((0, (outer_top, inner_top)), (1, (outer_bottom, inner_bottom))):
        copies += [
            (cells.at[0, row], outer.at[0], sems.at[row, 0]),
            (cells.at[last, row], outer.at[1], sems.at[row, 1]),
            (cells.at[pl.ds(1, last - 1), row], inner, sems.at[row, 2]),
        ]
    start(*copies)
    wait(*copies)


def space_first(cells_far, weight_far, part, weight, cells, sems, cells_sem):
    copy = (cells_far, cells, cells_sem.at[0])
    start(copy)
    space_own(cells, weight_far, part, weight, sems, back=False, copy=copy)


def space_own(cells, weight_far, part, weight, sems, *, back, copy=None):
    copies = [(weight_far.at[i], weight.at[i], sems.at[i]) for i in range(3)]
    start(*copies)
    if copy:
        wait(copy)
    first = taps(cells[:, 0])
    second = taps(cells[:, 1])
    wait(*copies)
    part[0] = row_sum(first, weight, 1, back) + row_sum(second, weight, 2, back)
    part[1] = row_sum(second, weight, 1, back) + row_sum(first, weight, 0, back)


def inside(above, below):
    at = lax.axis_index("space")
    last = lax.axis_size("space") - 1
    return (
        jnp.where(at > 0, above, jnp.zeros_like(above)),
        jnp.where(at < last, below, jnp.zeros_like(below)),
    )


def spatial_outer(part, above, below, weight, first, last):
    columns = above.shape[1]
    for r, (i, rim) in enumerate(zip((0, 2), inside(above[...], below[...]))):
        own = jnp.concatenate([part[r, :columns], part[r, -columns:]], axis=0)
        row = (own + row_sum(taps(rim), weight, i, False)).astype(bf16)
        first[0, r] = row[:columns]
        last[0, r] = row[columns:]


def spatial_inner(part, above, below, weight, first, last, time_far, sums, time, moments_out, cells, sems):
    copy = (time_far, time, sems.at[0])
    start(copy)
    columns = above.shape[1]
    frames, rows = cells.shape[:2]
    for r, (i, rim) in enumerate(zip((0, 2), inside(above[...], below[...]))):
        row = part[r, columns:-columns] + row_sum(taps(rim), weight, i, False)
        cells[1 : frames - 1, r] = row.astype(bf16).reshape(frames - 2, *cells.shape[2:])
    cells[0] = first[0]
    cells[frames - 1] = last[0]
    wait(copy)
    time_own(cells, time, sums)
    step = sums.shape[0] // frames
    for f in range(1, frames - 1):
        frame_sums(sums[f * step : (f + 1) * step], f, moments_out)


def frame_sums(cells, f, out):
    frames = out.shape[0] // 2
    out[f : f + 1] = jnp.sum(cells, axis=0, keepdims=True)
    out[frames + f : frames + f + 1] = jnp.sum(cells * cells, axis=0, keepdims=True)


def time_own(cells, weight, part):
    frames, _, _, channels = cells.shape
    flat = cells[...].reshape(-1, channels)
    step = flat.shape[0] // frames
    part[...] = dot(flat, weight[1])
    part[step:] += dot(flat[:-step], weight[0])
    part[:-step] += dot(flat[step:], weight[2])


def members(channels):
    channel = lax.broadcasted_iota(jnp.int32, (channels, LANES), 0)
    group = lax.broadcasted_iota(jnp.int32, (channels, LANES), 1)
    return belong(channel, group, channels)


def belong(channel, group, channels):
    width = channels // GROUPS
    inside_group = (channel >= group * width) & (channel < (group + 1) * width)
    return jnp.where(inside_group, 1.0, 0.0).astype(bf16)


def spread(statistic, channels):
    group = lax.broadcasted_iota(jnp.int32, (LANES, channels), 0)
    channel = lax.broadcasted_iota(jnp.int32, (LANES, channels), 1)
    return dot_sums(statistic, belong(channel, group, channels))


def temporal_finish(part, before, after, weight, inner, temporal, stats, sums):
    at = lax.axis_index("frame")
    ends = lax.axis_size("frame") - 1
    channels = before.shape[-1]
    frames = inner.shape[0] // 2
    step = part.shape[0] // frames
    sums[...] = inner[...]
    for f, edge, i, there in ((0, before, 0, at > 0), (frames - 1, after, 2, at < ends)):
        here = slice(f * step, (f + 1) * step)
        halo = jnp.where(there, edge[...], jnp.zeros_like(edge[...])).reshape(-1, channels)
        cells = part[here] + dot(halo, weight[i])
        temporal[here] = cells
        frame_sums(cells, f, sums)
    stats[...] = jnp.broadcast_to(dot_sums(sums[...], members(channels))[None], stats.shape)


def moments(stats, frames, cell_count, channels):
    total = jnp.sum(stats[...], axis=0)
    mean = total[:frames] / cell_count
    inv = lax.rsqrt(total[frames:] / cell_count - mean * mean + 1e-05)
    both = spread(jnp.concatenate([mean, inv], axis=0), channels)
    return both[:frames], both[frames:]


def pairs(half):
    row = lax.broadcasted_iota(jnp.int32, (half, 2 * half), 0)
    col = lax.broadcasted_iota(jnp.int32, (half, 2 * half), 1)
    return jnp.where((col == 2 * row) | (col == 2 * row + 1), 1.0, 0.0).astype(bf16)


def pack(parts, wide, chunks, payload):
    used = 0
    for part in parts:
        wide[:, used : used + part.shape[1]] = part.astype(f32)
        used += part.shape[1]
    pixels, width = wide.shape
    if used < width:
        wide[:, used:] = jnp.zeros((pixels, width - used), f32)
    for k in range(PAYLOAD):
        here = pl.ds(k, pixels, stride=PAYLOAD)
        if k * LANES < width:
            chunks[here, :] = wide[:, k * LANES : (k + 1) * LANES]
        else:
            chunks[here, :] = jnp.zeros((pixels, LANES), f32)
    payload[...] = chunks[...].reshape(payload.shape).astype(bf16)


def unpack(payload, wide, chunks):
    chunks[...] = payload[...].astype(f32).reshape(chunks.shape)
    pixels = wide.shape[0]
    for k in range(wide.shape[1] // LANES):
        wide[:, k * LANES : (k + 1) * LANES] = chunks[pl.ds(k, pixels, stride=PAYLOAD), :]


def activation(normed, gain):
    gated = normed * gain
    sig = jax.nn.sigmoid(gated)
    return gated * sig, sig * (1.0 + gated * (1.0 - sig))


def pool_out(
    temporal, stats, cells, gain, grad_heads, cot_in, payload, pooled, wide, chunks, *, cell_count
):
    frames, rows, columns, channels = cells.shape
    mean, inv = moments(stats, frames, cell_count, channels)
    half = columns // 2
    fine = jnp.zeros((columns, channels), f32)
    sway = jnp.zeros((columns, channels), f32)
    for f in range(frames):
        for r in range(rows):
            at = (f * rows + r) * columns
            normed = (temporal[at : at + columns] - mean[f : f + 1]) * inv[f : f + 1]
            silu, slope = activation(normed, gain[...])
            fine += cells[f, r].astype(f32) + silu
            sway += slope * normed
    select = pairs(half)
    low = (dot_chosen(select, fine) * (1.0 / 16.0)).astype(bf16)
    pooled[...] = low
    sway = dot_chosen(select, sway) * (1.0 / 16.0)
    pack([low, sway, grad_heads[...], cot_in[...]], wide, chunks, payload)


def slopes(
    temporal, stats, gain, normed_out, slope_out, inv_out, head, tail, token, *, frames, cell_count
):
    channels = temporal.shape[1]
    step = temporal.shape[0] // frames
    mean, inv = moments(stats, frames, cell_count, channels)
    inv_out[...] = inv
    for f in range(frames):
        here = slice(f * step, (f + 1) * step)
        normed = (temporal[here] - mean[f : f + 1]) * inv[f : f + 1]
        normed_out[here] = normed.astype(bf16)
        slope_out[here] = slope_of(normed, gain)
    for f, edge in ((0, head), (frames - 1, tail)):
        high = inv[f : f + 1].astype(bf16).astype(f32)
        edge[:step] = normed_out[f * step : (f + 1) * step]
        edge[step:] = jnp.concatenate(
            [high, inv[f : f + 1] - high, jnp.zeros((edge.shape[0] - step - 2, channels), f32)],
            axis=0,
        ).astype(bf16)
    token[...] = jnp.zeros_like(token)


def slope_of(normed, gain):
    return (activation(normed, gain[...])[1] * gain[...] * (1.0 / 16.0)).astype(bf16)


def slopes_beside(before, after, gain, slope_out, inv_out):
    step = slope_out.shape[1]
    for at, edge in enumerate((before, after)):
        extra = edge[step:].astype(f32)
        inv_out[at : at + 1] = extra[0:1] + extra[1:2]
        slope_out[at] = slope_of(edge[:step].astype(f32), gain)


def coarse(payload, merged, bias, out, wide, out_wide, chunks, placed, *, heads, channels):
    unpack(payload, wide, chunks)
    frames = payload.shape[0]
    pooled = wide[:, :channels].astype(bf16)
    sway = wide[:, channels : 2 * channels]
    width = merged.shape[1] // 3
    grad_heads = wide[:, 2 * channels : 2 * channels + width].astype(bf16)
    cot_in = wide[:, 2 * channels + width : 3 * channels + width]
    depth = width // heads
    factor = 1.0 / math.sqrt(depth)
    qkv = dot(pooled, merged[...]).astype(bf16)
    queries, keys, values = (qkv[:, i * width : (i + 1) * width] for i in range(3))

    def by_head(matrix, place):
        place[...] = jnp.zeros_like(place)
        for h in range(heads):
            lanes = slice(h * depth, (h + 1) * depth)
            place[h * frames : (h + 1) * frames, lanes] = matrix[:, lanes]
        return place[...]

    def gather(product):
        return jnp.concatenate(
            [
                product[h * frames : (h + 1) * frames, h * depth : (h + 1) * depth]
                for h in range(heads)
            ],
            axis=1,
        )

    grad_rows = by_head(grad_heads, placed.at[1])
    query_rows = by_head(queries, placed.at[0])
    scores = dot_nt(keys, query_rows) * factor + bias[...]
    expd = jnp.exp(scores - jnp.max(scores, axis=0, keepdims=True))
    weights = expd / jnp.sum(expd, axis=0, keepdims=True)
    rounded = weights.astype(bf16)
    grad_weights = dot_nt(values, grad_rows)
    centre = jnp.sum(weights * grad_weights, axis=0, keepdims=True)
    grad_scores = (weights * (grad_weights - centre)).astype(bf16)
    blended = gather(dot_tn(rounded, values))
    grad_values = dot(rounded, grad_rows)
    grad_queries = gather(dot_tn(grad_scores, keys)) * factor
    grad_keys = dot(grad_scores, query_rows) * factor
    grads = jnp.concatenate([grad_queries, grad_keys, grad_values], axis=1).astype(bf16)
    grad_pooled = (cot_in + dot_nt(merged[...], grads).T).astype(bf16)
    low = grad_pooled.astype(f32)
    gain = jnp.sum(low * sway, axis=0, keepdims=True)
    outside = jnp.zeros((1, channels), f32)
    pack(
        [
            jnp.concatenate([outside, low[:-1]], axis=0),
            low,
            jnp.concatenate([low[1:], outside], axis=0),
            jnp.broadcast_to(gain, (frames, channels)),
            blended,
        ],
        out_wide,
        chunks,
        out,
    )


def totals(
    payload,
    normed,
    slope,
    before,
    after,
    beside_slope,
    stats,
    grad_pooled,
    blended,
    wide,
    chunks,
    *,
    frames,
):
    unpack(payload, wide, chunks)
    channels = normed.shape[1]
    step = normed.shape[0] // frames
    for i in range(3):
        grad_pooled[i] = wide[:, i * channels : (i + 1) * channels].astype(bf16)
    blended[...] = wide[:, 4 * channels : 4 * channels + blended.shape[1]].astype(bf16)
    gain = jnp.sum(wide[:, 3 * channels : 4 * channels], axis=0, keepdims=True)
    grown = [unpooled(grad_pooled[i]) for i in range(3)]
    firsts, seconds = [], []

    def add(low, cells_slope, cells_normed):
        repeated = jnp.concatenate([low] * (step // low.shape[0]), axis=0)
        first = repeated * cells_slope.astype(f32)
        firsts.append(jnp.sum(first, axis=0, keepdims=True))
        seconds.append(jnp.sum(first * cells_normed.astype(f32), axis=0, keepdims=True))

    add(grown[0], beside_slope[0], before[:step])
    for f in range(frames):
        here = slice(f * step, (f + 1) * step)
        add(grown[1], slope[here], normed[here])
    add(grown[2], beside_slope[1], after[:step])
    gain = jnp.concatenate([gain, jnp.zeros((1, SLOT - channels), f32)], axis=1)
    count = 2 * (frames + 2)
    block = jnp.concatenate(
        [
            dot_sums(jnp.concatenate(firsts + seconds, axis=0), members(channels)),
            *[gain[:, k * LANES : (k + 1) * LANES] for k in range(SLOT // LANES)],
            jnp.zeros((stats.shape[1] - count - SLOT // LANES, LANES), f32),
        ],
        axis=0,
    )
    stats[...] = jnp.broadcast_to(block[None], stats.shape)


def unpooled(grad_pooled):
    half = grad_pooled.shape[0]
    row = lax.broadcasted_iota(jnp.int32, (2 * half, half), 0)
    col = lax.broadcasted_iota(jnp.int32, (2 * half, half), 1)
    grow = jnp.where((row == 2 * col) | (row == 2 * col + 1), 1.0, 0.0).astype(bf16)
    return dot(grow, grad_pooled)


def norm_back(grown, cells_normed, cells_slope, scale, first, second):
    repeated = jnp.concatenate([grown] * (cells_slope.shape[0] // grown.shape[0]), axis=0)
    return scale * (
        repeated * cells_slope.astype(f32) - first - cells_normed.astype(f32) * second
    )


def time_back(cells, time, grad, top, bottom):
    frames, rows, columns, channels = grad.shape
    step = rows * columns
    size = frames * step
    sums = dot_nt(cells[:size], time[2])
    sums += dot_nt(cells[step : step + size], time[1])
    sums += dot_nt(cells[2 * step : 2 * step + size], time[0])
    spatial = sums.astype(bf16).reshape(grad.shape)
    grad[...] = spatial
    top[...] = spatial[:, 0]
    bottom[...] = spatial[:, -1]


def frames_back(
    stats,
    grad_pooled,
    normed,
    slope,
    inv,
    before,
    after,
    beside_slope,
    beside_inv,
    time,
    grad,
    top,
    bottom,
    gain,
    cells,
    *,
    cell_count,
):
    frames = inv.shape[0]
    channels = normed.shape[1]
    step = normed.shape[0] // frames
    count = frames + 2
    total = jnp.sum(stats[...], axis=0)
    for k in range(gain.shape[1] // LANES):
        gain[:, k * LANES : (k + 1) * LANES] = total[2 * count + k : 2 * count + k + 1]
    means = spread(total[: 2 * count] / cell_count, channels)
    at = lax.axis_index("frame")

    def coefficients(f):
        return means[f : f + 1], means[count + f : count + f + 1]

    early = norm_back(
        unpooled(grad_pooled[0]), before[:step], beside_slope[0], beside_inv[0:1], *coefficients(0)
    )
    cells[:step] = jnp.where(at > 0, early, 0.0).astype(bf16)
    grown = unpooled(grad_pooled[1])
    for f in range(frames):
        here = slice(f * step, (f + 1) * step)
        value = norm_back(grown, normed[here], slope[here], inv[f : f + 1], *coefficients(f + 1))
        cells[(f + 1) * step : (f + 2) * step] = value.astype(bf16)
    late = norm_back(
        unpooled(grad_pooled[2]),
        after[:step],
        beside_slope[1],
        beside_inv[1:2],
        *coefficients(count - 1),
    )
    there = at < lax.axis_size("frame") - 1
    cells[(count - 1) * step :] = jnp.where(there, late, 0.0).astype(bf16)
    time_back(cells, time, grad, top, bottom)


def space_back(cells, weight_far, part, weight, sems):
    space_own(cells, weight_far, part, weight, sems, back=True)


def space_back_finish(part, above, below, weight, grad_pooled, out, block, sem):
    grown = unpooled(grad_pooled[1]) * (1.0 / 16.0)
    frames, rows, columns, channels = block.shape
    copies = []
    for r, (i, rim) in enumerate(zip((0, 2), inside(above[...], below[...]))):
        row = part[r] + row_sum(taps(rim), weight, i, True)
        block[:, r] = (row.reshape(frames, columns, channels) + grown[None]).astype(bf16)
        copies.append((block.at[:, r], out.at[:, r], sem.at[r]))
        start(copies[r])
    wait(*copies)


def project_cot(cot, proj_in, proj_out, grad_heads, cot_in, low, high, sems):
    copies = ((proj_in, low, sems.at[0]), (proj_out, high, sems.at[1]))
    start(*copies)
    wait(copies[0])
    cot_in[...] = dot_nt(cot[...], low[...])
    wait(copies[1])
    grad_heads[...] = dot_nt(cot[...], high[...]).astype(bf16)


def merge(
    proj_in, proj_query, proj_key, proj_value, bias, merged, bias_out, low, weights, bias_here, sems
):
    bias_copy = (bias, bias_here, sems.at[1, 3])
    depth, width = proj_query.shape
    parts = weights.shape[0]
    piece = depth // parts
    first = (proj_in, low, sems.at[0, 3])
    start(first, bias_copy)
    copies = []
    for k in range(parts):
        here = pl.ds(k * piece, piece)
        copies.append(
            [
                (weight.at[here], weights.at[k, :, pl.ds(at * width, width)], sems.at[k, at])
                for at, weight in enumerate((proj_query, proj_key, proj_value))
            ]
        )
        start(*copies[k])
    wait(first)
    sums = None
    for k in range(parts):
        wait(*copies[k])
        product = dot(low[:, k * piece : (k + 1) * piece], weights[k])
        sums = product if sums is None else sums + product
    merged[...] = sums.astype(bf16)
    wait(bias_copy)
    bias_out[...] = bias_here[...].reshape(-1, bias_here.shape[2]).T


def coarse_finish(pooled, proj_in, blended, proj_out, time_far, out, time, low, high, sems):
    time_copy = (time_far, time, sems.at[2])
    copies = ((proj_in, low, sems.at[0]), (proj_out, high, sems.at[1]))
    start(*copies, time_copy)
    wait(copies[0])
    base = dot(pooled[...], low[...]).astype(bf16).astype(f32)
    wait(copies[1])
    out[...] = (base + dot(blended[...], high[...])).astype(bf16)
    wait(time_copy)


def neighbours(tail, head, axis):
    count = lax.axis_size(axis)
    return (
        lax.ppermute(tail, axis, [(i, (i + 1) % count) for i in range(count)]),
        lax.ppermute(head, axis, [((i + 1) % count, i) for i in range(count)]),
    )


def exchange(payload, axis):
    return lax.all_to_all(payload, axis, split_axis=0, concat_axis=0, tiled=True)


def local(
    frames_in,
    kernel_space,
    kernel_time,
    norm_gain,
    proj_in,
    proj_query,
    proj_key,
    proj_value,
    proj_out,
    frame_bias,
    cotangent,
):
    frames, rows, columns, channels = frames_in.shape
    bands = lax.axis_size("space")
    cell_count = rows * bands * columns * (channels // GROUPS)
    cells = frames * rows * columns
    half = columns // 2
    heads = frame_bias.shape[0]
    width = proj_query.shape[1]
    depth = cotangent.shape[-1]
    flat = shape((cells, channels), f32)
    low_flat = shape((cells, channels), bf16)
    edge = shape((1, rows, columns, channels), bf16)
    band = shape(frames_in.shape, bf16)
    gain = norm_gain.reshape(1, channels)
    packing = (
        pltpu.VMEM((half, -(-(3 * channels + width) // LANES) * LANES), f32),
        pltpu.VMEM((half * PAYLOAD, LANES), f32),
    )
    payload = shape((half, PAYLOAD, LANES), bf16)
    partial = shape((rows, frames * columns, channels), f32)

    outer = shape((2, columns, channels), bf16)
    inner = shape((frames - 2, columns, channels), bf16)
    outer_top, outer_bottom, inner_top, inner_bottom = call(
        rims,
        (outer, outer, inner, inner),
        frames_in,
        scratch=(pltpu.SemaphoreType.DMA((2, 3)),),
        far=(0,),
        pin=(0, 1, 2, 3),
    )
    outer_above, outer_below = neighbours(outer_bottom, outer_top, "space")
    inner_above, inner_below = neighbours(inner_bottom, inner_top, "space")
    space_here = shape(kernel_space.shape, bf16)
    part, weight = call(
        space_first,
        (partial, space_here),
        frames_in,
        kernel_space,
        scratch=(
            pltpu.VMEM(frames_in.shape, bf16),
            pltpu.SemaphoreType.DMA((3,)),
            pltpu.SemaphoreType.DMA((1,)),
        ),
        far=(0, 1),
        pin=(0, 1),
    )
    first, last = call(
        spatial_outer, (edge, edge), part, outer_above, outer_below, weight, pin=(0, 1)
    )
    before, after = neighbours(last, first, "frame")
    part, weight, inner_sums = call(
        spatial_inner,
        (flat, shape(kernel_time.shape, bf16), shape((2 * frames, channels), f32)),
        part,
        inner_above,
        inner_below,
        weight,
        first,
        last,
        kernel_time,
        scratch=(pltpu.VMEM(frames_in.shape, bf16), pltpu.SemaphoreType.DMA((1,))),
        far=(6,),
        pin=(0, 1, 2),
    )
    temporal, stats = call(
        temporal_finish,
        (flat, shape((bands, 2 * frames, LANES), f32)),
        part,
        before,
        after,
        weight,
        inner_sums,
        scratch=(pltpu.VMEM((2 * frames, channels), f32),),
        pin=(0,),
        alias={0: 0},
    )
    cot = cotangent.reshape(half, depth)
    token = shape((8, LANES), f32)
    low = pltpu.VMEM(proj_in.shape, bf16)
    high = pltpu.VMEM(proj_out.shape, bf16)
    grad_heads, cot_in = call(
        project_cot,
        (shape((half, width), bf16), shape((half, channels), f32)),
        cot,
        proj_in,
        proj_out,
        scratch=(low, high, pltpu.SemaphoreType.DMA((2,))),
        far=(1, 2),
        after=(stats,),
    )
    stats = exchange(stats, "space")
    sent, pooled = call(
        lambda *refs: pool_out(*refs, cell_count=cell_count),
        (payload, shape((half, channels), bf16)),
        temporal,
        stats,
        frames_in,
        gain,
        grad_heads,
        cot_in,
        scratch=packing,
    )
    received = exchange(sent, "frame")
    edge_frame = shape((rows * columns + 16, channels), bf16)
    normed, slope, inv, head, tail, slopes_token = call(
        lambda *refs: slopes(*refs, frames=frames, cell_count=cell_count),
        (low_flat, low_flat, shape((frames, channels), f32), edge_frame, edge_frame, token),
        temporal,
        stats,
        gain,
        pin=(0, 1, 2),
        after=(pooled,),
    )
    merged, bias = call(
        merge,
        (shape((channels, 3 * width), bf16), shape((half, heads * half), f32)),
        proj_in,
        proj_query,
        proj_key,
        proj_value,
        frame_bias,
        scratch=(
            low,
            pltpu.VMEM((5, depth // 5, 3 * width), bf16),
            pltpu.VMEM(frame_bias.shape, f32),
            pltpu.SemaphoreType.DMA((5, 4)),
        ),
        far=(0, 1, 2, 3, 4),
        pin=(0, 1),
        after=(slopes_token,),
    )
    before, after = neighbours(tail, head, "frame")
    sent = call(
        lambda *refs: coarse(*refs, heads=heads, channels=channels),
        payload,
        received,
        merged,
        bias,
        scratch=(
            packing[0],
            pltpu.VMEM((half, 4 * channels + width), f32),
            packing[1],
            pltpu.VMEM((2, heads * half, width), bf16),
        ),
    )
    beside_slope, beside_inv = call(
        slopes_beside,
        (shape((2, rows * columns, channels), bf16), shape((2, channels), f32)),
        before,
        after,
        gain,
        pin=(0, 1),
    )
    received = exchange(sent, "frame")
    stats, grad_pooled, blended = call(
        lambda *refs: totals(*refs, frames=frames),
        (
            shape((bands, 16, LANES), f32),
            shape((3, half, channels), bf16),
            shape((half, width), bf16),
        ),
        received,
        normed,
        slope,
        before,
        after,
        beside_slope,
        scratch=(pltpu.VMEM((half, 4 * channels + width), f32), packing[1]),
    )
    coarse_out, time = call(
        coarse_finish,
        (shape((half, depth), bf16), shape(kernel_time.shape, bf16)),
        pooled,
        proj_in,
        blended,
        proj_out,
        kernel_time,
        scratch=(low, high, pltpu.SemaphoreType.DMA((3,))),
        far=(1, 3, 4),
        pin=(1,),
        after=(stats,),
    )
    stats = exchange(stats, "space")
    row_edge = shape((frames, columns, channels), bf16)
    grad_spatial, top, bottom, grad_gain = call(
        lambda *refs: frames_back(*refs, cell_count=cell_count),
        (band, row_edge, row_edge, shape((1, SLOT), f32)),
        stats,
        grad_pooled,
        normed,
        slope,
        inv,
        before,
        after,
        beside_slope,
        beside_inv,
        time,
        scratch=(pltpu.VMEM(((frames + 2) * rows * columns, channels), bf16),),
        pin=(0, 1, 2, 3),
    )
    above, below = neighbours(bottom, top, "space")
    part, weight = call(
        space_back,
        (partial, space_here),
        grad_spatial,
        kernel_space,
        scratch=(pltpu.SemaphoreType.DMA((3,)),),
        far=(1,),
        pin=(0, 1),
    )
    grad_frames = call(
        space_back_finish,
        band,
        part,
        above,
        below,
        weight,
        grad_pooled,
        scratch=(pltpu.VMEM(band.shape, bf16), pltpu.SemaphoreType.DMA((2,))),
        far_out=(0,),
    )
    return coarse_out.reshape(cotangent.shape), grad_frames, grad_gain[0, :channels]


def solution(mesh):
    in_specs = (
        P("frame", "space", None, None),
        P(),
        P(),
        P(),
        P(),
        P(),
        P(),
        P(),
        P(),
        P(),
        P("frame", "space", None, None),
    )
    out_specs = (P("frame", "space", None, None), P("frame", "space", None, None), P())
    return jax.shard_map(local, mesh=mesh, in_specs=in_specs, out_specs=out_specs, check_vma=False)
```

```python
import math

import jax
import jax.numpy as jnp
from jax import lax
from jax.experimental import pallas as pl
from jax.experimental.pallas import tpu as pltpu
from jax.sharding import PartitionSpec as P

GROUPS = 32
LANES = 128
SLOT = 384
PAYLOAD = 16
bf16 = jnp.bfloat16
f32 = jnp.float32


def dot(a, b):
    return jnp.dot(a, b, preferred_element_type=f32)


def dot_nt(a, b):
    return lax.dot_general(a, b, (((1,), (1,)), ((), ())), preferred_element_type=f32)


def dot_tn(a, b):
    return lax.dot_general(a, b, (((0,), (0,)), ((), ())), preferred_element_type=f32)


def thirds(a):
    high = a.astype(bf16)
    rest = a - high.astype(f32)
    mid = rest.astype(bf16)
    return high, mid, (rest - mid.astype(f32)).astype(bf16)


def dot_sums(a, chosen):
    rows = a.shape[0]
    pad = -rows % 16
    if pad:
        a = jnp.concatenate([a, jnp.zeros((pad, a.shape[1]), f32)], axis=0)
    out = dot(jnp.concatenate(thirds(a), axis=0), chosen)
    step = rows + pad
    return (out[:step] + out[step : 2 * step] + out[2 * step :])[:rows]


def dot_chosen(chosen, b):
    return dot(jnp.concatenate([chosen] * 3, axis=1), jnp.concatenate(thirds(b), axis=0))


def call(kernel, out_shape, *operands, scratch=(), limit=12, far=(), far_out=(), pin=(), alias=None, after=()):
    count = len(operands)
    near = pl.BlockSpec(memory_space=pltpu.VMEM)
    away = pl.BlockSpec(memory_space=pltpu.HBM)
    single = not isinstance(out_shape, tuple)
    shapes = (out_shape,) if single else out_shape
    out_specs = tuple(away if i in far_out else near for i in range(len(shapes)))
    places = {**{i: pltpu.HBM for i in far_out}, **{i: pltpu.VMEM for i in pin}}
    shapes = tuple(
        places[i](each.shape, each.dtype) if i in places else each for i, each in enumerate(shapes)
    )
    operands = [
        pltpu.with_memory_space_constraint(each, pltpu.HBM) if i in far else each
        for i, each in enumerate(operands)
    ]

    def body(*refs):
        kernel(*refs[:count], *refs[count + len(after) :])

    return pl.pallas_call(
        body,
        out_shape=shapes[0] if single else shapes,
        in_specs=[away if i in far else near for i in range(count)] + [near] * len(after),
        out_specs=out_specs[0] if single else out_specs,
        scratch_shapes=list(scratch),
        input_output_aliases=alias or {},
        compiler_params=pltpu.CompilerParams(vmem_limit_bytes=limit * 1024 * 1024),
    )(*operands, *after)


def start(*copies):
    for source, target, semaphore in copies:
        pltpu.make_async_copy(source, target, semaphore).start()


def wait(*copies):
    for source, target, semaphore in copies:
        pltpu.make_async_copy(source, target, semaphore).wait()


def shape(dims, dtype):
    return jax.ShapeDtypeStruct(dims, dtype)


def taps(cells):
    wide = cells.astype(f32)
    columns = cells.shape[1]
    col = lax.broadcasted_iota(jnp.int32, cells.shape, 1)
    left = jnp.where(col == 0, 0.0, pltpu.roll(wide, 1, 1)).astype(bf16)
    right = jnp.where(col == columns - 1, 0.0, pltpu.roll(wide, columns - 1, 1)).astype(bf16)
    return [each.reshape(-1, cells.shape[2]) for each in (left, cells, right)]


def row_sum(cells, weight, i, back):
    if back:
        return sum(dot_nt(cells[j], weight[2 - i, 2 - j]) for j in range(3))
    channels = cells[0].shape[1]
    merged = jnp.concatenate(cells, axis=1)
    return dot(merged, weight[i].reshape(3 * channels, channels))


def rims(cells, outer_top, outer_bottom, inner_top, inner_bottom, sems):
    last = cells.shape[0] - 1
    copies = []
    for row, (outer, inner) in ((0, (outer_top, inner_top)), (1, (outer_bottom, inner_bottom))):
        copies += [
            (cells.at[0, row], outer.at[0], sems.at[row, 0]),
            (cells.at[last, row], outer.at[1], sems.at[row, 1]),
            (cells.at[pl.ds(1, last - 1), row], inner, sems.at[row, 2]),
        ]
    start(*copies)
    wait(*copies)


def space_first(cells_far, weight_far, time_far, part, weight, time, cells, sems, more_sems):
    copy = (cells_far, cells, more_sems.at[0])
    time_copy = (time_far, time, more_sems.at[1])
    start(copy)
    space_own(cells, weight_far, part, weight, sems, back=False, copy=copy, last=time_copy)


def space_own(cells, weight_far, part, weight, sems, *, back, copy=None, last=None):
    copies = [(weight_far.at[i], weight.at[i], sems.at[i]) for i in range(3)]
    start(*copies)
    if last:
        start(last)
    if copy:
        wait(copy)
    first = taps(cells[:, 0])
    second = taps(cells[:, 1])
    wait(*copies)
    part[0] = row_sum(first, weight, 1, back) + row_sum(second, weight, 2, back)
    part[1] = row_sum(second, weight, 1, back) + row_sum(first, weight, 0, back)
    if last:
        wait(last)


def inside(above, below):
    at = lax.axis_index("space")
    last = lax.axis_size("space") - 1
    return (
        jnp.where(at > 0, above, jnp.zeros_like(above)),
        jnp.where(at < last, below, jnp.zeros_like(below)),
    )


def spatial_outer(part, above, below, weight, first, last):
    columns = above.shape[1]
    for r, (i, rim) in enumerate(zip((0, 2), inside(above[...], below[...]))):
        own = jnp.concatenate([part[r, :columns], part[r, -columns:]], axis=0)
        row = (own + row_sum(taps(rim), weight, i, False)).astype(bf16)
        first[0, r] = row[:columns]
        last[0, r] = row[columns:]


def spatial_inner(part, above, below, weight, first, last, time, sums, moments_out, cells):
    columns = above.shape[1]
    frames, rows = cells.shape[:2]
    for r, (i, rim) in enumerate(zip((0, 2), inside(above[...], below[...]))):
        row = part[r, columns:-columns] + row_sum(taps(rim), weight, i, False)
        cells[1 : frames - 1, r] = row.astype(bf16).reshape(frames - 2, *cells.shape[2:])
    cells[0] = first[0]
    cells[frames - 1] = last[0]
    time_own(cells, time, sums)
    step = sums.shape[0] // frames
    for f in range(1, frames - 1):
        frame_sums(sums[f * step : (f + 1) * step], f, moments_out)


def frame_sums(cells, f, out):
    frames = out.shape[0] // 2
    out[f : f + 1] = jnp.sum(cells, axis=0, keepdims=True)
    out[frames + f : frames + f + 1] = jnp.sum(cells * cells, axis=0, keepdims=True)


def time_own(cells, weight, part):
    frames, _, _, channels = cells.shape
    flat = cells[...].reshape(-1, channels)
    step = flat.shape[0] // frames
    part[...] = dot(flat, weight[1])
    part[step:] += dot(flat[:-step], weight[0])
    part[:-step] += dot(flat[step:], weight[2])


def members(channels):
    channel = lax.broadcasted_iota(jnp.int32, (channels, LANES), 0)
    group = lax.broadcasted_iota(jnp.int32, (channels, LANES), 1)
    return belong(channel, group, channels)


def belong(channel, group, channels):
    width = channels // GROUPS
    inside_group = (channel >= group * width) & (channel < (group + 1) * width)
    return jnp.where(inside_group, 1.0, 0.0).astype(bf16)


def spread(statistic, channels):
    group = lax.broadcasted_iota(jnp.int32, (LANES, channels), 0)
    channel = lax.broadcasted_iota(jnp.int32, (LANES, channels), 1)
    return dot_sums(statistic, belong(channel, group, channels))


def temporal_finish(part, before, after, weight, inner, temporal, stats, sums):
    at = lax.axis_index("frame")
    ends = lax.axis_size("frame") - 1
    channels = before.shape[-1]
    frames = inner.shape[0] // 2
    step = part.shape[0] // frames
    sums[...] = inner[...]
    for f, edge, i, there in ((0, before, 0, at > 0), (frames - 1, after, 2, at < ends)):
        here = slice(f * step, (f + 1) * step)
        halo = jnp.where(there, edge[...], jnp.zeros_like(edge[...])).reshape(-1, channels)
        cells = part[here] + dot(halo, weight[i])
        temporal[here] = cells
        frame_sums(cells, f, sums)
    stats[...] = jnp.broadcast_to(dot_sums(sums[...], members(channels))[None], stats.shape)


def moments(stats, frames, cell_count, channels):
    total = jnp.sum(stats[...], axis=0)
    mean = total[:frames] / cell_count
    inv = lax.rsqrt(total[frames:] / cell_count - mean * mean + 1e-05)
    both = spread(jnp.concatenate([mean, inv], axis=0), channels)
    return both[:frames], both[frames:]


def pairs(half):
    row = lax.broadcasted_iota(jnp.int32, (half, 2 * half), 0)
    col = lax.broadcasted_iota(jnp.int32, (half, 2 * half), 1)
    return jnp.where((col == 2 * row) | (col == 2 * row + 1), 1.0, 0.0).astype(bf16)


def pack(parts, wide, chunks, payload):
    used = 0
    for part in parts:
        wide[:, used : used + part.shape[1]] = part.astype(f32)
        used += part.shape[1]
    pixels, width = wide.shape
    if used < width:
        wide[:, used:] = jnp.zeros((pixels, width - used), f32)
    for k in range(PAYLOAD):
        here = pl.ds(k, pixels, stride=PAYLOAD)
        if k * LANES < width:
            chunks[here, :] = wide[:, k * LANES : (k + 1) * LANES]
        else:
            chunks[here, :] = jnp.zeros((pixels, LANES), f32)
    payload[...] = chunks[...].reshape(payload.shape).astype(bf16)


def unpack(payload, wide, chunks):
    chunks[...] = payload[...].astype(f32).reshape(chunks.shape)
    pixels = wide.shape[0]
    for k in range(wide.shape[1] // LANES):
        wide[:, k * LANES : (k + 1) * LANES] = chunks[pl.ds(k, pixels, stride=PAYLOAD), :]


def activation(normed, gain):
    gated = normed * gain
    sig = jax.nn.sigmoid(gated)
    return gated * sig, sig * (1.0 + gated * (1.0 - sig))


def pool_out(
    temporal, stats, cells, gain, grad_heads, cot_in, payload, pooled, wide, chunks, *, cell_count
):
    frames, rows, columns, channels = cells.shape
    mean, inv = moments(stats, frames, cell_count, channels)
    half = columns // 2
    fine = jnp.zeros((columns, channels), f32)
    sway = jnp.zeros((columns, channels), f32)
    for f in range(frames):
        for r in range(rows):
            at = (f * rows + r) * columns
            normed = (temporal[at : at + columns] - mean[f : f + 1]) * inv[f : f + 1]
            silu, slope = activation(normed, gain[...])
            fine += cells[f, r].astype(f32) + silu
            sway += slope * normed
    select = pairs(half)
    low = (dot_chosen(select, fine) * (1.0 / 16.0)).astype(bf16)
    pooled[...] = low
    sway = dot_chosen(select, sway) * (1.0 / 16.0)
    pack([low, sway, grad_heads[...], cot_in[...]], wide, chunks, payload)


def slopes(
    temporal, stats, gain, normed_out, slope_out, inv_out, head, tail, token, *, frames, cell_count
):
    channels = temporal.shape[1]
    step = temporal.shape[0] // frames
    mean, inv = moments(stats, frames, cell_count, channels)
    inv_out[...] = inv
    for f in range(frames):
        here = slice(f * step, (f + 1) * step)
        normed = (temporal[here] - mean[f : f + 1]) * inv[f : f + 1]
        normed_out[here] = normed.astype(bf16)
        slope_out[here] = slope_of(normed, gain)
    for f, edge in ((0, head), (frames - 1, tail)):
        high = inv[f : f + 1].astype(bf16).astype(f32)
        edge[:step] = normed_out[f * step : (f + 1) * step]
        edge[step:] = jnp.concatenate(
            [high, inv[f : f + 1] - high, jnp.zeros((edge.shape[0] - step - 2, channels), f32)],
            axis=0,
        ).astype(bf16)
    token[...] = jnp.zeros_like(token)


def slope_of(normed, gain):
    return (activation(normed, gain[...])[1] * gain[...] * (1.0 / 16.0)).astype(bf16)


def slopes_beside(before, after, gain, slope_out, inv_out):
    step = slope_out.shape[1]
    for at, edge in enumerate((before, after)):
        extra = edge[step:].astype(f32)
        inv_out[at : at + 1] = extra[0:1] + extra[1:2]
        slope_out[at] = slope_of(edge[:step].astype(f32), gain)


def coarse(payload, merged, bias, out, wide, out_wide, chunks, placed, *, heads, channels):
    unpack(payload, wide, chunks)
    frames = payload.shape[0]
    pooled = wide[:, :channels].astype(bf16)
    sway = wide[:, channels : 2 * channels]
    width = merged.shape[1] // 3
    grad_heads = wide[:, 2 * channels : 2 * channels + width].astype(bf16)
    cot_in = wide[:, 2 * channels + width : 3 * channels + width]
    depth = width // heads
    factor = 1.0 / math.sqrt(depth)
    qkv = dot(pooled, merged[...]).astype(bf16)
    queries, keys, values = (qkv[:, i * width : (i + 1) * width] for i in range(3))

    def by_head(matrix, place):
        place[...] = jnp.zeros_like(place)
        for h in range(heads):
            lanes = slice(h * depth, (h + 1) * depth)
            place[h * frames : (h + 1) * frames, lanes] = matrix[:, lanes]
        return place[...]

    def gather(product):
        return jnp.concatenate(
            [
                product[h * frames : (h + 1) * frames, h * depth : (h + 1) * depth]
                for h in range(heads)
            ],
            axis=1,
        )

    grad_rows = by_head(grad_heads, placed.at[1])
    query_rows = by_head(queries, placed.at[0])
    scores = dot_nt(keys, query_rows) * factor + bias[...]
    expd = jnp.exp(scores - jnp.max(scores, axis=0, keepdims=True))
    weights = expd / jnp.sum(expd, axis=0, keepdims=True)
    rounded = weights.astype(bf16)
    grad_weights = dot_nt(values, grad_rows)
    centre = jnp.sum(weights * grad_weights, axis=0, keepdims=True)
    grad_scores = (weights * (grad_weights - centre)).astype(bf16)
    blended = gather(dot_tn(rounded, values))
    grad_values = dot(rounded, grad_rows)
    grad_queries = gather(dot_tn(grad_scores, keys)) * factor
    grad_keys = dot(grad_scores, query_rows) * factor
    grads = jnp.concatenate([grad_queries, grad_keys, grad_values], axis=1).astype(bf16)
    grad_pooled = (cot_in + dot_nt(merged[...], grads).T).astype(bf16)
    low = grad_pooled.astype(f32)
    gain = jnp.sum(low * sway, axis=0, keepdims=True)
    outside = jnp.zeros((1, channels), f32)
    pack(
        [
            jnp.concatenate([outside, low[:-1]], axis=0),
            low,
            jnp.concatenate([low[1:], outside], axis=0),
            jnp.broadcast_to(gain, (frames, channels)),
            blended,
        ],
        out_wide,
        chunks,
        out,
    )


def totals(
    payload,
    normed,
    slope,
    before,
    after,
    beside_slope,
    stats,
    grad_pooled,
    blended,
    wide,
    chunks,
    *,
    frames,
):
    unpack(payload, wide, chunks)
    channels = normed.shape[1]
    step = normed.shape[0] // frames
    for i in range(3):
        grad_pooled[i] = wide[:, i * channels : (i + 1) * channels].astype(bf16)
    blended[...] = wide[:, 4 * channels : 4 * channels + blended.shape[1]].astype(bf16)
    gain = jnp.sum(wide[:, 3 * channels : 4 * channels], axis=0, keepdims=True)
    grown = [unpooled(grad_pooled[i]) for i in range(3)]
    firsts, seconds = [], []

    def add(low, cells_slope, cells_normed):
        repeated = jnp.concatenate([low] * (step // low.shape[0]), axis=0)
        first = repeated * cells_slope.astype(f32)
        firsts.append(jnp.sum(first, axis=0, keepdims=True))
        seconds.append(jnp.sum(first * cells_normed.astype(f32), axis=0, keepdims=True))

    add(grown[0], beside_slope[0], before[:step])
    for f in range(frames):
        here = slice(f * step, (f + 1) * step)
        add(grown[1], slope[here], normed[here])
    add(grown[2], beside_slope[1], after[:step])
    gain = jnp.concatenate([gain, jnp.zeros((1, SLOT - channels), f32)], axis=1)
    count = 2 * (frames + 2)
    block = jnp.concatenate(
        [
            dot_sums(jnp.concatenate(firsts + seconds, axis=0), members(channels)),
            *[gain[:, k * LANES : (k + 1) * LANES] for k in range(SLOT // LANES)],
            jnp.zeros((stats.shape[1] - count - SLOT // LANES, LANES), f32),
        ],
        axis=0,
    )
    stats[...] = jnp.broadcast_to(block[None], stats.shape)


def unpooled(grad_pooled):
    half = grad_pooled.shape[0]
    row = lax.broadcasted_iota(jnp.int32, (2 * half, half), 0)
    col = lax.broadcasted_iota(jnp.int32, (2 * half, half), 1)
    grow = jnp.where((row == 2 * col) | (row == 2 * col + 1), 1.0, 0.0).astype(bf16)
    return dot(grow, grad_pooled)


def norm_back(grown, cells_normed, cells_slope, scale, first, second):
    repeated = jnp.concatenate([grown] * (cells_slope.shape[0] // grown.shape[0]), axis=0)
    return scale * (
        repeated * cells_slope.astype(f32) - first - cells_normed.astype(f32) * second
    )


def time_back(cells, time, grad, top, bottom):
    frames, rows, columns, channels = grad.shape
    step = rows * columns
    size = frames * step
    sums = dot_nt(cells[:size], time[2])
    sums += dot_nt(cells[step : step + size], time[1])
    sums += dot_nt(cells[2 * step : 2 * step + size], time[0])
    spatial = sums.astype(bf16).reshape(grad.shape)
    grad[...] = spatial
    top[...] = spatial[:, 0]
    bottom[...] = spatial[:, -1]


def frames_back(
    stats,
    grad_pooled,
    normed,
    slope,
    inv,
    before,
    after,
    beside_slope,
    beside_inv,
    time,
    grad,
    top,
    bottom,
    gain,
    cells,
    *,
    cell_count,
):
    frames = inv.shape[0]
    channels = normed.shape[1]
    step = normed.shape[0] // frames
    count = frames + 2
    total = jnp.sum(stats[...], axis=0)
    for k in range(gain.shape[1] // LANES):
        gain[:, k * LANES : (k + 1) * LANES] = total[2 * count + k : 2 * count + k + 1]
    means = spread(total[: 2 * count] / cell_count, channels)
    at = lax.axis_index("frame")

    def coefficients(f):
        return means[f : f + 1], means[count + f : count + f + 1]

    early = norm_back(
        unpooled(grad_pooled[0]), before[:step], beside_slope[0], beside_inv[0:1], *coefficients(0)
    )
    cells[:step] = jnp.where(at > 0, early, 0.0).astype(bf16)
    grown = unpooled(grad_pooled[1])
    for f in range(frames):
        here = slice(f * step, (f + 1) * step)
        value = norm_back(grown, normed[here], slope[here], inv[f : f + 1], *coefficients(f + 1))
        cells[(f + 1) * step : (f + 2) * step] = value.astype(bf16)
    late = norm_back(
        unpooled(grad_pooled[2]),
        after[:step],
        beside_slope[1],
        beside_inv[1:2],
        *coefficients(count - 1),
    )
    there = at < lax.axis_size("frame") - 1
    cells[(count - 1) * step :] = jnp.where(there, late, 0.0).astype(bf16)
    time_back(cells, time, grad, top, bottom)


def space_back(cells, weight_far, part, weight, sems):
    space_own(cells, weight_far, part, weight, sems, back=True)


def space_back_finish(part, above, below, weight, grad_pooled, out, block, sem):
    grown = unpooled(grad_pooled[1]) * (1.0 / 16.0)
    frames, rows, columns, channels = block.shape
    copies = []
    for r, (i, rim) in enumerate(zip((0, 2), inside(above[...], below[...]))):
        row = part[r] + row_sum(taps(rim), weight, i, True)
        block[:, r] = (row.reshape(frames, columns, channels) + grown[None]).astype(bf16)
        copies.append((block.at[:, r], out.at[:, r], sem.at[r]))
        start(copies[r])
    wait(*copies)


def project_cot(cot, proj_in, proj_out, grad_heads, cot_in, low, high, sems):
    copies = ((proj_in, low, sems.at[0]), (proj_out, high, sems.at[1]))
    start(*copies)
    wait(copies[0])
    cot_in[...] = dot_nt(cot[...], low[...])
    wait(copies[1])
    grad_heads[...] = dot_nt(cot[...], high[...]).astype(bf16)


def merge(
    proj_in, proj_query, proj_key, proj_value, bias, merged, bias_out, low, weights, bias_here, sems
):
    bias_copy = (bias, bias_here, sems.at[1, 3])
    depth, width = proj_query.shape
    parts = weights.shape[0]
    piece = depth // parts
    first = (proj_in, low, sems.at[0, 3])
    start(first, bias_copy)
    copies = []
    for k in range(parts):
        here = pl.ds(k * piece, piece)
        copies.append(
            [
                (weight.at[here], weights.at[k, :, pl.ds(at * width, width)], sems.at[k, at])
                for at, weight in enumerate((proj_query, proj_key, proj_value))
            ]
        )
        start(*copies[k])
    wait(first)
    sums = None
    for k in range(parts):
        wait(*copies[k])
        product = dot(low[:, k * piece : (k + 1) * piece], weights[k])
        sums = product if sums is None else sums + product
    merged[...] = sums.astype(bf16)
    wait(bias_copy)
    bias_out[...] = bias_here[...].reshape(-1, bias_here.shape[2]).T


def coarse_finish(pooled, proj_in, blended, proj_out, time_far, out, time, low, high, sems):
    time_copy = (time_far, time, sems.at[2])
    copies = ((proj_in, low, sems.at[0]), (proj_out, high, sems.at[1]))
    start(*copies, time_copy)
    wait(copies[0])
    base = dot(pooled[...], low[...]).astype(bf16).astype(f32)
    wait(copies[1])
    out[...] = (base + dot(blended[...], high[...])).astype(bf16)
    wait(time_copy)


def neighbours(tail, head, axis):
    count = lax.axis_size(axis)
    return (
        lax.ppermute(tail, axis, [(i, (i + 1) % count) for i in range(count)]),
        lax.ppermute(head, axis, [((i + 1) % count, i) for i in range(count)]),
    )


def exchange(payload, axis):
    return lax.all_to_all(payload, axis, split_axis=0, concat_axis=0, tiled=True)


def local(
    frames_in,
    kernel_space,
    kernel_time,
    norm_gain,
    proj_in,
    proj_query,
    proj_key,
    proj_value,
    proj_out,
    frame_bias,
    cotangent,
):
    frames, rows, columns, channels = frames_in.shape
    bands = lax.axis_size("space")
    cell_count = rows * bands * columns * (channels // GROUPS)
    cells = frames * rows * columns
    half = columns // 2
    heads = frame_bias.shape[0]
    width = proj_query.shape[1]
    depth = cotangent.shape[-1]
    flat = shape((cells, channels), f32)
    low_flat = shape((cells, channels), bf16)
    edge = shape((1, rows, columns, channels), bf16)
    band = shape(frames_in.shape, bf16)
    gain = norm_gain.reshape(1, channels)
    packing = (
        pltpu.VMEM((half, -(-(3 * channels + width) // LANES) * LANES), f32),
        pltpu.VMEM((half * PAYLOAD, LANES), f32),
    )
    payload = shape((half, PAYLOAD, LANES), bf16)
    partial = shape((rows, frames * columns, channels), f32)

    outer = shape((2, columns, channels), bf16)
    inner = shape((frames - 2, columns, channels), bf16)
    outer_top, outer_bottom, inner_top, inner_bottom = call(
        rims,
        (outer, outer, inner, inner),
        frames_in,
        scratch=(pltpu.SemaphoreType.DMA((2, 3)),),
        far=(0,),
        pin=(0, 1, 2, 3),
    )
    outer_above, outer_below = neighbours(outer_bottom, outer_top, "space")
    inner_above, inner_below = neighbours(inner_bottom, inner_top, "space")
    space_here = shape(kernel_space.shape, bf16)
    part, weight, time = call(
        space_first,
        (partial, space_here, shape(kernel_time.shape, bf16)),
        frames_in,
        kernel_space,
        kernel_time,
        scratch=(
            pltpu.VMEM(frames_in.shape, bf16),
            pltpu.SemaphoreType.DMA((3,)),
            pltpu.SemaphoreType.DMA((2,)),
        ),
        far=(0, 1, 2),
        pin=(0, 1, 2),
    )
    first, last = call(
        spatial_outer, (edge, edge), part, outer_above, outer_below, weight, pin=(0, 1)
    )
    before, after = neighbours(last, first, "frame")
    part, inner_sums = call(
        spatial_inner,
        (flat, shape((2 * frames, channels), f32)),
        part,
        inner_above,
        inner_below,
        weight,
        first,
        last,
        time,
        scratch=(pltpu.VMEM(frames_in.shape, bf16),),
        pin=(0, 1),
    )
    temporal, stats = call(
        temporal_finish,
        (flat, shape((bands, 2 * frames, LANES), f32)),
        part,
        before,
        after,
        time,
        inner_sums,
        scratch=(pltpu.VMEM((2 * frames, channels), f32),),
        pin=(0,),
        alias={0: 0},
    )
    cot = cotangent.reshape(half, depth)
    token = shape((8, LANES), f32)
    low = pltpu.VMEM(proj_in.shape, bf16)
    high = pltpu.VMEM(proj_out.shape, bf16)
    grad_heads, cot_in = call(
        project_cot,
        (shape((half, width), bf16), shape((half, channels), f32)),
        cot,
        proj_in,
        proj_out,
        scratch=(low, high, pltpu.SemaphoreType.DMA((2,))),
        far=(1, 2),
        after=(stats,),
    )
    stats = exchange(stats, "space")
    sent, pooled = call(
        lambda *refs: pool_out(*refs, cell_count=cell_count),
        (payload, shape((half, channels), bf16)),
        temporal,
        stats,
        frames_in,
        gain,
        grad_heads,
        cot_in,
        scratch=packing,
    )
    received = exchange(sent, "frame")
    edge_frame = shape((rows * columns + 16, channels), bf16)
    normed, slope, inv, head, tail, slopes_token = call(
        lambda *refs: slopes(*refs, frames=frames, cell_count=cell_count),
        (low_flat, low_flat, shape((frames, channels), f32), edge_frame, edge_frame, token),
        temporal,
        stats,
        gain,
        pin=(0, 1, 2),
        after=(pooled,),
    )
    merged, bias = call(
        merge,
        (shape((channels, 3 * width), bf16), shape((half, heads * half), f32)),
        proj_in,
        proj_query,
        proj_key,
        proj_value,
        frame_bias,
        scratch=(
            low,
            pltpu.VMEM((5, depth // 5, 3 * width), bf16),
            pltpu.VMEM(frame_bias.shape, f32),
            pltpu.SemaphoreType.DMA((5, 4)),
        ),
        far=(0, 1, 2, 3, 4),
        pin=(0, 1),
        after=(slopes_token,),
    )
    before, after = neighbours(tail, head, "frame")
    sent = call(
        lambda *refs: coarse(*refs, heads=heads, channels=channels),
        payload,
        received,
        merged,
        bias,
        scratch=(
            packing[0],
            pltpu.VMEM((half, 4 * channels + width), f32),
            packing[1],
            pltpu.VMEM((2, heads * half, width), bf16),
        ),
    )
    beside_slope, beside_inv = call(
        slopes_beside,
        (shape((2, rows * columns, channels), bf16), shape((2, channels), f32)),
        before,
        after,
        gain,
        pin=(0, 1),
    )
    received = exchange(sent, "frame")
    stats, grad_pooled, blended = call(
        lambda *refs: totals(*refs, frames=frames),
        (
            shape((bands, 16, LANES), f32),
            shape((3, half, channels), bf16),
            shape((half, width), bf16),
        ),
        received,
        normed,
        slope,
        before,
        after,
        beside_slope,
        scratch=(pltpu.VMEM((half, 4 * channels + width), f32), packing[1]),
    )
    coarse_out, time = call(
        coarse_finish,
        (shape((half, depth), bf16), shape(kernel_time.shape, bf16)),
        pooled,
        proj_in,
        blended,
        proj_out,
        kernel_time,
        scratch=(low, high, pltpu.SemaphoreType.DMA((3,))),
        far=(1, 3, 4),
        pin=(1,),
        after=(stats,),
    )
    stats = exchange(stats, "space")
    row_edge = shape((frames, columns, channels), bf16)
    grad_spatial, top, bottom, grad_gain = call(
        lambda *refs: frames_back(*refs, cell_count=cell_count),
        (band, row_edge, row_edge, shape((1, SLOT), f32)),
        stats,
        grad_pooled,
        normed,
        slope,
        inv,
        before,
        after,
        beside_slope,
        beside_inv,
        time,
        scratch=(pltpu.VMEM(((frames + 2) * rows * columns, channels), bf16),),
        pin=(0, 1, 2, 3),
    )
    above, below = neighbours(bottom, top, "space")
    part, weight = call(
        space_back,
        (partial, space_here),
        grad_spatial,
        kernel_space,
        scratch=(pltpu.SemaphoreType.DMA((3,)),),
        far=(1,),
        pin=(0, 1),
    )
    grad_frames = call(
        space_back_finish,
        band,
        part,
        above,
        below,
        weight,
        grad_pooled,
        scratch=(pltpu.VMEM(band.shape, bf16), pltpu.SemaphoreType.DMA((2,))),
        far_out=(0,),
    )
    return coarse_out.reshape(cotangent.shape), grad_frames, grad_gain[0, :channels]


def solution(mesh):
    in_specs = (
        P("frame", "space", None, None),
        P(),
        P(),
        P(),
        P(),
        P(),
        P(),
        P(),
        P(),
        P(),
        P("frame", "space", None, None),
    )
    out_specs = (P("frame", "space", None, None), P("frame", "space", None, None), P())
    return jax.shard_map(local, mesh=mesh, in_specs=in_specs, out_specs=out_specs, check_vma=False)
```

```python
import math

import jax
import jax.numpy as jnp
from jax import lax
from jax.experimental import pallas as pl
from jax.experimental.pallas import tpu as pltpu
from jax.sharding import PartitionSpec as P

GROUPS = 32
LANES = 128
SLOT = 384
PAYLOAD = 16
bf16 = jnp.bfloat16
f32 = jnp.float32


def dot(a, b):
    return jnp.dot(a, b, preferred_element_type=f32)


def dot_nt(a, b):
    return lax.dot_general(a, b, (((1,), (1,)), ((), ())), preferred_element_type=f32)


def dot_tn(a, b):
    return lax.dot_general(a, b, (((0,), (0,)), ((), ())), preferred_element_type=f32)


def thirds(a):
    high = a.astype(bf16)
    rest = a - high.astype(f32)
    mid = rest.astype(bf16)
    return high, mid, (rest - mid.astype(f32)).astype(bf16)


def dot_sums(a, chosen):
    rows = a.shape[0]
    pad = -rows % 16
    if pad:
        a = jnp.concatenate([a, jnp.zeros((pad, a.shape[1]), f32)], axis=0)
    out = dot(jnp.concatenate(thirds(a), axis=0), chosen)
    step = rows + pad
    return (out[:step] + out[step : 2 * step] + out[2 * step :])[:rows]


def dot_chosen(chosen, b):
    return dot(jnp.concatenate([chosen] * 3, axis=1), jnp.concatenate(thirds(b), axis=0))


def call(kernel, out_shape, *operands, scratch=(), limit=12, far=(), far_out=(), pin=(), alias=None, after=()):
    count = len(operands)
    near = pl.BlockSpec(memory_space=pltpu.VMEM)
    away = pl.BlockSpec(memory_space=pltpu.HBM)
    single = not isinstance(out_shape, tuple)
    shapes = (out_shape,) if single else out_shape
    out_specs = tuple(away if i in far_out else near for i in range(len(shapes)))
    places = {**{i: pltpu.HBM for i in far_out}, **{i: pltpu.VMEM for i in pin}}
    shapes = tuple(
        places[i](each.shape, each.dtype) if i in places else each for i, each in enumerate(shapes)
    )
    operands = [
        pltpu.with_memory_space_constraint(each, pltpu.HBM) if i in far else each
        for i, each in enumerate(operands)
    ]

    def body(*refs):
        kernel(*refs[:count], *refs[count + len(after) :])

    return pl.pallas_call(
        body,
        out_shape=shapes[0] if single else shapes,
        in_specs=[away if i in far else near for i in range(count)] + [near] * len(after),
        out_specs=out_specs[0] if single else out_specs,
        scratch_shapes=list(scratch),
        input_output_aliases=alias or {},
        compiler_params=pltpu.CompilerParams(vmem_limit_bytes=limit * 1024 * 1024),
    )(*operands, *after)


def start(*copies):
    for source, target, semaphore in copies:
        pltpu.make_async_copy(source, target, semaphore).start()


def wait(*copies):
    for source, target, semaphore in copies:
        pltpu.make_async_copy(source, target, semaphore).wait()


def shape(dims, dtype):
    return jax.ShapeDtypeStruct(dims, dtype)


def taps(cells):
    wide = cells.astype(f32)
    columns = cells.shape[1]
    col = lax.broadcasted_iota(jnp.int32, cells.shape, 1)
    left = jnp.where(col == 0, 0.0, pltpu.roll(wide, 1, 1)).astype(bf16)
    right = jnp.where(col == columns - 1, 0.0, pltpu.roll(wide, columns - 1, 1)).astype(bf16)
    return [each.reshape(-1, cells.shape[2]) for each in (left, cells, right)]


def row_sum(cells, weight, i, back):
    if back:
        return sum(dot_nt(cells[j], weight[2 - i, 2 - j]) for j in range(3))
    channels = cells[0].shape[1]
    merged = jnp.concatenate(cells, axis=1)
    return dot(merged, weight[i].reshape(3 * channels, channels))


def rims(cells, outer_top, outer_bottom, inner_top, inner_bottom, sems):
    last = cells.shape[0] - 1
    copies = []
    for row, (outer, inner) in ((0, (outer_top, inner_top)), (1, (outer_bottom, inner_bottom))):
        copies += [
            (cells.at[0, row], outer.at[0], sems.at[row, 0]),
            (cells.at[last, row], outer.at[1], sems.at[row, 1]),
            (cells.at[pl.ds(1, last - 1), row], inner, sems.at[row, 2]),
        ]
    start(*copies)
    wait(*copies)


def space_first(cells_far, weight_far, part, weight, cells, sems, cells_sem):
    copy = (cells_far, cells, cells_sem.at[0])
    start(copy)
    space_own(cells, weight_far, part, weight, sems, back=False, copy=copy)


def space_own(cells, weight_far, part, weight, sems, *, back, copy=None):
    copies = [(weight_far.at[i], weight.at[i], sems.at[i]) for i in range(3)]
    start(*copies)
    if copy:
        wait(copy)
    first = taps(cells[:, 0])
    second = taps(cells[:, 1])
    wait(*copies)
    part[0] = row_sum(first, weight, 1, back) + row_sum(second, weight, 2, back)
    part[1] = row_sum(second, weight, 1, back) + row_sum(first, weight, 0, back)


def inside(above, below):
    at = lax.axis_index("space")
    last = lax.axis_size("space") - 1
    return (
        jnp.where(at > 0, above, jnp.zeros_like(above)),
        jnp.where(at < last, below, jnp.zeros_like(below)),
    )


def spatial_outer(part, above, below, weight, first, last):
    columns = above.shape[1]
    for r, (i, rim) in enumerate(zip((0, 2), inside(above[...], below[...]))):
        own = jnp.concatenate([part[r, :columns], part[r, -columns:]], axis=0)
        row = (own + row_sum(taps(rim), weight, i, False)).astype(bf16)
        first[0, r] = row[:columns]
        last[0, r] = row[columns:]


def spatial_inner(part, above, below, weight, first, last, time_far, sums, time, moments_out, cells, sems):
    copy = (time_far, time, sems.at[0])
    start(copy)
    columns = above.shape[1]
    frames, rows = cells.shape[:2]
    for r, (i, rim) in enumerate(zip((0, 2), inside(above[...], below[...]))):
        row = part[r, columns:-columns] + row_sum(taps(rim), weight, i, False)
        cells[1 : frames - 1, r] = row.astype(bf16).reshape(frames - 2, *cells.shape[2:])
    cells[0] = first[0]
    cells[frames - 1] = last[0]
    wait(copy)
    time_own(cells, time, sums)
    step = sums.shape[0] // frames
    for f in range(1, frames - 1):
        frame_sums(sums[f * step : (f + 1) * step], f, moments_out)


def frame_sums(cells, f, out):
    frames = out.shape[0] // 2
    out[f : f + 1] = jnp.sum(cells, axis=0, keepdims=True)
    out[frames + f : frames + f + 1] = jnp.sum(cells * cells, axis=0, keepdims=True)


def time_own(cells, weight, part):
    frames, _, _, channels = cells.shape
    flat = cells[...].reshape(-1, channels)
    step = flat.shape[0] // frames
    part[...] = dot(flat, weight[1])
    part[step:] += dot(flat[:-step], weight[0])
    part[:-step] += dot(flat[step:], weight[2])


def members(channels):
    channel = lax.broadcasted_iota(jnp.int32, (channels, LANES), 0)
    group = lax.broadcasted_iota(jnp.int32, (channels, LANES), 1)
    return belong(channel, group, channels)


def belong(channel, group, channels):
    width = channels // GROUPS
    inside_group = (channel >= group * width) & (channel < (group + 1) * width)
    return jnp.where(inside_group, 1.0, 0.0).astype(bf16)


def spread(statistic, channels):
    group = lax.broadcasted_iota(jnp.int32, (statistic.shape[1], channels), 0)
    channel = lax.broadcasted_iota(jnp.int32, (statistic.shape[1], channels), 1)
    return dot_sums(statistic, belong(channel, group, channels))


def temporal_finish(part, before, after, weight, inner, temporal, stats, sums):
    at = lax.axis_index("frame")
    ends = lax.axis_size("frame") - 1
    channels = before.shape[-1]
    frames = inner.shape[0] // 2
    step = part.shape[0] // frames
    sums[...] = inner[...]
    for f, edge, i, there in ((0, before, 0, at > 0), (frames - 1, after, 2, at < ends)):
        here = slice(f * step, (f + 1) * step)
        halo = jnp.where(there, edge[...], jnp.zeros_like(edge[...])).reshape(-1, channels)
        cells = part[here] + dot(halo, weight[i])
        temporal[here] = cells
        frame_sums(cells, f, sums)
    stats[...] = jnp.broadcast_to(dot_sums(sums[...], members(channels))[None], stats.shape)


def moments(stats, frames, cell_count, channels):
    total = jnp.sum(stats[...], axis=0)
    mean = total[:frames] / cell_count
    inv = lax.rsqrt(total[frames:] / cell_count - mean * mean + 1e-05)
    both = spread(jnp.concatenate([mean, inv], axis=0), channels)
    return both[:frames], both[frames:]


def pairs(half):
    row = lax.broadcasted_iota(jnp.int32, (half, 2 * half), 0)
    col = lax.broadcasted_iota(jnp.int32, (half, 2 * half), 1)
    return jnp.where((col == 2 * row) | (col == 2 * row + 1), 1.0, 0.0).astype(bf16)


def pack(parts, wide, chunks, payload):
    used = 0
    for part in parts:
        wide[:, used : used + part.shape[1]] = part.astype(f32)
        used += part.shape[1]
    pixels, width = wide.shape
    if used < width:
        wide[:, used:] = jnp.zeros((pixels, width - used), f32)
    for k in range(PAYLOAD):
        here = pl.ds(k, pixels, stride=PAYLOAD)
        if k * LANES < width:
            chunks[here, :] = wide[:, k * LANES : (k + 1) * LANES]
        else:
            chunks[here, :] = jnp.zeros((pixels, LANES), f32)
    payload[...] = chunks[...].reshape(payload.shape).astype(bf16)


def unpack(payload, wide, chunks):
    chunks[...] = payload[...].astype(f32).reshape(chunks.shape)
    pixels = wide.shape[0]
    for k in range(wide.shape[1] // LANES):
        wide[:, k * LANES : (k + 1) * LANES] = chunks[pl.ds(k, pixels, stride=PAYLOAD), :]


def activation(normed, gain):
    gated = normed * gain
    sig = jax.nn.sigmoid(gated)
    return gated * sig, sig * (1.0 + gated * (1.0 - sig))


def pool_out(
    temporal, stats, cells, gain, grad_heads, cot_in, payload, pooled, wide, chunks, *, cell_count
):
    frames, rows, columns, channels = cells.shape
    mean, inv = moments(stats, frames, cell_count, channels)
    half = columns // 2
    fine = jnp.zeros((columns, channels), f32)
    sway = jnp.zeros((columns, channels), f32)
    for f in range(frames):
        for r in range(rows):
            at = (f * rows + r) * columns
            normed = (temporal[at : at + columns] - mean[f : f + 1]) * inv[f : f + 1]
            silu, slope = activation(normed, gain[...])
            fine += cells[f, r].astype(f32) + silu
            sway += slope * normed
    select = pairs(half)
    low = (dot_chosen(select, fine) * (1.0 / 16.0)).astype(bf16)
    pooled[...] = low
    sway = dot_chosen(select, sway) * (1.0 / 16.0)
    pack([low, sway, grad_heads[...], cot_in[...]], wide, chunks, payload)


def slopes(
    temporal, stats, gain, normed_out, slope_out, inv_out, head, tail, token, *, frames, cell_count
):
    channels = temporal.shape[1]
    step = temporal.shape[0] // frames
    mean, inv = moments(stats, frames, cell_count, channels)
    inv_out[...] = inv
    for f in range(frames):
        here = slice(f * step, (f + 1) * step)
        normed = (temporal[here] - mean[f : f + 1]) * inv[f : f + 1]
        normed_out[here] = normed.astype(bf16)
        slope_out[here] = slope_of(normed, gain)
    for f, edge in ((0, head), (frames - 1, tail)):
        high = inv[f : f + 1].astype(bf16).astype(f32)
        edge[:step] = normed_out[f * step : (f + 1) * step]
        edge[step:] = jnp.concatenate(
            [high, inv[f : f + 1] - high, jnp.zeros((edge.shape[0] - step - 2, channels), f32)],
            axis=0,
        ).astype(bf16)
    token[...] = jnp.zeros_like(token)


def slope_of(normed, gain):
    return (activation(normed, gain[...])[1] * gain[...] * (1.0 / 16.0)).astype(bf16)


def slopes_beside(before, after, gain, slope_out, inv_out):
    step = slope_out.shape[1]
    for at, edge in enumerate((before, after)):
        extra = edge[step:].astype(f32)
        inv_out[at : at + 1] = extra[0:1] + extra[1:2]
        slope_out[at] = slope_of(edge[:step].astype(f32), gain)


def coarse(payload, merged, bias, out, wide, out_wide, chunks, placed, *, heads, channels):
    unpack(payload, wide, chunks)
    frames = payload.shape[0]
    pooled = wide[:, :channels].astype(bf16)
    sway = wide[:, channels : 2 * channels]
    width = merged.shape[1] // 3
    grad_heads = wide[:, 2 * channels : 2 * channels + width].astype(bf16)
    cot_in = wide[:, 2 * channels + width : 3 * channels + width]
    depth = width // heads
    factor = 1.0 / math.sqrt(depth)
    qkv = dot(pooled, merged[...]).astype(bf16)
    queries, keys, values = (qkv[:, i * width : (i + 1) * width] for i in range(3))

    def by_head(matrix, place):
        place[...] = jnp.zeros_like(place)
        for h in range(heads):
            lanes = slice(h * depth, (h + 1) * depth)
            place[h * frames : (h + 1) * frames, lanes] = matrix[:, lanes]
        return place[...]

    def gather(product):
        return jnp.concatenate(
            [
                product[h * frames : (h + 1) * frames, h * depth : (h + 1) * depth]
                for h in range(heads)
            ],
            axis=1,
        )

    grad_rows = by_head(grad_heads, placed.at[1])
    query_rows = by_head(queries, placed.at[0])
    scores = dot_nt(keys, query_rows) * factor + bias[...]
    expd = jnp.exp(scores - jnp.max(scores, axis=0, keepdims=True))
    weights = expd / jnp.sum(expd, axis=0, keepdims=True)
    rounded = weights.astype(bf16)
    grad_weights = dot_nt(values, grad_rows)
    centre = jnp.sum(weights * grad_weights, axis=0, keepdims=True)
    grad_scores = (weights * (grad_weights - centre)).astype(bf16)
    blended = gather(dot_tn(rounded, values))
    grad_values = dot(rounded, grad_rows)
    grad_queries = gather(dot_tn(grad_scores, keys)) * factor
    grad_keys = dot(grad_scores, query_rows) * factor
    grads = jnp.concatenate([grad_queries, grad_keys, grad_values], axis=1).astype(bf16)
    grad_pooled = (cot_in + dot_nt(merged[...], grads).T).astype(bf16)
    low = grad_pooled.astype(f32)
    gain = jnp.sum(low * sway, axis=0, keepdims=True)
    outside = jnp.zeros((1, channels), f32)
    pack(
        [
            jnp.concatenate([outside, low[:-1]], axis=0),
            low,
            jnp.concatenate([low[1:], outside], axis=0),
            jnp.broadcast_to(gain, (frames, channels)),
            blended,
        ],
        out_wide,
        chunks,
        out,
    )


def totals(
    payload,
    normed,
    slope,
    before,
    after,
    beside_slope,
    stats,
    grad_pooled,
    blended,
    wide,
    chunks,
    *,
    frames,
):
    unpack(payload, wide, chunks)
    channels = normed.shape[1]
    step = normed.shape[0] // frames
    for i in range(3):
        grad_pooled[i] = wide[:, i * channels : (i + 1) * channels].astype(bf16)
    blended[...] = wide[:, 4 * channels : 4 * channels + blended.shape[1]].astype(bf16)
    gain = jnp.sum(wide[:, 3 * channels : 4 * channels], axis=0, keepdims=True)
    grown = [unpooled(grad_pooled[i]) for i in range(3)]
    firsts, seconds = [], []

    def add(low, cells_slope, cells_normed):
        repeated = jnp.concatenate([low] * (step // low.shape[0]), axis=0)
        first = repeated * cells_slope.astype(f32)
        firsts.append(jnp.sum(first, axis=0, keepdims=True))
        seconds.append(jnp.sum(first * cells_normed.astype(f32), axis=0, keepdims=True))

    add(grown[0], beside_slope[0], before[:step])
    for f in range(frames):
        here = slice(f * step, (f + 1) * step)
        add(grown[1], slope[here], normed[here])
    add(grown[2], beside_slope[1], after[:step])
    gain = jnp.concatenate([gain, jnp.zeros((1, SLOT - channels), f32)], axis=1)
    sums = dot_sums(jnp.concatenate(firsts + seconds, axis=0), members(channels))
    beside = LANES // GROUPS
    count = sums.shape[0] // beside
    block = jnp.concatenate(
        [
            jnp.concatenate(
                [sums[q * count : (q + 1) * count, :GROUPS] for q in range(beside)], axis=1
            ),
            *[gain[:, k * LANES : (k + 1) * LANES] for k in range(SLOT // LANES)],
            jnp.zeros((stats.shape[1] - count - SLOT // LANES, LANES), f32),
        ],
        axis=0,
    )
    stats[...] = jnp.broadcast_to(block[None], stats.shape)


def unpooled(grad_pooled):
    half = grad_pooled.shape[0]
    row = lax.broadcasted_iota(jnp.int32, (2 * half, half), 0)
    col = lax.broadcasted_iota(jnp.int32, (2 * half, half), 1)
    grow = jnp.where((row == 2 * col) | (row == 2 * col + 1), 1.0, 0.0).astype(bf16)
    return dot(grow, grad_pooled)


def norm_back(grown, cells_normed, cells_slope, scale, first, second):
    repeated = jnp.concatenate([grown] * (cells_slope.shape[0] // grown.shape[0]), axis=0)
    return scale * (
        repeated * cells_slope.astype(f32) - first - cells_normed.astype(f32) * second
    )


def time_back(cells, time, grad, top, bottom):
    frames, rows, columns, channels = grad.shape
    step = rows * columns
    size = frames * step
    sums = dot_nt(cells[:size], time[2])
    sums += dot_nt(cells[step : step + size], time[1])
    sums += dot_nt(cells[2 * step : 2 * step + size], time[0])
    spatial = sums.astype(bf16).reshape(grad.shape)
    grad[...] = spatial
    top[...] = spatial[:, 0]
    bottom[...] = spatial[:, -1]


def frames_back(
    stats,
    grad_pooled,
    normed,
    slope,
    inv,
    before,
    after,
    beside_slope,
    beside_inv,
    time,
    grad,
    top,
    bottom,
    gain,
    cells,
    *,
    cell_count,
):
    frames = inv.shape[0]
    channels = normed.shape[1]
    step = normed.shape[0] // frames
    count = frames + 2
    total = jnp.sum(stats[...], axis=0)
    beside = LANES // GROUPS
    held = 2 * count // beside
    for k in range(gain.shape[1] // LANES):
        gain[:, k * LANES : (k + 1) * LANES] = total[held + k : held + k + 1]
    sums = jnp.concatenate(
        [total[:held, q * GROUPS : (q + 1) * GROUPS] for q in range(beside)], axis=0
    )
    means = spread(sums / cell_count, channels)
    at = lax.axis_index("frame")

    def coefficients(f):
        return means[f : f + 1], means[count + f : count + f + 1]

    early = norm_back(
        unpooled(grad_pooled[0]), before[:step], beside_slope[0], beside_inv[0:1], *coefficients(0)
    )
    cells[:step] = jnp.where(at > 0, early, 0.0).astype(bf16)
    grown = unpooled(grad_pooled[1])
    for f in range(frames):
        here = slice(f * step, (f + 1) * step)
        value = norm_back(grown, normed[here], slope[here], inv[f : f + 1], *coefficients(f + 1))
        cells[(f + 1) * step : (f + 2) * step] = value.astype(bf16)
    late = norm_back(
        unpooled(grad_pooled[2]),
        after[:step],
        beside_slope[1],
        beside_inv[1:2],
        *coefficients(count - 1),
    )
    there = at < lax.axis_size("frame") - 1
    cells[(count - 1) * step :] = jnp.where(there, late, 0.0).astype(bf16)
    time_back(cells, time, grad, top, bottom)


def space_back(cells, weight_far, part, weight, sems):
    space_own(cells, weight_far, part, weight, sems, back=True)


def space_back_finish(part, above, below, weight, grad_pooled, out, block, sem):
    grown = unpooled(grad_pooled[1]) * (1.0 / 16.0)
    frames, rows, columns, channels = block.shape
    copies = []
    for r, (i, rim) in enumerate(zip((0, 2), inside(above[...], below[...]))):
        row = part[r] + row_sum(taps(rim), weight, i, True)
        block[:, r] = (row.reshape(frames, columns, channels) + grown[None]).astype(bf16)
        copies.append((block.at[:, r], out.at[:, r], sem.at[r]))
        start(copies[r])
    wait(*copies)


def project_cot(cot, proj_in, proj_out, grad_heads, cot_in, low, high, sems):
    copies = ((proj_in, low, sems.at[0]), (proj_out, high, sems.at[1]))
    start(*copies)
    wait(copies[0])
    cot_in[...] = dot_nt(cot[...], low[...])
    wait(copies[1])
    grad_heads[...] = dot_nt(cot[...], high[...]).astype(bf16)


def merge(
    proj_in, proj_query, proj_key, proj_value, bias, merged, bias_out, low, weights, bias_here, sems
):
    bias_copy = (bias, bias_here, sems.at[1, 3])
    depth, width = proj_query.shape
    parts = weights.shape[0]
    piece = depth // parts
    first = (proj_in, low, sems.at[0, 3])
    start(first, bias_copy)
    copies = []
    for k in range(parts):
        here = pl.ds(k * piece, piece)
        copies.append(
            [
                (weight.at[here], weights.at[k, :, pl.ds(at * width, width)], sems.at[k, at])
                for at, weight in enumerate((proj_query, proj_key, proj_value))
            ]
        )
        start(*copies[k])
    wait(first)
    sums = None
    for k in range(parts):
        wait(*copies[k])
        product = dot(low[:, k * piece : (k + 1) * piece], weights[k])
        sums = product if sums is None else sums + product
    merged[...] = sums.astype(bf16)
    wait(bias_copy)
    bias_out[...] = bias_here[...].reshape(-1, bias_here.shape[2]).T


def coarse_finish(pooled, proj_in, blended, proj_out, time_far, out, time, low, high, sems):
    time_copy = (time_far, time, sems.at[2])
    copies = ((proj_in, low, sems.at[0]), (proj_out, high, sems.at[1]))
    start(*copies, time_copy)
    wait(copies[0])
    base = dot(pooled[...], low[...]).astype(bf16).astype(f32)
    wait(copies[1])
    out[...] = (base + dot(blended[...], high[...])).astype(bf16)
    wait(time_copy)


def neighbours(tail, head, axis):
    count = lax.axis_size(axis)
    return (
        lax.ppermute(tail, axis, [(i, (i + 1) % count) for i in range(count)]),
        lax.ppermute(head, axis, [((i + 1) % count, i) for i in range(count)]),
    )


def exchange(payload, axis):
    return lax.all_to_all(payload, axis, split_axis=0, concat_axis=0, tiled=True)


def local(
    frames_in,
    kernel_space,
    kernel_time,
    norm_gain,
    proj_in,
    proj_query,
    proj_key,
    proj_value,
    proj_out,
    frame_bias,
    cotangent,
):
    frames, rows, columns, channels = frames_in.shape
    bands = lax.axis_size("space")
    cell_count = rows * bands * columns * (channels // GROUPS)
    cells = frames * rows * columns
    half = columns // 2
    heads = frame_bias.shape[0]
    width = proj_query.shape[1]
    depth = cotangent.shape[-1]
    flat = shape((cells, channels), f32)
    low_flat = shape((cells, channels), bf16)
    edge = shape((1, rows, columns, channels), bf16)
    band = shape(frames_in.shape, bf16)
    gain = norm_gain.reshape(1, channels)
    packing = (
        pltpu.VMEM((half, -(-(3 * channels + width) // LANES) * LANES), f32),
        pltpu.VMEM((half * PAYLOAD, LANES), f32),
    )
    payload = shape((half, PAYLOAD, LANES), bf16)
    partial = shape((rows, frames * columns, channels), f32)

    outer = shape((2, columns, channels), bf16)
    inner = shape((frames - 2, columns, channels), bf16)
    outer_top, outer_bottom, inner_top, inner_bottom = call(
        rims,
        (outer, outer, inner, inner),
        frames_in,
        scratch=(pltpu.SemaphoreType.DMA((2, 3)),),
        far=(0,),
        pin=(0, 1, 2, 3),
    )
    outer_above, outer_below = neighbours(outer_bottom, outer_top, "space")
    inner_above, inner_below = neighbours(inner_bottom, inner_top, "space")
    space_here = shape(kernel_space.shape, bf16)
    part, weight = call(
        space_first,
        (partial, space_here),
        frames_in,
        kernel_space,
        scratch=(
            pltpu.VMEM(frames_in.shape, bf16),
            pltpu.SemaphoreType.DMA((3,)),
            pltpu.SemaphoreType.DMA((1,)),
        ),
        far=(0, 1),
        pin=(0, 1),
    )
    first, last = call(
        spatial_outer, (edge, edge), part, outer_above, outer_below, weight, pin=(0, 1)
    )
    before, after = neighbours(last, first, "frame")
    part, weight, inner_sums = call(
        spatial_inner,
        (flat, shape(kernel_time.shape, bf16), shape((2 * frames, channels), f32)),
        part,
        inner_above,
        inner_below,
        weight,
        first,
        last,
        kernel_time,
        scratch=(pltpu.VMEM(frames_in.shape, bf16), pltpu.SemaphoreType.DMA((1,))),
        far=(6,),
        pin=(0, 1, 2),
    )
    temporal, stats = call(
        temporal_finish,
        (flat, shape((bands, 2 * frames, LANES), f32)),
        part,
        before,
        after,
        weight,
        inner_sums,
        scratch=(pltpu.VMEM((2 * frames, channels), f32),),
        pin=(0,),
        alias={0: 0},
    )
    cot = cotangent.reshape(half, depth)
    token = shape((8, LANES), f32)
    low = pltpu.VMEM(proj_in.shape, bf16)
    high = pltpu.VMEM(proj_out.shape, bf16)
    grad_heads, cot_in = call(
        project_cot,
        (shape((half, width), bf16), shape((half, channels), f32)),
        cot,
        proj_in,
        proj_out,
        scratch=(low, high, pltpu.SemaphoreType.DMA((2,))),
        far=(1, 2),
        after=(stats,),
    )
    stats = exchange(stats, "space")
    sent, pooled = call(
        lambda *refs: pool_out(*refs, cell_count=cell_count),
        (payload, shape((half, channels), bf16)),
        temporal,
        stats,
        frames_in,
        gain,
        grad_heads,
        cot_in,
        scratch=packing,
    )
    received = exchange(sent, "frame")
    edge_frame = shape((rows * columns + 16, channels), bf16)
    normed, slope, inv, head, tail, slopes_token = call(
        lambda *refs: slopes(*refs, frames=frames, cell_count=cell_count),
        (low_flat, low_flat, shape((frames, channels), f32), edge_frame, edge_frame, token),
        temporal,
        stats,
        gain,
        pin=(0, 1, 2),
        after=(pooled,),
    )
    merged, bias = call(
        merge,
        (shape((channels, 3 * width), bf16), shape((half, heads * half), f32)),
        proj_in,
        proj_query,
        proj_key,
        proj_value,
        frame_bias,
        scratch=(
            low,
            pltpu.VMEM((5, depth // 5, 3 * width), bf16),
            pltpu.VMEM(frame_bias.shape, f32),
            pltpu.SemaphoreType.DMA((5, 4)),
        ),
        far=(0, 1, 2, 3, 4),
        pin=(0, 1),
        after=(slopes_token,),
    )
    before, after = neighbours(tail, head, "frame")
    sent = call(
        lambda *refs: coarse(*refs, heads=heads, channels=channels),
        payload,
        received,
        merged,
        bias,
        scratch=(
            packing[0],
            pltpu.VMEM((half, 4 * channels + width), f32),
            packing[1],
            pltpu.VMEM((2, heads * half, width), bf16),
        ),
    )
    beside_slope, beside_inv = call(
        slopes_beside,
        (shape((2, rows * columns, channels), bf16), shape((2, channels), f32)),
        before,
        after,
        gain,
        pin=(0, 1),
    )
    received = exchange(sent, "frame")
    stats, grad_pooled, blended = call(
        lambda *refs: totals(*refs, frames=frames),
        (
            shape((bands, 8, LANES), f32),
            shape((3, half, channels), bf16),
            shape((half, width), bf16),
        ),
        received,
        normed,
        slope,
        before,
        after,
        beside_slope,
        scratch=(pltpu.VMEM((half, 4 * channels + width), f32), packing[1]),
    )
    coarse_out, time = call(
        coarse_finish,
        (shape((half, depth), bf16), shape(kernel_time.shape, bf16)),
        pooled,
        proj_in,
        blended,
        proj_out,
        kernel_time,
        scratch=(low, high, pltpu.SemaphoreType.DMA((3,))),
        far=(1, 3, 4),
        pin=(1,),
        after=(stats,),
    )
    stats = exchange(stats, "space")
    row_edge = shape((frames, columns, channels), bf16)
    grad_spatial, top, bottom, grad_gain = call(
        lambda *refs: frames_back(*refs, cell_count=cell_count),
        (band, row_edge, row_edge, shape((1, SLOT), f32)),
        stats,
        grad_pooled,
        normed,
        slope,
        inv,
        before,
        after,
        beside_slope,
        beside_inv,
        time,
        scratch=(pltpu.VMEM(((frames + 2) * rows * columns, channels), bf16),),
        pin=(0, 1, 2, 3),
    )
    above, below = neighbours(bottom, top, "space")
    part, weight = call(
        space_back,
        (partial, space_here),
        grad_spatial,
        kernel_space,
        scratch=(pltpu.SemaphoreType.DMA((3,)),),
        far=(1,),
        pin=(0, 1),
    )
    grad_frames = call(
        space_back_finish,
        band,
        part,
        above,
        below,
        weight,
        grad_pooled,
        scratch=(pltpu.VMEM(band.shape, bf16), pltpu.SemaphoreType.DMA((2,))),
        far_out=(0,),
    )
    return coarse_out.reshape(cotangent.shape), grad_frames, grad_gain[0, :channels]


def solution(mesh):
    in_specs = (
        P("frame", "space", None, None),
        P(),
        P(),
        P(),
        P(),
        P(),
        P(),
        P(),
        P(),
        P(),
        P("frame", "space", None, None),
    )
    out_specs = (P("frame", "space", None, None), P("frame", "space", None, None), P())
    return jax.shard_map(local, mesh=mesh, in_specs=in_specs, out_specs=out_specs, check_vma=False)
```
